32 devices in a mesh: dp: 4 (over z), mp: 4 (over y, x), teach: 2 (over core).
Axes of the slice: x: 2, y: 2, z: 4, core: 2. Of those that a mesh axis runs over, the one named last changes fastest.
Arguments:
- patches: bfloat16 [64, 280, 768], P(('dp', 'teach')), may hold values from -6 to 6
- grid_sizes: int32 [64, 2], P(('dp', 'teach')), may hold values from 1 to 24, as said below
- label_ids: int32 [64, 2], P(('dp', 'teach')), may hold values from 0 to 999
- label_mix: float32 [64], P(('dp', 'teach')), may hold values from 0.3 to 0.7
- image_weight: float32 [64], P(('dp', 'teach')), may hold values from 0.5 to 13.5
- teacher_stem: bfloat16 [768, 224], replicated, may hold values from -0.21875 to 0.21875
- teacher_head: bfloat16 [224, 1000], P(None, 'mp'), may hold values from -2.390625 to 2.390625
- patch_weight: float32 [768, 768], P(('dp', 'teach')), may hold values from -0.21875 to 0.21875
- attn_weight: float32 [2, 4, 768, 768], P(None, None, ('dp', 'teach'), 'mp'), may hold values from -0.21875 to 0.21875
- mlp_weight: float32 [2, 2, 768, 3072], P(None, None, ('dp', 'teach'), 'mp'), may hold values from -0.15309311 to 0.15309311
- head_weight: float32 [2, 768, 1000], P(None, ('dp', 'teach'), 'mp'), may hold values from -0.4330127 to 0.4330127
- vector_params: float32 [65, 768], replicated, may hold values from -1.7 to 1.7
- split_biases: float32 [11216], P('mp'), may hold values from -1.8 to 1.8
- patch_first: float32 [768, 768], P(('dp', 'teach')), may hold values from -0.02734375 to 0.02734375
- attn_first: float32 [2, 4, 768, 768], P(None, None, ('dp', 'teach'), 'mp'), may hold values from -0.02734375 to 0.02734375
- mlp_first: float32 [2, 2, 768, 3072], P(None, None, ('dp', 'teach'), 'mp'), may hold values from -0.02734375 to 0.02734375
- head_first: float32 [2, 768, 1000], P(None, ('dp', 'teach'), 'mp'), may hold values from -0.02734375 to 0.02734375
- vector_first: float32 [65, 768], replicated, may hold values from -0.02734375 to 0.02734375
- bias_first: float32 [11216], P('mp'), may hold values from -0.02734375 to 0.02734375
- patch_second: float32 [768, 768], P(('dp', 'teach')), may hold values from 2.0345053e-05 to 8.138021e-05
- attn_second: float32 [2, 4, 768, 768], P(None, None, ('dp', 'teach'), 'mp'), may hold values from 2.0345053e-05 to 8.138021e-05
- mlp_second: float32 [2, 2, 768, 3072], P(None, None, ('dp', 'teach'), 'mp'), may hold values from 2.0345053e-05 to 8.138021e-05
- head_second: float32 [2, 768, 1000], P(None, ('dp', 'teach'), 'mp'), may hold values from 2.0345053e-05 to 8.138021e-05
- vector_second: float32 [65, 768], replicated, may hold values from 2.0345053e-05 to 8.138021e-05
- bias_second: float32 [11216], P('mp'), may hold values from 2.0345053e-05 to 8.138021e-05
- decay_mask: int32 [17], replicated, may hold values from 0 to 1
- layer_ids: int32 [17], replicated, may hold values from 0 to 2
- step_count: int32 [1], replicated, may hold values from 2 to 20
Outputs:
- patch_updated: float32 [768, 768], P(('dp', 'teach'))
- attn_updated: float32 [2, 4, 768, 768], P(None, None, ('dp', 'teach'), 'mp')
- mlp_updated: float32 [2, 2, 768, 3072], P(None, None, ('dp', 'teach'), 'mp')
- head_updated: float32 [2, 768, 1000], P(None, ('dp', 'teach'), 'mp')
- vector_updated: float32 [65, 768], replicated
- bias_updated: float32 [11216], P('mp')
- patch_moment: float32 [768, 768], P(('dp', 'teach'))
- attn_moment: float32 [2, 4, 768, 768], P(None, None, ('dp', 'teach'), 'mp')
- mlp_moment: float32 [2, 2, 768, 3072], P(None, None, ('dp', 'teach'), 'mp')
- head_moment: float32 [2, 768, 1000], P(None, ('dp', 'teach'), 'mp')
- vector_moment: float32 [65, 768], replicated
- bias_moment: float32 [11216], P('mp')
- patch_square: float32 [768, 768], P(('dp', 'teach'))
- attn_square: float32 [2, 4, 768, 768], P(None, None, ('dp', 'teach'), 'mp')
- mlp_square: float32 [2, 2, 768, 3072], P(None, None, ('dp', 'teach'), 'mp')
- head_square: float32 [2, 768, 1000], P(None, ('dp', 'teach'), 'mp')
- vector_square: float32 [65, 768], replicated
- bias_square: float32 [11216], P('mp')
- lamb_norms: float32 [2, 17], replicated
- trust_ratios: float32 [17], replicated
- loss_value: float32 [], replicated
The draws below stay inside these ranges and needn't reach their ends.
Inputs may be any that keep to these rules, and one draw needn't show every extreme that they name: `grid_sizes`: each image's grid has gh * gw <= 280.
All inputs are finite; a program needn't handle non-finite values.
Results may differ from the reference program's by a relative error of at most 0.014.
The reference program's roundings to bfloat16 on the way count: a program that leaves them out, or rounds other values in their place, can miss the bound.
Values may be sent and summed in bfloat16 or wider, within the bound.
No kernel may reach another device: no remote copies, remote signals or barrier semaphores. Data moves between devices by JAX's collectives and lax.ppermute only.
A program may use at most 256 MiB of HBM per device.

```python
import math
import jax
import jax.numpy as jnp
from jax import lax

D = 768
H = 12
HD = 64
FF = 3072
CLS = 1000
PD = 768
TW = 224
G = 24
PMAX = 280
L = 2
IMAGES = 64
R = 282
NV = 65
SB = 11216
NPAR = 17
N_MP = 4


def draw_grid_sizes(key, part):
    key = jax.random.fold_in(key, 11)
    lowest = max(1, PMAX // 35)
    highest = max(lowest, PMAX // 14)
    subkeys = jax.random.split(key, 4)
    grid_rows = jax.random.randint(subkeys[0], (IMAGES,), lowest, highest + 1)
    grid_cols = jnp.minimum(G, PMAX // grid_rows)
    grid_cols = grid_cols - jax.random.randint(subkeys[1], (IMAGES,), 0, 1 + grid_cols // 4)
    fullest = jax.random.randint(subkeys[2], (), 0, IMAGES)
    widest = (fullest + 1 + jax.random.randint(subkeys[3], (), 0, IMAGES - 1)) % IMAGES
    positions = jnp.arange(IMAGES)
    grid_rows = jnp.where(positions == fullest, highest, jnp.where(positions == widest, lowest, grid_rows))
    grid_cols = jnp.where(positions == fullest, min(G, PMAX // highest), jnp.where(positions == widest, min(G, PMAX // lowest), grid_cols))
    return jnp.stack([grid_rows, grid_cols], axis=1).astype(jnp.int32)


def draw_image_weight(key, part):
    key = jax.random.fold_in(key, 23)
    ramp_base = jnp.arange(IMAGES, dtype=jnp.float32) / (IMAGES - 1)
    factor = jax.random.uniform(key, (IMAGES,), jnp.float32, 0.5, 1.5)
    return factor * (1.0 + 2.0 * ramp_base)


def draw_vector_params(key, part):
    key = jax.random.fold_in(key, 37)
    row_count = 6 * L + 5 + 2 * G
    rows_all = jnp.arange(row_count)[:, None]
    base = jax.random.uniform(key, (row_count, D), jnp.float32, -1.0, 1.0)
    slot_kind = rows_all % 6
    is_gain = (rows_all < 6 * L) & ((slot_kind == 0) | (slot_kind == 2)) | (rows_all == 6 * L)
    is_token = (rows_all == 6 * L + 3) | (rows_all == 6 * L + 4)
    is_position = rows_all >= 6 * L + 5
    scale_rows = jnp.where(is_token, 1.7, jnp.where(is_position, 0.5, 0.3))
    return jnp.where(is_gain, 1.0 + 0.3 * base, scale_rows * base)


def place_ends(drawn, key, smallest, top_value):
    longest = drawn.shape.index(max(drawn.shape))
    spots = []
    for shift in (0, 1):
        where = [jax.random.randint(jax.random.fold_in(key, axis), (), 0, length) for axis, length in enumerate(drawn.shape)]
        where[longest] = (where[longest] + shift) % drawn.shape[longest]
        spots.append(tuple(where))
    return drawn.at[spots[0]].set(smallest).at[spots[1]].set(top_value)


def block_levels(rng, dims, cuts, low, largest):
    factor_of = 1.0
    for axis_at, parts in cuts:
        heights = jax.random.uniform(jax.random.fold_in(jax.random.fold_in(rng, 6), axis_at), (parts,), jnp.float32, low / len(cuts), largest / len(cuts))
        factor_of = factor_of * jnp.repeat(jnp.exp(heights), dims[axis_at] // parts).reshape((-1,) + (1,) * (len(dims) - 1 - axis_at))
    return factor_of


def noise(stream_key, extent, spread, bound, shards=(), held_as=jnp.bfloat16):
    result = spread * jax.random.normal(stream_key, extent, jnp.float32)
    if shards:
        result = result * block_levels(stream_key, extent, shards, -0.22, 0.18)
    return jnp.clip(result, -bound, bound).astype(held_as)


def setup_inputs(seed: int = 0) -> dict:
    streams_of = jax.random.split(jax.random.key(seed), 29)
    patches = noise(streams_of[0], (IMAGES, PMAX, PD), 1.0, 6.0, ((0, 8),))
    grid_sizes = draw_grid_sizes(jax.random.fold_in(streams_of[28], 71), 0)
    label_ids = place_ends(jax.random.randint(streams_of[2], (IMAGES, 2), 0, CLS), jax.random.fold_in(streams_of[2], 1), 0, CLS - 1).astype(jnp.int32)
    label_mix = jnp.clip(0.3 + 0.39999998 * jax.random.uniform(streams_of[3], (IMAGES,), jnp.float32) ** block_levels(streams_of[3], (IMAGES,), ((0, 8),), -0.2, 0.2), 0.3, 0.7)
    image_weight = draw_image_weight(jax.random.fold_in(streams_of[28], 71), 0)
    teacher_stem = noise(streams_of[5], (PD, TW), PD ** -0.5, 0.21875)
    teacher_head = noise(streams_of[6], (TW, CLS), (6.0 * TW ** -0.5), 2.390625, ((1, 4),))
    patch_weight = noise(streams_of[7], (PD, D), PD ** -0.5, 0.21875, ((0, 8),), jnp.float32)
    attn_weight = noise(streams_of[8], (L, 4, D, D), D ** -0.5, 0.21875, ((2, 8), (3, 4)), jnp.float32)
    mlp_weight = noise(streams_of[9], (L, 2, D, FF), ((D * FF) ** -0.25), 0.15309311, ((2, 8), (3, 4)), jnp.float32)
    head_weight = noise(streams_of[10], (2, D, CLS), (2.0 * D ** -0.5), 0.4330127, ((1, 8), (2, 4)), jnp.float32)
    vector_params = draw_vector_params(jax.random.fold_in(streams_of[28], 71), 0)
    split_biases = noise(streams_of[12], (SB,), 0.3, 1.8, ((0, 4),), jnp.float32)
    patch_first = noise(streams_of[13], (PD, D), ((D * IMAGES) ** -0.5), 0.02734375, ((0, 8),), jnp.float32)
    attn_first = noise(streams_of[14], (L, 4, D, D), ((D * IMAGES) ** -0.5), 0.02734375, ((2, 8), (3, 4)), jnp.float32)
    mlp_first = noise(streams_of[15], (L, 2, D, FF), ((D * IMAGES) ** -0.5), 0.02734375, ((2, 8), (3, 4)), jnp.float32)
    head_first = noise(streams_of[16], (2, D, CLS), ((D * IMAGES) ** -0.5), 0.02734375, ((1, 8), (2, 4)), jnp.float32)
    vector_first = noise(streams_of[17], (NV, D), ((D * IMAGES) ** -0.5), 0.02734375, (), jnp.float32)
    bias_first = noise(streams_of[18], (SB,), ((D * IMAGES) ** -0.5), 0.02734375, ((0, 4),), jnp.float32)
    patch_second = jnp.clip(jnp.exp(math.log(8.138021075865254e-05) - 1.3862944 * jax.random.uniform(streams_of[19], (PD, D), jnp.float32) ** block_levels(streams_of[19], (PD, D), ((0, 8),), -0.2, 0.2)), 2.0345052689663135e-05, 8.138021075865254e-05)
    attn_second = jnp.clip(jnp.exp(math.log(8.138021075865254e-05) - 1.3862944 * jax.random.uniform(streams_of[20], (L, 4, D, D), jnp.float32) ** block_levels(streams_of[20], (L, 4, D, D), ((2, 8), (3, 4)), -0.2, 0.2)), 2.0345052689663135e-05, 8.138021075865254e-05)
    mlp_second = jnp.clip(jnp.exp(math.log(8.138021075865254e-05) - 1.3862944 * jax.random.uniform(streams_of[21], (L, 2, D, FF), jnp.float32) ** block_levels(streams_of[21], (L, 2, D, FF), ((2, 8), (3, 4)), -0.2, 0.2)), 2.0345052689663135e-05, 8.138021075865254e-05)
    head_second = jnp.clip(jnp.exp(math.log(8.138021075865254e-05) - 1.3862944 * jax.random.uniform(streams_of[22], (2, D, CLS), jnp.float32) ** block_levels(streams_of[22], (2, D, CLS), ((1, 8), (2, 4)), -0.2, 0.2)), 2.0345052689663135e-05, 8.138021075865254e-05)
    vector_second = jnp.clip(jnp.exp(jax.random.uniform(streams_of[23], (NV, D), jnp.float32, math.log(2.0345052689663135e-05), math.log(8.138021075865254e-05))), 2.0345052689663135e-05, 8.138021075865254e-05)
    bias_second = jnp.clip(jnp.exp(math.log(8.138021075865254e-05) - 1.3862944 * jax.random.uniform(streams_of[24], (SB,), jnp.float32) ** block_levels(streams_of[24], (SB,), ((0, 4),), -0.2, 0.2)), 2.0345052689663135e-05, 8.138021075865254e-05)
    decay_mask = place_ends(jax.random.randint(streams_of[25], (NPAR,), 0, 2), jax.random.fold_in(streams_of[25], 1), 0, 1).astype(jnp.int32)
    layer_ids = place_ends(jax.random.randint(streams_of[26], (NPAR,), 0, 3), jax.random.fold_in(streams_of[26], 1), 0, 2).astype(jnp.int32)
    step_count = jax.random.randint(streams_of[27], (1,), 2, 21).astype(jnp.int32)
    return dict(patches=patches, grid_sizes=grid_sizes, label_ids=label_ids, label_mix=label_mix, image_weight=image_weight, teacher_stem=teacher_stem, teacher_head=teacher_head, patch_weight=patch_weight, attn_weight=attn_weight, mlp_weight=mlp_weight, head_weight=head_weight, vector_params=vector_params, split_biases=split_biases, patch_first=patch_first, attn_first=attn_first, mlp_first=mlp_first, head_first=head_first, vector_first=vector_first, bias_first=bias_first, patch_second=patch_second, attn_second=attn_second, mlp_second=mlp_second, head_second=head_second, vector_second=vector_second, bias_second=bias_second, decay_mask=decay_mask, layer_ids=layer_ids, step_count=step_count)


EPS_NORM = 1e-06
EPS_LAMB = 1e-06
BETA = 0.5
DECAY = 0.05
BASE_RATE = 0.4
LAYER_DECAY = 0.8
SCALE = 0.125
MASKED = -1e+30
HIGH = lax.Precision.HIGHEST

@jax.custom_vjp
def low(v):
    return lax.optimization_barrier(v.astype(jnp.bfloat16)).astype(jnp.float32)

@jax.custom_vjp
def low_back(v):
    return v

def low_keep(v):
    return (low(v), None)

def low_pass(kept, grad):
    return (grad,)

def back_keep(v):
    return (v, None)

def back_low(kept, grad):
    return (low(grad),)
low.defvjp(low_keep, low_pass)
low_back.defvjp(back_keep, back_low)

def layer_norm(values, gain_row, bias_row):
    centre = values - lax.optimization_barrier(jnp.mean(values, axis=-1, keepdims=True))
    return centre * lax.rsqrt(lax.optimization_barrier(jnp.mean(centre * centre, axis=-1, keepdims=True)) + EPS_NORM) * gain_row + bias_row

def log_sum_exp(values):
    row_peak = lax.optimization_barrier(jnp.max(values, axis=-1, keepdims=True))
    return (row_peak + jnp.log(lax.optimization_barrier(jnp.sum(jnp.exp(values - row_peak), axis=-1, keepdims=True))))[..., 0]

def dense(left, right):
    return jnp.einsum('ird,de->ire', left, right, precision=HIGH)

def attend_one(operands):
    queries, key_rows, value_rows, valid_keys = operands
    scores = low_back(jnp.einsum('qhd,khd->hqk', queries, key_rows, precision=HIGH) * SCALE)
    scores = jnp.where(valid_keys[None, None, :], scores, MASKED)
    row_peak = lax.optimization_barrier(jnp.max(scores, axis=-1, keepdims=True))
    exponent = jnp.exp(scores - row_peak)
    soft_rows = low(exponent / lax.optimization_barrier(jnp.sum(exponent, axis=-1, keepdims=True)))
    return jnp.einsum('hqk,khd->qhd', soft_rows, value_rows, precision=HIGH)

def unpack_biases(biases):
    width_local = D // N_MP
    ff_local = FF // N_MP
    class_local = CLS // N_MP
    blocks = biases.reshape(N_MP, SB // N_MP)
    layer_biases = []
    for layer_num in range(L):
        offset = layer_num * (2 * width_local + ff_local)
        layer_biases.append((blocks[:, offset:offset + width_local].reshape(D), blocks[:, offset + width_local:offset + 2 * width_local].reshape(D), blocks[:, offset + 2 * width_local:offset + 2 * width_local + ff_local].reshape(FF)))
    offset = L * (2 * width_local + ff_local)
    return (layer_biases, blocks[:, offset:offset + class_local].reshape(CLS), blocks[:, offset + class_local:offset + 2 * class_local].reshape(CLS))

def adam_direction(gradient, first_moment, second_moment, correct_first, correct_second):
    new_first = BETA * first_moment + (1.0 - BETA) * gradient
    new_second = BETA * second_moment + (1.0 - BETA) * gradient * gradient
    return (new_first, new_second, new_first / correct_first / (jnp.sqrt(new_second / correct_second) + EPS_LAMB))

def split_params(values):
    layered = values[1:1 + 6 * L].reshape(L, 6)
    return (values[0], layered[:, :4], layered[:, 4:], values[1 + 6 * L:3 + 6 * L], values[3 + 6 * L], values[4 + 6 * L])

def expand_params(pieces):
    return (pieces[0], pieces[1][:, :, None, None], pieces[2][:, :, None, None], pieces[3][:, None, None], pieces[4], pieces[5])

def order_params(pieces):
    layered = jnp.concatenate([pieces[1], pieces[2]], axis=1).reshape(-1)
    return jnp.concatenate([pieces[0][None], layered, pieces[3], pieces[4][None], pieces[5][None]])

def squares_of(pieces):
    return order_params((jnp.sum(pieces[0] * pieces[0]), lax.optimization_barrier(jnp.sum(pieces[1] * pieces[1], axis=(2, 3))), lax.optimization_barrier(jnp.sum(pieces[2] * pieces[2], axis=(2, 3))), lax.optimization_barrier(jnp.sum(pieces[3] * pieces[3], axis=(1, 2))), jnp.sum(pieces[4] * pieces[4]), jnp.sum(pieces[5] * pieces[5])))

def reference(patches, grid_sizes, label_ids, label_mix, image_weight, teacher_stem, teacher_head, patch_weight, attn_weight, mlp_weight, head_weight, vector_params, split_biases, patch_first, attn_first, mlp_first, head_first, vector_first, bias_first, patch_second, attn_second, mlp_second, head_second, vector_second, bias_second, decay_mask, layer_ids, step_count):
    patches_f = patches.astype(jnp.float32)
    grid_rows = grid_sizes[:, 0:1]
    grid_cols = grid_sizes[:, 1:2]
    slot_ids = jnp.arange(PMAX, dtype=jnp.int32)[None, :]
    patch_live = slot_ids < grid_rows * grid_cols
    table_slots = jnp.arange(G, dtype=jnp.int32)
    row_onehot = ((slot_ids // grid_cols)[..., None] == table_slots).astype(jnp.float32)
    col_onehot = ((slot_ids % grid_cols)[..., None] == table_slots).astype(jnp.float32)
    key_live = jnp.concatenate([jnp.ones((IMAGES, 2), dtype=bool), patch_live], axis=1)
    live_float = patch_live.astype(jnp.float32)
    stem_rows = jax.nn.gelu(jnp.einsum('ipc,ct->ipt', patches_f, teacher_stem.astype(jnp.float32), precision=HIGH), approximate=False)
    pooled = low(lax.optimization_barrier(jnp.sum(stem_rows * live_float[..., None], axis=1)) / lax.optimization_barrier(jnp.sum(live_float, axis=1, keepdims=True)))
    logits_teacher = jnp.dot(pooled, teacher_head.astype(jnp.float32), precision=HIGH)
    teacher_soft = jnp.exp(logits_teacher - log_sum_exp(logits_teacher)[:, None])
    class_ids = jnp.arange(CLS, dtype=jnp.int32)
    target = label_mix[:, None] * (label_ids[:, 0:1] == class_ids).astype(jnp.float32) + (1.0 - label_mix[:, None]) * (label_ids[:, 1:2] == class_ids).astype(jnp.float32)
    head_row = 6 * L

    def forward(patch_mat, attn_mat, mlp_mat, head_mat, vectors, biases):
        layer_biases, cls_bias, dist_bias = unpack_biases(biases)
        embedded = low_back(jnp.einsum('ipc,cd->ipd', patches_f, low(patch_mat), precision=HIGH))
        positional = jnp.einsum('ipg,gd->ipd', row_onehot, vectors[head_row + 5:head_row + 5 + G], precision=HIGH) + jnp.einsum('ipg,gd->ipd', col_onehot, vectors[head_row + 5 + G:], precision=HIGH)
        residual = jnp.concatenate([jnp.broadcast_to(vectors[head_row + 3], (IMAGES, 1, D)), jnp.broadcast_to(vectors[head_row + 4], (IMAGES, 1, D)), embedded + vectors[head_row + 2] + positional], axis=1)
        for layer_num in range(L):
            gain_rows = vectors[6 * layer_num:6 * layer_num + 6]
            query_bias, value_bias, up_bias = layer_biases[layer_num]
            first_in = low(layer_norm(residual, gain_rows[0], gain_rows[1]))
            queries = low(low_back(dense(first_in, low(attn_mat[layer_num, 0])) + query_bias))
            key_rows = low(low_back(dense(first_in, low(attn_mat[layer_num, 1]))))
            value_rows = low(low_back(dense(first_in, low(attn_mat[layer_num, 2])) + value_bias))
            attended = lax.map(jax.checkpoint(attend_one), (queries.reshape(IMAGES, R, H, HD), key_rows.reshape(IMAGES, R, H, HD), value_rows.reshape(IMAGES, R, H, HD), key_live))
            attended = low(low_back(attended.reshape(IMAGES, R, D)))
            residual = residual + low_back(dense(attended, low(attn_mat[layer_num, 3]).T)) + gain_rows[4]
            second_in = low(layer_norm(residual, gain_rows[2], gain_rows[3]))
            upward = low_back(dense(second_in, low(mlp_mat[layer_num, 0])) + up_bias)
            hidden = low(jax.nn.gelu(upward, approximate=False))
            residual = residual + low_back(dense(hidden, low(mlp_mat[layer_num, 1]).T)) + gain_rows[5]
        final_rows = low(layer_norm(residual[:, :2], vectors[head_row], vectors[head_row + 1]))
        logits_cls = low_back(jnp.dot(final_rows[:, 0], low(head_mat[0]), precision=HIGH)) + cls_bias
        logits_dist = low_back(jnp.dot(final_rows[:, 1], low(head_mat[1]), precision=HIGH)) + dist_bias
        loss_rows = 0.5 * (log_sum_exp(logits_cls) - lax.optimization_barrier(jnp.sum(target * logits_cls, axis=1))) + 0.5 * (log_sum_exp(logits_dist) - lax.optimization_barrier(jnp.sum(teacher_soft * logits_dist, axis=1)))
        return jnp.sum(image_weight * loss_rows) / jnp.sum(image_weight)
    weights = (patch_weight, attn_weight, mlp_weight, head_weight, vector_params, split_biases)
    loss_value, pullback = jax.vjp(forward, *weights)
    gradients = pullback(jnp.ones_like(loss_value))
    step_power = step_count[0].astype(jnp.float32)
    correct_first = 1.0 - jnp.power(BETA, step_power)
    correct_second = 1.0 - jnp.power(BETA, step_power)
    firsts = (patch_first, attn_first, mlp_first, head_first, vector_first, bias_first)
    seconds = (patch_second, attn_second, mlp_second, head_second, vector_second, bias_second)
    decay_pieces = expand_params(split_params(decay_mask.astype(jnp.float32)))
    results = [adam_direction(gradients[slot], firsts[slot], seconds[slot], correct_first, correct_second) for slot in range(6)]
    directions = [results[slot][2] + DECAY * decay_pieces[slot] * weights[slot] for slot in range(6)]
    weight_norm = jnp.sqrt(squares_of(weights))
    update_norm = jnp.sqrt(squares_of(directions))
    trust_ratio = weight_norm / update_norm
    rates = BASE_RATE * jnp.power(LAYER_DECAY, 2.0 - layer_ids.astype(jnp.float32)) * trust_ratio
    rate_pieces = expand_params(split_params(rates))
    updated = [weights[slot] - rate_pieces[slot] * directions[slot] for slot in range(6)]
    norm_table = jnp.stack([weight_norm, update_norm])
    return (updated[0], updated[1], updated[2], updated[3], updated[4], updated[5], results[0][0], results[1][0], results[2][0], results[3][0], results[4][0], results[5][0], results[0][1], results[1][1], results[2][1], results[3][1], results[4][1], results[5][1], norm_table, trust_ratio, loss_value)
```

```python
import functools

import jax
import jax.numpy as jnp
from jax import lax
from jax.experimental import pallas as pl
from jax.experimental.pallas import tpu as pltpu
from jax.sharding import PartitionSpec as P

D = 768
HD = 64
G = 24
PMAX = 280
L = 2
RP = 288
TOK = 280
HR = 16

EPS_NORM = 1e-06
EPS_LAMB = 1e-06
BETA = 0.5
DECAY = 0.05
BASE_RATE = 0.4
LAYER_DECAY = 0.8
SCALE = 0.125
MASKED = -1e30
HIGH = lax.Precision.HIGHEST
ROOT_HALF = 0.7071067811865476
DENSITY = 0.3989422804014327
BF = jnp.bfloat16
F32 = jnp.float32
ALL = ("dp", "mp", "teach")
VMEM_LIMIT = 56 * 1024 * 1024
FLOP_PER_US = 1_150_000_000


def dot_nn(left, right):
    return lax.dot_general(
        left, right, (((1,), (0,)), ((), ())), preferred_element_type=F32
    )


def dot_nt(left, right):
    return lax.dot_general(
        left, right, (((1,), (1,)), ((), ())), preferred_element_type=F32
    )


def dot_tn(left, right):
    return lax.dot_general(
        left, right, (((0,), (0,)), ((), ())), preferred_element_type=F32
    )


def gelu_erf(values):
    return 0.5 * values * (1.0 + lax.erf(values * ROOT_HALF))


def norm_stats(values):
    centre = values - jnp.mean(values, axis=-1, keepdims=True)
    scaled = lax.rsqrt(jnp.mean(centre * centre, axis=-1, keepdims=True) + EPS_NORM)
    return centre * scaled, scaled


def norm_back(grad_out, normed, scaled, gain_row):
    grad_normed = grad_out * gain_row
    inner_sum = jnp.mean(grad_normed, axis=-1, keepdims=True)
    cross_term = jnp.mean(grad_normed * normed, axis=-1, keepdims=True)
    return scaled * (grad_normed - inner_sum - normed * cross_term)


def row_sum(values):
    return jnp.sum(values, axis=0, keepdims=True)


def start_weights(full, buf, sems):
    steps, _, teach, rows, _ = full.shape
    copies = []
    for core in range(teach):
        for step in range(steps):
            at = (core * steps + step) * rows
            copies.append(
                pltpu.make_async_copy(
                    full.at[step, :, core], buf.at[:, pl.ds(at, rows)], sems.at[core * steps + step]
                )
            )
    for copy in copies:
        copy.start()
    return copies


def split_out(half, place, grad_buf, mine_ref, other_ref, block):
    mine = pl.multiple_of(place * half, 128)
    theirs = pl.multiple_of((1 - place) * half, 128)
    mine_ref[block] = grad_buf[pl.ds(mine, half), :]
    other_ref[block] = grad_buf[pl.ds(theirs, half), :]


def attn_forward_kernel(
    mp,
    ni,
    wl,
    resid_ref,
    vec_ref,
    bias_ref,
    live_ref,
    full,
    first_ref,
    qkv_ref,
    att_ref,
    lse_ref,
    mid_ref,
    buf,
    sems,
):
    copies = start_weights(full, buf, sems)
    resid = resid_ref[...]
    normed, _ = norm_stats(resid)
    first_ref[...] = (normed * vec_ref[0:1] + vec_ref[1:2]).astype(BF)
    mid_ref[...] = resid + vec_ref[4:5]
    for copy in copies:
        copy.wait()

    def body(block, carry):
        qkv = dot_nn(first_ref[...], buf[block, :, : 3 * wl]) + bias_ref[block]
        qkv_ref[block] = qkv.astype(BF)
        for image in range(ni):
            rows = slice(image * RP, (image + 1) * RP)
            live = live_ref[image] > 0.0
            for head in range(wl // HD):
                at = head * HD
                queries = qkv_ref[block, rows, at : at + HD]
                keys = qkv_ref[block, rows, wl + at : wl + at + HD]
                vals = qkv_ref[block, rows, 2 * wl + at : 2 * wl + at + HD]
                scores = jnp.where(live, dot_nt(queries, keys) * SCALE, MASKED)
                peak = jnp.max(scores, axis=-1, keepdims=True)
                expo = jnp.exp(scores - peak)
                total = jnp.sum(expo, axis=-1, keepdims=True)
                soft = (expo * (1.0 / total)).astype(BF)
                att_ref[block, rows, at : at + HD] = dot_nn(soft, vals).astype(BF)
                lse_ref[block, rows, head : head + 1] = peak + jnp.log(total)
        mid_ref[...] += dot_nt(att_ref[block], buf[block, :, 3 * wl :])
        return carry

    lax.fori_loop(0, mp, body, 0)


def mlp_forward_kernel(
    mp,
    chunk,
    mid_ref,
    vec_ref,
    bias_ref,
    full,
    second_ref,
    hidden_ref,
    slope_ref,
    out_ref,
    buf,
    sems,
):
    fl = hidden_ref.shape[2]
    copies = start_weights(full, buf, sems)
    middle = mid_ref[...]
    normed, _ = norm_stats(middle)
    second_ref[...] = (normed * vec_ref[2:3] + vec_ref[3:4]).astype(BF)
    out_ref[...] = middle + vec_ref[5:6]
    for copy in copies:
        copy.wait()
    row_count = mid_ref.shape[0]

    def body(block, carry):
        for start in range(0, row_count, chunk):
            rows = slice(start, start + chunk)
            upward = dot_nn(second_ref[rows, :], buf[block, :, :fl]) + bias_ref[block]
            share = 0.5 + 0.5 * lax.erf(upward * ROOT_HALF)
            hidden = (upward * share).astype(BF)
            hidden_ref[block, rows, :] = hidden
            slope_ref[block, rows, :] = share + upward * (
                DENSITY * jnp.exp(-0.5 * upward * upward)
            )
            out_ref[rows, :] += dot_nt(hidden, buf[block, :, fl:])
        return carry

    lax.fori_loop(0, mp, body, 0)


def head_kernel(
    mp,
    ni,
    wc,
    place_ref,
    resid_ref,
    vec_ref,
    bias_ref,
    ids_ref,
    labels_ref,
    mix_ref,
    scale_ref,
    weight_ref,
    pooled_ref,
    teacher_ref,
    full,
    mine_ref,
    other_ref,
    hbias_ref,
    grad_ref,
    vgrad_ref,
    loss_ref,
    buf,
    cls_buf,
    dist_buf,
    gw_buf,
    sems,
):
    half = mine_ref.shape[1]
    copies = start_weights(full, buf, sems)
    cls_buf[...] = jnp.zeros_like(cls_buf)
    dist_buf[...] = jnp.zeros_like(dist_buf)
    for image in range(ni):
        at = image * RP + TOK
        cls_buf[image : image + 1, :] = resid_ref[at : at + 1, :]
        dist_buf[image : image + 1, :] = resid_ref[at + 1 : at + 2, :]
    grad_ref[...] = jnp.zeros_like(grad_ref)
    normed_c, scaled_c = norm_stats(cls_buf[...])
    normed_d, scaled_d = norm_stats(dist_buf[...])
    gain, shift = vec_ref[0:1], vec_ref[1:2]
    final_c = (normed_c * gain + shift).astype(BF)
    final_d = (normed_d * gain + shift).astype(BF)
    for copy in copies:
        copy.wait()
    cls, dist, teach, goal = [], [], [], []
    mix = mix_ref[:, 0:1]
    for block in range(mp):
        ids = ids_ref[block]
        valid = ids >= 0
        both = bias_ref[block]
        cls.append(
            jnp.where(valid, dot_nn(final_c, buf[block, :, :wc]) + both[:, :wc], MASKED)
        )
        dist.append(
            jnp.where(valid, dot_nn(final_d, buf[block, :, wc:]) + both[:, wc:], MASKED)
        )
        teach.append(jnp.where(valid, dot_nn(pooled_ref[...], teacher_ref[block]), MASKED))
        first = (labels_ref[:, 0:1] == ids).astype(F32)
        second = (labels_ref[:, 1:2] == ids).astype(F32)
        goal.append(mix * first + (1.0 - mix) * second)

    def log_total(parts):
        peak = functools.reduce(
            jnp.maximum, [jnp.max(part, axis=-1, keepdims=True) for part in parts]
        )
        total = sum(jnp.sum(jnp.exp(part - peak), axis=-1, keepdims=True) for part in parts)
        return peak + jnp.log(total)

    log_c, log_d, log_t = log_total(cls), log_total(dist), log_total(teach)
    prob = [jnp.exp(part - log_t) for part in teach]
    dot_c = sum(jnp.sum(g * c, axis=-1, keepdims=True) for g, c in zip(goal, cls))
    dot_d = sum(jnp.sum(p * d, axis=-1, keepdims=True) for p, d in zip(prob, dist))
    loss_rows = 0.5 * (log_c - dot_c) + 0.5 * (log_d - dot_d)
    loss_ref[...] = jnp.broadcast_to(row_sum(weight_ref[:, 0:1] * loss_rows), loss_ref.shape)
    scale = scale_ref[:, 0:1]
    gfin_c = jnp.zeros(cls_buf.shape, F32)
    gfin_d = jnp.zeros(dist_buf.shape, F32)
    for block in range(mp):
        grad_c = scale * (jnp.exp(cls[block] - log_c) - goal[block])
        grad_d = scale * (jnp.exp(dist[block] - log_d) - prob[block])
        hbias_ref[block, :, :wc] = row_sum(grad_c)
        hbias_ref[block, :, wc:] = row_sum(grad_d)
        low_c, low_d = grad_c.astype(BF), grad_d.astype(BF)
        gw_buf[:, :wc] = dot_tn(final_c, low_c).astype(BF)
        gw_buf[:, wc:] = dot_tn(final_d, low_d).astype(BF)
        split_out(half, place_ref[0], gw_buf, mine_ref, other_ref, block)
        gfin_c += dot_nt(low_c, buf[block, :, :wc])
        gfin_d += dot_nt(low_d, buf[block, :, wc:])
    vgrad_ref[...] = jnp.zeros_like(vgrad_ref)
    vgrad_ref[0:1, :] = row_sum(gfin_c * normed_c) + row_sum(gfin_d * normed_d)
    vgrad_ref[1:2, :] = row_sum(gfin_c) + row_sum(gfin_d)
    cls_buf[...] = norm_back(gfin_c, normed_c, scaled_c, gain)
    dist_buf[...] = norm_back(gfin_d, normed_d, scaled_d, gain)
    for image in range(ni):
        at = image * RP + TOK
        grad_ref[at : at + 1, :] = cls_buf[image : image + 1, :]
        grad_ref[at + 1 : at + 2, :] = dist_buf[image : image + 1, :]


def mlp_backward_kernel(
    mp,
    place_ref,
    grad_ref,
    mid_ref,
    vec_ref,
    second_ref,
    hidden_ref,
    slope_ref,
    full,
    gmid_ref,
    mine_ref,
    other_ref,
    gbias_ref,
    vgrad_ref,
    buf,
    branch_buf,
    branch_t,
    second_t,
    gw_buf,
    sems,
):
    fl = hidden_ref.shape[2]
    half = mine_ref.shape[1]
    place = place_ref[0]
    copies = start_weights(full, buf, sems)
    branch_buf[...] = grad_ref[...].astype(BF)
    branch_t[...] = branch_buf[...].T
    second_t[...] = second_ref[...].T
    gmid_ref[...] = jnp.zeros_like(gmid_ref)
    for copy in copies:
        copy.wait()

    def body(block, carry):
        gup = (dot_nn(branch_buf[...], buf[block, :, fl:]) * slope_ref[block]).astype(BF)
        gbias_ref[block] = row_sum(gup.astype(F32))
        gmid_ref[...] += dot_nt(gup, buf[block, :, :fl])
        gw_buf[:, :fl] = dot_nn(second_t[...], gup).astype(BF)
        gw_buf[:, fl:] = dot_nn(branch_t[...], hidden_ref[block]).astype(BF)
        split_out(half, place, gw_buf, mine_ref, other_ref, block)
        return carry

    lax.fori_loop(0, mp, body, 0)
    normed, scaled = norm_stats(mid_ref[...])
    gsec = gmid_ref[...]
    grad = grad_ref[...]
    vgrad_ref[...] = jnp.zeros_like(vgrad_ref)
    vgrad_ref[2:3, :] = row_sum(gsec * normed)
    vgrad_ref[3:4, :] = row_sum(gsec)
    vgrad_ref[5:6, :] = row_sum(grad)
    gmid = norm_back(gsec, normed, scaled, vec_ref[2:3]) + grad
    vgrad_ref[4:5, :] = row_sum(gmid)
    gmid_ref[...] = gmid


def attn_backward_kernel(
    mp,
    ni,
    wl,
    place_ref,
    gmid_ref,
    resid_ref,
    vec_ref,
    live_ref,
    first_ref,
    qkv_ref,
    att_ref,
    lse_ref,
    full,
    gres_ref,
    mine_ref,
    other_ref,
    gbias_ref,
    vgrad_ref,
    buf,
    mixed_buf,
    mixed_t,
    first_t,
    gatt_buf,
    gqkv_buf,
    gw_buf,
    sems,
):
    half = mine_ref.shape[1]
    place = place_ref[0]
    copies = start_weights(full, buf, sems)
    mixed_buf[...] = gmid_ref[...].astype(BF)
    mixed_t[...] = mixed_buf[...].T
    first_t[...] = first_ref[...].T
    gres_ref[...] = jnp.zeros_like(gres_ref)
    for copy in copies:
        copy.wait()

    def body(block, carry):
        gatt_buf[...] = dot_nn(mixed_buf[...], buf[block, :, 3 * wl :]).astype(BF)
        for image in range(ni):
            rows = slice(image * RP, (image + 1) * RP)
            live = live_ref[image] > 0.0
            for head in range(wl // HD):
                at = head * HD
                queries = qkv_ref[block, rows, at : at + HD]
                keys = qkv_ref[block, rows, wl + at : wl + at + HD]
                vals = qkv_ref[block, rows, 2 * wl + at : 2 * wl + at + HD]
                gatt = gatt_buf[rows, at : at + HD]
                scores = jnp.where(live, dot_nt(queries, keys) * SCALE, MASKED)
                soft = jnp.exp(scores - lse_ref[block, rows, head : head + 1])
                gsoft = dot_nt(gatt, vals)
                inner = jnp.sum(soft * gsoft, axis=-1, keepdims=True)
                gscore = (soft * (gsoft - inner)).astype(BF)
                gqkv_buf[rows, at : at + HD] = (dot_nn(gscore, keys) * SCALE).astype(BF)
                gqkv_buf[rows, wl + at : wl + at + HD] = (dot_tn(gscore, queries) * SCALE).astype(BF)
                gqkv_buf[rows, 2 * wl + at : 2 * wl + at + HD] = dot_tn(soft.astype(BF), gatt).astype(BF)
        gqkv = gqkv_buf[...]
        gbias_ref[block] = row_sum(gqkv.astype(F32))
        gres_ref[...] += dot_nt(gqkv, buf[block, :, : 3 * wl])
        gw_buf[:, : 3 * wl] = dot_nn(first_t[...], gqkv).astype(BF)
        gw_buf[:, 3 * wl :] = dot_nn(mixed_t[...], att_ref[block]).astype(BF)
        split_out(half, place, gw_buf, mine_ref, other_ref, block)
        return carry

    lax.fori_loop(0, mp, body, 0)
    normed, scaled = norm_stats(resid_ref[...])
    gfirst = gres_ref[...]
    vgrad_ref[...] = jnp.zeros_like(vgrad_ref)
    vgrad_ref[0:1, :] = row_sum(gfirst * normed)
    vgrad_ref[1:2, :] = row_sum(gfirst)
    gres_ref[...] = norm_back(gfirst, normed, scaled, vec_ref[0:1]) + gmid_ref[...]


def call(kernel, outs, scratch, ins, micros, after=()):
    specs, arrays = [], []

    def ordered(*refs):
        return kernel(*refs[: len(ins)], *refs[len(ins) + len(after) :])

    for item in [*ins, *[("hbm", array) for array in after]]:
        if isinstance(item, tuple):
            specs.append(pl.BlockSpec(memory_space=pl.ANY if item[0] == "hbm" else pltpu.SMEM))
            arrays.append(item[1])
        else:
            specs.append(pl.BlockSpec(memory_space=pltpu.VMEM))
            arrays.append(item)
    out_shape = [jax.ShapeDtypeStruct(shape, dtype) for shape, dtype in outs]
    moved = sum(a.size * a.dtype.itemsize for a in arrays)
    moved += sum(s.size * s.dtype.itemsize for s in out_shape)
    return pl.pallas_call(
        ordered if after else kernel,
        out_shape=out_shape,
        in_specs=specs,
        out_specs=[pl.BlockSpec(memory_space=pltpu.VMEM)] * len(out_shape),
        scratch_shapes=scratch,
        compiler_params=pltpu.CompilerParams(vmem_limit_bytes=VMEM_LIMIT),
        cost_estimate=pl.CostEstimate(
            flops=micros * FLOP_PER_US, bytes_accessed=moved, transcendentals=0
        ),
    )(*arrays)


def gather_unit(local):
    dp, mp, teach = lax.axis_size("dp"), lax.axis_size("mp"), lax.axis_size("teach")
    rows, width = local.shape
    full = lax.all_gather(local, ALL, axis=0, tiled=True).reshape(dp, mp, teach, rows, width)
    if rows % 16:
        full = full.transpose(1, 2, 0, 3, 4).reshape(1, mp, teach, dp * rows, width)
    return ("hbm", full)


def swap(values, axis, distance):
    size = lax.axis_size(axis)
    return lax.ppermute(values, axis, [(rank, rank ^ distance) for rank in range(size)])


def add_low(left, right):
    return (left.astype(F32) + right.astype(F32)).astype(BF)


def sum_all(values):
    for axis in ("teach", "mp", "dp"):
        distance = 1
        while distance < lax.axis_size(axis):
            values = values + swap(values, axis, distance)
            distance *= 2
    return values


def gather_mp(values):
    size = lax.axis_size("mp")
    parts = jnp.stack([values] + [swap(values, "mp", step) for step in range(1, size)])
    return parts[lax.axis_index("mp") ^ jnp.arange(size, dtype=jnp.int32)]


class Scatter:
    def __init__(self, mine, other):
        self.mine = mine
        self.got = swap(other, "teach", 1)
        self.stage = 0
        self.total = None

    def step(self):
        self.stage += 1
        if self.stage == 1:
            here = lax.axis_index("mp")
            self.cut = cut = self.mine.shape[1] // 2
            self.blocks = [
                add_low(
                    lax.dynamic_index_in_dim(self.mine, here ^ far, 0, False),
                    lax.dynamic_index_in_dim(self.got, here ^ far, 0, False),
                )
                for far in range(4)
            ]
            sent = [self.blocks[3][:cut], self.blocks[3][cut:]]
        elif self.stage == 2:
            cut, blocks = self.cut, self.blocks
            sent = [
                jnp.concatenate([blocks[1][:cut], add_low(blocks[1][cut:], self.by_two)]),
                jnp.concatenate([add_low(blocks[2][:cut], self.by_one), blocks[2][cut:]]),
            ]
        elif self.stage == 3:
            near = self.by_one.astype(F32) + self.by_two.astype(F32)
            total = (self.blocks[0].astype(F32) + near).astype(BF)
            self.total = lax.psum_scatter(total, "dp", scatter_dimension=0, tiled=True)
            return [total]
        else:
            return []
        self.by_one = swap(sent[0], "mp", 1)
        self.by_two = swap(sent[1], "mp", 2)
        return sent

    def result(self):
        while self.total is None:
            self.step()
        return self.total.astype(F32)


def adam_direction(gradient, first_moment, second_moment, correct_first, correct_second):
    new_first = BETA * first_moment + (1.0 - BETA) * gradient
    new_second = BETA * second_moment + (1.0 - BETA) * gradient * gradient
    return (
        new_first,
        new_second,
        new_first / correct_first / (jnp.sqrt(new_second / correct_second) + EPS_LAMB),
    )


def split_params(values):
    layered = values[1 : 1 + 6 * L].reshape(L, 6)
    return (
        values[0],
        layered[:, :4],
        layered[:, 4:],
        values[1 + 6 * L : 3 + 6 * L],
        values[3 + 6 * L],
        values[4 + 6 * L],
    )


def expand_params(pieces):
    return (
        pieces[0],
        pieces[1][:, :, None, None],
        pieces[2][:, :, None, None],
        pieces[3][:, None, None],
        pieces[4],
        pieces[5],
    )


def order_params(pieces):
    layered = jnp.concatenate([pieces[1], pieces[2]], axis=1).reshape(-1)
    return jnp.concatenate([pieces[0][None], layered, pieces[3], pieces[4][None], pieces[5][None]])


def squares_of(pieces, mp_first, data_first):
    return order_params(
        (
            jnp.sum(pieces[0] * pieces[0]) * mp_first,
            jnp.sum(pieces[1] * pieces[1], axis=(2, 3)),
            jnp.sum(pieces[2] * pieces[2], axis=(2, 3)),
            jnp.sum(pieces[3] * pieces[3], axis=(1, 2)),
            jnp.sum(pieces[4] * pieces[4]) * mp_first * data_first,
            jnp.sum(pieces[5] * pieces[5]) * data_first,
        )
    )


def per_device(
    patches,
    grid_sizes,
    label_ids,
    label_mix,
    image_weight,
    teacher_stem,
    teacher_head,
    patch_weight,
    attn_weight,
    mlp_weight,
    head_weight,
    vector_params,
    split_biases,
    patch_first,
    attn_first,
    mlp_first,
    head_first,
    vector_first,
    bias_first,
    patch_second,
    attn_second,
    mlp_second,
    head_second,
    vector_second,
    bias_second,
    decay_mask,
    layer_ids,
    step_count,
):
    dp, mp, teach = lax.axis_size("dp"), lax.axis_size("mp"), lax.axis_size("teach")
    here_mp = lax.axis_index("mp")
    here_teach = lax.axis_index("teach")
    place = here_teach.astype(jnp.int32).reshape(1)
    mp_first = (here_mp == 0).astype(F32)
    data_first = (lax.axis_index(("dp", "teach")) == 0).astype(F32)
    rows_own = patch_weight.shape[0]
    half = dp * rows_own
    wl = attn_weight.shape[3]
    fl = mlp_weight.shape[3]
    cl = head_weight.shape[2]
    wc = -(-cl // 128) * 128
    head_row = 6 * L

    def inward(values):
        lead = values.shape[:-1]
        cut = values.reshape(*lead, dp, teach, rows_own)
        return jnp.swapaxes(cut, -3, -2).reshape(*lead, D)

    def outward(values):
        lead = values.shape[:-1]
        cut = values.reshape(*lead, teach, dp, rows_own)
        return jnp.swapaxes(cut, -3, -2).reshape(*lead, D)

    ni = patches.shape[0] // mp

    def take(array):
        return lax.dynamic_slice_in_dim(array, here_mp * ni, ni, 0)

    patches, grid_sizes, label_ids = take(patches), take(grid_sizes), take(label_ids)
    label_mix, image_weight = take(label_mix), take(image_weight)
    weight_sum = sum_all(jnp.sum(image_weight).reshape(1))[0]

    quarter = rows_own // mp
    patch_low = inward(patch_weight).astype(BF)
    patch_all = lax.all_gather(
        lax.dynamic_slice_in_dim(patch_low, here_mp * quarter, quarter, 0), ALL, axis=0, tiled=True
    ).reshape(dp, mp, teach, quarter, D)
    attn_units, mlp_units = [], []
    for layer in range(L):
        attn_low = jnp.concatenate([attn_weight[layer, part] for part in range(4)], axis=1)
        attn_units.append(gather_unit(attn_low.astype(BF)))
        mlp_low = jnp.concatenate([mlp_weight[layer, 0], mlp_weight[layer, 1]], axis=1)
        mlp_units.append(gather_unit(mlp_low.astype(BF)))
    head_pad = jnp.pad(head_weight, ((0, 0), (0, 0), (0, wc - cl)))
    head_unit = gather_unit(jnp.concatenate([head_pad[0], head_pad[1]], axis=1).astype(BF))
    teacher_all = gather_mp(jnp.pad(teacher_head, ((0, 0), (0, wc - cl))))
    bias_all = gather_mp(split_biases)

    vec_in = inward(vector_params)
    layer_vecs = [
        jnp.pad(vec_in[6 * layer : 6 * layer + 6], ((0, 2), (0, 0))) for layer in range(L)
    ]
    final_vec = jnp.pad(vec_in[head_row : head_row + 2], ((0, 6), (0, 0)))
    attn_bias, up_bias = [], []
    span = 2 * wl + fl
    for layer in range(L):
        part = bias_all[:, layer * span : (layer + 1) * span]
        zero = jnp.zeros((mp, wl), F32)
        attn_bias.append(
            jnp.concatenate([part[:, :wl], zero, part[:, wl : 2 * wl]], axis=1)[:, None]
        )
        up_bias.append(part[:, None, 2 * wl :])
    pad_class = ((0, 0), (0, wc - cl))
    head_bias = jnp.concatenate(
        [
            jnp.pad(bias_all[:, L * span : L * span + cl], pad_class),
            jnp.pad(bias_all[:, L * span + cl : L * span + 2 * cl], pad_class),
        ],
        axis=1,
    )[:, None]

    grid_rows, grid_cols = grid_sizes[:, 0:1], grid_sizes[:, 1:2]
    slot_ids = jnp.arange(PMAX, dtype=jnp.int32)[None, :]
    patch_live = slot_ids < grid_rows * grid_cols
    live_float = patch_live.astype(F32)
    live_rows = jnp.concatenate(
        [live_float, jnp.ones((ni, 2), F32), jnp.zeros((ni, RP - PMAX - 2), F32)], axis=1
    )[:, None, :]
    table = jnp.arange(G, dtype=jnp.int32)
    source_patch = jnp.concatenate(
        [
            jnp.ones((ni, PMAX, 1), F32),
            jnp.zeros((ni, PMAX, 2), F32),
            ((slot_ids // grid_cols)[..., None] == table).astype(F32),
            ((slot_ids % grid_cols)[..., None] == table).astype(F32),
        ],
        axis=2,
    )
    source_token = jnp.broadcast_to(jnp.eye(2, 3 + 2 * G, 1, dtype=F32), (ni, 2, 3 + 2 * G))
    sources = jnp.concatenate(
        [source_patch, source_token, jnp.zeros((ni, RP - PMAX - 2, 3 + 2 * G), F32)], axis=1
    ).reshape(ni * RP, 3 + 2 * G)

    stem_rows = gelu_erf(dot_nn(patches.reshape(ni * PMAX, -1), teacher_stem)).reshape(ni, PMAX, -1)
    pooled = (
        jnp.sum(stem_rows * live_float[..., None], axis=1)
        / jnp.sum(live_float, axis=1, keepdims=True)
    ).astype(BF)

    patch_full = patch_all.transpose(0, 2, 1, 3, 4).reshape(D, D)
    patch_rows = jnp.pad(patches, ((0, 0), (0, RP - PMAX), (0, 0))).reshape(ni * RP, -1)
    residual = dot_nn(patch_rows, patch_full) + jnp.dot(
        sources, vec_in[head_row + 2 :], precision=HIGH
    )

    n = ni * RP
    parts = head_unit[1].shape[0] * teach
    saved = []
    for layer in range(L):
        first, qkv, attended, lse, middle = call(
            functools.partial(attn_forward_kernel, mp, ni, wl),
            [
                ((n, D), BF),
                ((mp, n, 3 * wl), BF),
                ((mp, n, wl), BF),
                ((mp, n, wl // HD), F32),
                ((n, D), F32),
            ],
            [pltpu.VMEM((mp, D, 4 * wl), BF), pltpu.SemaphoreType.DMA((parts,))],
            [residual, layer_vecs[layer], attn_bias[layer], live_rows, attn_units[layer]],
            20,
        )
        second, hidden, slope, output = call(
            functools.partial(mlp_forward_kernel, mp, n // 4),
            [((n, D), BF), ((mp, n, fl), BF), ((mp, n, fl), F32), ((n, D), F32)],
            [pltpu.VMEM((mp, D, 2 * fl), BF), pltpu.SemaphoreType.DMA((parts,))],
            [middle, layer_vecs[layer], up_bias[layer], mlp_units[layer]],
            20,
        )
        saved.append((residual, first, qkv, attended, lse, middle, second, hidden, slope))
        residual = output

    def wide(values):
        return jnp.pad(values.reshape(ni, -1), ((0, HR - ni), (0, 0)))

    lanes = jnp.arange(wc, dtype=jnp.int32)
    class_ids = jnp.where(lanes[None] < cl, jnp.arange(mp, dtype=jnp.int32)[:, None] * cl + lanes[None], -1)[:, None]
    head_mine, head_other, head_bgrad, grad, final_vgrad, loss_part = call(
        functools.partial(head_kernel, mp, ni, wc),
        [
            ((mp, half, 2 * wc), BF),
            ((mp, half, 2 * wc), BF),
            ((mp, 1, 2 * wc), F32),
            ((n, D), F32),
            ((8, D), F32),
            ((8, 128), F32),
        ],
        [
            pltpu.VMEM((mp, D, 2 * wc), BF),
            pltpu.VMEM((HR, D), F32),
            pltpu.VMEM((HR, D), F32),
            pltpu.VMEM((D, 2 * wc), BF),
            pltpu.SemaphoreType.DMA((parts,)),
        ],
        [
            ("smem", place),
            residual,
            final_vec,
            head_bias,
            class_ids,
            wide(label_ids),
            wide(label_mix),
            wide(0.5 * image_weight / weight_sum),
            wide(image_weight / weight_sum),
            wide(pooled),
            teacher_all,
            head_unit,
        ],
        8,
    )
    head_scatter = Scatter(head_mine, head_other)
    flying = [head_scatter]
    sending = [head_other]

    def proceed(fresh):
        moved = [array for unit in flying for array in unit.step()]
        flying.append(fresh)
        return moved

    attn_list, mlp_list = [None] * L, [None] * L
    gain_list, bias_list = [None] * L, [None] * L
    for layer in reversed(range(L)):
        resid_in, first, qkv, attended, lse, middle, second, hidden, slope = saved[layer]
        gmid, mlp_mine, mlp_other, up_bgrad, mlp_vgrad = call(
            functools.partial(mlp_backward_kernel, mp),
            [
                ((n, D), F32),
                ((mp, half, 2 * fl), BF),
                ((mp, half, 2 * fl), BF),
                ((mp, 1, fl), F32),
                ((8, D), F32),
            ],
            [
                pltpu.VMEM((mp, D, 2 * fl), BF),
                pltpu.VMEM((n, D), BF),
                pltpu.VMEM((D, n), BF),
                pltpu.VMEM((D, n), BF),
                pltpu.VMEM((D, 2 * fl), BF),
                pltpu.SemaphoreType.DMA((parts,)),
            ],
            [
                ("smem", place),
                grad,
                middle,
                layer_vecs[layer],
                second,
                hidden,
                slope,
                mlp_units[layer],
            ],
            27,
            sending,
        )
        mlp_list[layer] = Scatter(mlp_mine, mlp_other)
        sending = proceed(mlp_list[layer])
        grad, attn_mine, attn_other, qkv_bgrad, attn_vgrad = call(
            functools.partial(attn_backward_kernel, mp, ni, wl),
            [
                ((n, D), F32),
                ((mp, half, 4 * wl), BF),
                ((mp, half, 4 * wl), BF),
                ((mp, 1, 3 * wl), F32),
                ((8, D), F32),
            ],
            [
                pltpu.VMEM((mp, D, 4 * wl), BF),
                pltpu.VMEM((n, D), BF),
                pltpu.VMEM((D, n), BF),
                pltpu.VMEM((D, n), BF),
                pltpu.VMEM((n, wl), BF),
                pltpu.VMEM((n, 3 * wl), BF),
                pltpu.VMEM((D, 4 * wl), BF),
                pltpu.SemaphoreType.DMA((parts,)),
            ],
            [
                ("smem", place),
                gmid,
                resid_in,
                layer_vecs[layer],
                live_rows,
                first,
                qkv,
                attended,
                lse,
                attn_units[layer],
            ],
            33,
            sending,
        )
        attn_list[layer] = Scatter(attn_mine, attn_other)
        sending = proceed(attn_list[layer])
        gain_list[layer] = (attn_vgrad + mlp_vgrad)[:6]
        bias_list[layer] = jnp.concatenate(
            [qkv_bgrad[:, 0, :wl], qkv_bgrad[:, 0, 2 * wl :], up_bgrad[:, 0]], axis=1
        )

    patch_grad = dot_tn(patch_rows, grad.astype(BF)).astype(BF)
    patch_grad = patch_grad.reshape(dp, 2, mp, quarter, D).transpose(1, 2, 0, 3, 4)
    patch_grad = patch_grad.reshape(2, mp, dp * quarter, D)
    patch_grad = Scatter(
        lax.dynamic_index_in_dim(patch_grad, here_teach, 0, False),
        lax.dynamic_index_in_dim(patch_grad, 1 - here_teach, 0, False),
    ).result()
    patch_grad = outward(gather_mp(patch_grad).reshape(rows_own, D))

    source_grads = lax.dot_general(
        sources, grad, (((0,), (0,)), ((), ())), precision=HIGH, preferred_element_type=F32
    )
    vector_grads = outward(
        jnp.concatenate(gain_list + [final_vgrad[:2], source_grads], axis=0)
    )
    bias_blocks = jnp.concatenate(
        bias_list + [head_bgrad[:, 0, :cl], head_bgrad[:, 0, wc : wc + cl]], axis=1
    )
    bias_size = bias_blocks.shape[1]
    flat = jnp.concatenate([vector_grads.reshape(-1), bias_blocks.reshape(-1)])
    flat = jnp.pad(flat, (0, -flat.size % 1024)).reshape(-1, 128)
    flat = sum_all(flat).reshape(-1)
    vector_grads = flat[: vector_params.size].reshape(vector_params.shape)
    bias_grads = lax.dynamic_slice_in_dim(
        flat, vector_params.size + here_mp * bias_size, bias_size, 0
    )

    attn_list = [unit.result() for unit in attn_list]
    mlp_list = [unit.result() for unit in mlp_list]
    head_grads = head_scatter.result()
    attn_grads = jnp.stack(
        [
            jnp.stack([attn_list[layer][:, part * wl : (part + 1) * wl] for part in range(4)])
            for layer in range(L)
        ]
    )
    mlp_grads = jnp.stack(
        [jnp.stack([mlp_list[layer][:, :fl], mlp_list[layer][:, fl:]]) for layer in range(L)]
    )
    head_grads = jnp.stack([head_grads[:, :cl], head_grads[:, wc : wc + cl]])

    step_power = step_count[0].astype(F32)
    correct_first = 1.0 - jnp.power(BETA, step_power)
    correct_second = 1.0 - jnp.power(BETA, step_power)
    weights = (patch_weight, attn_weight, mlp_weight, head_weight, vector_params, split_biases)
    gradients = (patch_grad, attn_grads, mlp_grads, head_grads, vector_grads, bias_grads)
    firsts = (patch_first, attn_first, mlp_first, head_first, vector_first, bias_first)
    seconds = (patch_second, attn_second, mlp_second, head_second, vector_second, bias_second)
    decay_pieces = expand_params(split_params(decay_mask.astype(F32)))
    results = [
        adam_direction(gradients[slot], firsts[slot], seconds[slot], correct_first, correct_second)
        for slot in range(6)
    ]
    directions = [
        results[slot][2] + DECAY * decay_pieces[slot] * weights[slot] for slot in range(6)
    ]
    totals = sum_all(
        jnp.concatenate(
            [
                squares_of(weights, mp_first, data_first),
                squares_of(directions, mp_first, data_first),
                loss_part[0, :1],
            ]
        )
    )
    npar = (totals.size - 1) // 2
    weights_sq, direction_sq, loss_value = totals[:npar], totals[npar : 2 * npar], totals[2 * npar]
    weight_norm = jnp.sqrt(weights_sq)
    update_norm = jnp.sqrt(direction_sq)
    trust_ratio = weight_norm / update_norm
    rates = BASE_RATE * jnp.power(LAYER_DECAY, 2.0 - layer_ids.astype(F32)) * trust_ratio
    rate_pieces = expand_params(split_params(rates))
    updated = [weights[slot] - rate_pieces[slot] * directions[slot] for slot in range(6)]
    norm_table = jnp.stack([weight_norm, update_norm])
    return (
        *updated,
        *[results[slot][0] for slot in range(6)],
        *[results[slot][1] for slot in range(6)],
        norm_table,
        trust_ratio,
        loss_value,
    )


def solution(mesh):
    rows = ("dp", "teach")
    moments = (
        P(rows, None),
        P(None, None, rows, "mp"),
        P(None, None, rows, "mp"),
        P(None, rows, "mp"),
        P(),
        P("mp"),
    )
    placed = (
        P(rows, None, None),
        P(rows, None),
        P(rows, None),
        P(rows),
        P(rows),
        P(),
        P(None, "mp"),
        *moments,
        *moments,
        *moments,
        P(),
        P(),
        P(),
    )
    return jax.shard_map(
        per_device,
        mesh=mesh,
        in_specs=placed,
        out_specs=(*moments, *moments, *moments, P(), P(), P()),
        check_vma=False,
    )
```

```python
import functools

import jax
import jax.numpy as jnp
from jax import lax
from jax.experimental import pallas as pl
from jax.experimental.pallas import tpu as pltpu
from jax.sharding import PartitionSpec as P

D = 768
HD = 64
G = 24
PMAX = 280
L = 2
RP = 288
TOK = 280
HR = 16

EPS_NORM = 1e-06
EPS_LAMB = 1e-06
BETA = 0.5
DECAY = 0.05
BASE_RATE = 0.4
LAYER_DECAY = 0.8
SCALE = 0.125
MASKED = -1e30
HIGH = lax.Precision.HIGHEST
ROOT_HALF = 0.7071067811865476
DENSITY = 0.3989422804014327
BF = jnp.bfloat16
F32 = jnp.float32
ALL = ("dp", "mp", "teach")
VMEM_LIMIT = 56 * 1024 * 1024
FLOP_PER_US = 1_150_000_000
BRIEF = 2
FAR = 3
PARTS = ((3, 1), (2, 0))


def dot_nn(left, right):
    return lax.dot_general(
        left, right, (((1,), (0,)), ((), ())), preferred_element_type=F32
    )


def dot_nt(left, right):
    return lax.dot_general(
        left, right, (((1,), (1,)), ((), ())), preferred_element_type=F32
    )


def dot_tn(left, right):
    return lax.dot_general(
        left, right, (((0,), (0,)), ((), ())), preferred_element_type=F32
    )


def gelu_erf(values):
    return 0.5 * values * (1.0 + lax.erf(values * ROOT_HALF))


def norm_stats(values):
    centre = values - jnp.mean(values, axis=-1, keepdims=True)
    scaled = lax.rsqrt(jnp.mean(centre * centre, axis=-1, keepdims=True) + EPS_NORM)
    return centre * scaled, scaled


def norm_back(grad_out, normed, scaled, gain_row):
    grad_normed = grad_out * gain_row
    inner_sum = jnp.mean(grad_normed, axis=-1, keepdims=True)
    cross_term = jnp.mean(grad_normed * normed, axis=-1, keepdims=True)
    return scaled * (grad_normed - inner_sum - normed * cross_term)


def row_sum(values):
    return jnp.sum(values, axis=0, keepdims=True)


def weight_copies(place_ref, steps, own, other, buf, sems):
    half = own[0].shape[0]
    here = place_ref[0]
    slots, sem = [], 0
    for slot, step in enumerate(steps):
        pieces = (FAR, FAR + 1) if step == FAR else (step,)
        copies = []
        for piece in pieces:
            size = half // len(pieces)
            for source, core in ((own[piece], here), (other[piece], 1 - here)):
                at = pl.multiple_of(core * half + (piece - pieces[0]) * size, 64)
                copies.append(
                    pltpu.make_async_copy(source, buf.at[slot, pl.ds(at, size)], sems.at[sem])
                )
                sem += 1
        slots.append(copies)
    return slots


def start_all(slots):
    for copies in slots:
        for copy in copies:
            copy.start()


def wait_slot(slots, now):
    for slot, copies in enumerate(slots):

        @pl.when(now == slot)
        def _():
            for copy in copies:
                copy.wait()


def split_out(half, place_ref, grad_buf, mine_ref, other_ref, slot):
    mine = pl.multiple_of(place_ref[0] * half, 128)
    theirs = pl.multiple_of((1 - place_ref[0]) * half, 128)
    mine_ref[slot] = grad_buf[pl.ds(mine, half), :]
    other_ref[slot] = grad_buf[pl.ds(theirs, half), :]


def attn_forward_kernel(
    mp,
    ni,
    wl,
    place_ref,
    resid_ref,
    vec_ref,
    bias_ref,
    live_ref,
    own,
    other,
    first_ref,
    qkv_ref,
    att_ref,
    lse_ref,
    mid_ref,
    buf,
    sems,
):
    now = pl.program_id(0)
    slots = weight_copies(place_ref, range(mp), own, other, buf, sems)

    @pl.when(now == 0)
    def _():
        start_all(slots)
        resid = resid_ref[...]
        normed, _ = norm_stats(resid)
        first_ref[...] = (normed * vec_ref[0:1] + vec_ref[1:2]).astype(BF)
        mid_ref[...] = resid + vec_ref[4:5]

    wait_slot(slots, now)
    qkv = dot_nn(first_ref[...], buf[now, :, : 3 * wl]) + bias_ref[0]
    qkv_ref[0] = qkv.astype(BF)
    for image in range(ni):
        rows = slice(image * RP, (image + 1) * RP)
        live = live_ref[image] > 0.0
        for head in range(wl // HD):
            at = head * HD
            queries = qkv_ref[0, rows, at : at + HD]
            keys = qkv_ref[0, rows, wl + at : wl + at + HD]
            vals = qkv_ref[0, rows, 2 * wl + at : 2 * wl + at + HD]
            scores = jnp.where(live, dot_nt(queries, keys) * SCALE, MASKED)
            peak = jnp.max(scores, axis=-1, keepdims=True)
            expo = jnp.exp(scores - peak)
            total = jnp.sum(expo, axis=-1, keepdims=True)
            soft = (expo * (1.0 / total)).astype(BF)
            att_ref[0, rows, at : at + HD] = dot_nn(soft, vals).astype(BF)
            lse_ref[0, rows, head : head + 1] = peak + jnp.log(total)
    mid_ref[...] += dot_nt(att_ref[0], buf[now, :, 3 * wl :])


def mlp_forward_kernel(
    mp,
    chunk,
    place_ref,
    mid_ref,
    vec_ref,
    bias_ref,
    own,
    other,
    second_ref,
    hidden_ref,
    slope_ref,
    out_ref,
    buf,
    sems,
):
    now = pl.program_id(0)
    fl = hidden_ref.shape[2]
    slots = weight_copies(place_ref, range(mp), own, other, buf, sems)

    @pl.when(now == 0)
    def _():
        start_all(slots)
        middle = mid_ref[...]
        normed, _ = norm_stats(middle)
        second_ref[...] = (normed * vec_ref[2:3] + vec_ref[3:4]).astype(BF)
        out_ref[...] = middle + vec_ref[5:6]

    wait_slot(slots, now)
    for start in range(0, mid_ref.shape[0], chunk):
        rows = slice(start, start + chunk)
        upward = dot_nn(second_ref[rows, :], buf[now, :, :fl]) + bias_ref[0]
        share = 0.5 + 0.5 * lax.erf(upward * ROOT_HALF)
        hidden = (upward * share).astype(BF)
        hidden_ref[0, rows, :] = hidden
        slope_ref[0, rows, :] = share + upward * (DENSITY * jnp.exp(-0.5 * upward * upward))
        out_ref[rows, :] += dot_nt(hidden, buf[now, :, fl:])


def head_kernel(
    mp,
    ni,
    wc,
    place_ref,
    resid_ref,
    vec_ref,
    bias_ref,
    ids_ref,
    labels_ref,
    mix_ref,
    scale_ref,
    weight_ref,
    pooled_ref,
    teacher_ref,
    own,
    other,
    mine_ref,
    other_ref,
    hbias_ref,
    grad_ref,
    vgrad_ref,
    loss_ref,
    buf,
    cls_buf,
    dist_buf,
    gw_buf,
    sems,
):
    half = mine_ref.shape[1]
    slots = weight_copies(place_ref, range(mp), own, other, buf, sems)
    start_all(slots)
    cls_buf[...] = jnp.zeros_like(cls_buf)
    dist_buf[...] = jnp.zeros_like(dist_buf)
    for image in range(ni):
        at = image * RP + TOK
        cls_buf[image : image + 1, :] = resid_ref[at : at + 1, :]
        dist_buf[image : image + 1, :] = resid_ref[at + 1 : at + 2, :]
    grad_ref[...] = jnp.zeros_like(grad_ref)
    normed_c, scaled_c = norm_stats(cls_buf[...])
    normed_d, scaled_d = norm_stats(dist_buf[...])
    gain, shift = vec_ref[0:1], vec_ref[1:2]
    final_c = (normed_c * gain + shift).astype(BF)
    final_d = (normed_d * gain + shift).astype(BF)
    for copies in slots:
        for copy in copies:
            copy.wait()
    cls, dist, teach, goal = [], [], [], []
    mix = mix_ref[:, 0:1]
    for block in range(mp):
        ids = ids_ref[block]
        valid = ids >= 0
        both = bias_ref[block]
        cls.append(
            jnp.where(valid, dot_nn(final_c, buf[block, :, :wc]) + both[:, :wc], MASKED)
        )
        dist.append(
            jnp.where(valid, dot_nn(final_d, buf[block, :, wc:]) + both[:, wc:], MASKED)
        )
        teach.append(jnp.where(valid, dot_nn(pooled_ref[...], teacher_ref[block]), MASKED))
        first = (labels_ref[:, 0:1] == ids).astype(F32)
        second = (labels_ref[:, 1:2] == ids).astype(F32)
        goal.append(mix * first + (1.0 - mix) * second)

    def log_total(parts):
        peak = functools.reduce(
            jnp.maximum, [jnp.max(part, axis=-1, keepdims=True) for part in parts]
        )
        total = sum(jnp.sum(jnp.exp(part - peak), axis=-1, keepdims=True) for part in parts)
        return peak + jnp.log(total)

    log_c, log_d, log_t = log_total(cls), log_total(dist), log_total(teach)
    prob = [jnp.exp(part - log_t) for part in teach]
    dot_c = sum(jnp.sum(g * c, axis=-1, keepdims=True) for g, c in zip(goal, cls))
    dot_d = sum(jnp.sum(p * d, axis=-1, keepdims=True) for p, d in zip(prob, dist))
    loss_rows = 0.5 * (log_c - dot_c) + 0.5 * (log_d - dot_d)
    loss_ref[...] = jnp.broadcast_to(row_sum(weight_ref[:, 0:1] * loss_rows), loss_ref.shape)
    scale = scale_ref[:, 0:1]
    gfin_c = jnp.zeros(cls_buf.shape, F32)
    gfin_d = jnp.zeros(dist_buf.shape, F32)
    for block in range(mp):
        grad_c = scale * (jnp.exp(cls[block] - log_c) - goal[block])
        grad_d = scale * (jnp.exp(dist[block] - log_d) - prob[block])
        hbias_ref[block, :, :wc] = row_sum(grad_c)
        hbias_ref[block, :, wc:] = row_sum(grad_d)
        low_c, low_d = grad_c.astype(BF), grad_d.astype(BF)
        gw_buf[:, :wc] = dot_tn(final_c, low_c).astype(BF)
        gw_buf[:, wc:] = dot_tn(final_d, low_d).astype(BF)
        split_out(half, place_ref, gw_buf, mine_ref, other_ref, block)
        gfin_c += dot_nt(low_c, buf[block, :, :wc])
        gfin_d += dot_nt(low_d, buf[block, :, wc:])
    vgrad_ref[...] = jnp.zeros_like(vgrad_ref)
    vgrad_ref[0:1, :] = row_sum(gfin_c * normed_c) + row_sum(gfin_d * normed_d)
    vgrad_ref[1:2, :] = row_sum(gfin_c) + row_sum(gfin_d)
    cls_buf[...] = norm_back(gfin_c, normed_c, scaled_c, gain)
    dist_buf[...] = norm_back(gfin_d, normed_d, scaled_d, gain)
    for image in range(ni):
        at = image * RP + TOK
        grad_ref[at : at + 1, :] = cls_buf[image : image + 1, :]
        grad_ref[at + 1 : at + 2, :] = dist_buf[image : image + 1, :]


def mlp_backward_kernel(
    steps,
    last,
    place_ref,
    grad_ref,
    mid_ref,
    vec_ref,
    second_ref,
    hidden_ref,
    slope_ref,
    own,
    other,
    *rest,
):
    if steps[0] != FAR:
        part_ref, *rest = rest
    (
        gmid_ref,
        mine_ref,
        other_ref,
        gbias_ref,
        vgrad_ref,
        buf,
        branch_buf,
        branch_t,
        second_t,
        gw_buf,
        sems,
    ) = rest
    now = pl.program_id(0)
    fl = hidden_ref.shape[2]
    half = mine_ref.shape[1]
    slots = weight_copies(place_ref, steps, own, other, buf, sems)

    @pl.when(now == 0)
    def _():
        start_all(slots)
        branch_buf[...] = grad_ref[...].astype(BF)
        branch_t[...] = branch_buf[...].T
        second_t[...] = second_ref[...].T
        if steps[0] == FAR:
            gmid_ref[...] = jnp.zeros_like(gmid_ref)
        else:
            gmid_ref[...] = part_ref[...]
        vgrad_ref[...] = jnp.zeros_like(vgrad_ref)

    wait_slot(slots, now)
    gup = (dot_nn(branch_buf[...], buf[now, :, fl:]) * slope_ref[0]).astype(BF)
    gbias_ref[0] = row_sum(gup.astype(F32))
    gmid_ref[...] += dot_nt(gup, buf[now, :, :fl])
    gw_buf[:, :fl] = dot_nn(second_t[...], gup).astype(BF)
    gw_buf[:, fl:] = dot_nn(branch_t[...], hidden_ref[0]).astype(BF)
    split_out(half, place_ref, gw_buf, mine_ref, other_ref, 0)
    if last:

        @pl.when(now == len(steps) - 1)
        def _():
            normed, scaled = norm_stats(mid_ref[...])
            gsec = gmid_ref[...]
            grad = grad_ref[...]
            vgrad_ref[2:3, :] = row_sum(gsec * normed)
            vgrad_ref[3:4, :] = row_sum(gsec)
            vgrad_ref[5:6, :] = row_sum(grad)
            gmid = norm_back(gsec, normed, scaled, vec_ref[2:3]) + grad
            vgrad_ref[4:5, :] = row_sum(gmid)
            gmid_ref[...] = gmid


def attn_backward_kernel(
    ni,
    wl,
    steps,
    last,
    place_ref,
    gmid_ref,
    resid_ref,
    vec_ref,
    live_ref,
    first_ref,
    qkv_ref,
    att_ref,
    lse_ref,
    own,
    other,
    *rest,
):
    if steps[0] != FAR:
        part_ref, *rest = rest
    (
        gres_ref,
        mine_ref,
        other_ref,
        gbias_ref,
        vgrad_ref,
        buf,
        mixed_buf,
        mixed_t,
        first_t,
        gatt_buf,
        gqkv_buf,
        gw_buf,
        sems,
    ) = rest
    now = pl.program_id(0)
    half = mine_ref.shape[1]
    slots = weight_copies(place_ref, steps, own, other, buf, sems)

    @pl.when(now == 0)
    def _():
        start_all(slots)
        mixed_buf[...] = gmid_ref[...].astype(BF)
        mixed_t[...] = mixed_buf[...].T
        first_t[...] = first_ref[...].T
        if steps[0] == FAR:
            gres_ref[...] = jnp.zeros_like(gres_ref)
        else:
            gres_ref[...] = part_ref[...]
        vgrad_ref[...] = jnp.zeros_like(vgrad_ref)

    wait_slot(slots, now)
    gatt_buf[...] = dot_nn(mixed_buf[...], buf[now, :, 3 * wl :]).astype(BF)
    for image in range(ni):
        rows = slice(image * RP, (image + 1) * RP)
        live = live_ref[image] > 0.0
        for head in range(wl // HD):
            at = head * HD
            queries = qkv_ref[0, rows, at : at + HD]
            keys = qkv_ref[0, rows, wl + at : wl + at + HD]
            vals = qkv_ref[0, rows, 2 * wl + at : 2 * wl + at + HD]
            gatt = gatt_buf[rows, at : at + HD]
            scores = jnp.where(live, dot_nt(queries, keys) * SCALE, MASKED)
            soft = jnp.exp(scores - lse_ref[0, rows, head : head + 1])
            gsoft = dot_nt(gatt, vals)
            inner = jnp.sum(soft * gsoft, axis=-1, keepdims=True)
            gscore = (soft * (gsoft - inner)).astype(BF)
            gqkv_buf[rows, at : at + HD] = (dot_nn(gscore, keys) * SCALE).astype(BF)
            gqkv_buf[rows, wl + at : wl + at + HD] = (dot_tn(gscore, queries) * SCALE).astype(BF)
            gqkv_buf[rows, 2 * wl + at : 2 * wl + at + HD] = dot_tn(soft.astype(BF), gatt).astype(BF)
    gqkv = gqkv_buf[...]
    gbias_ref[0] = row_sum(gqkv.astype(F32))
    gres_ref[...] += dot_nt(gqkv, buf[now, :, : 3 * wl])
    gw_buf[:, : 3 * wl] = dot_nn(first_t[...], gqkv).astype(BF)
    gw_buf[:, 3 * wl :] = dot_nn(mixed_t[...], att_ref[0]).astype(BF)
    split_out(half, place_ref, gw_buf, mine_ref, other_ref, 0)
    if last:

        @pl.when(now == len(steps) - 1)
        def _():
            normed, scaled = norm_stats(resid_ref[...])
            gfirst = gres_ref[...]
            vgrad_ref[0:1, :] = row_sum(gfirst * normed)
            vgrad_ref[1:2, :] = row_sum(gfirst)
            gres_ref[...] = norm_back(gfirst, normed, scaled, vec_ref[0:1]) + gmid_ref[...]


def call(kernel, outs, scratch, ins, steps=None, after=()):
    def whole(array):
        return pl.BlockSpec(array.shape, lambda i: (0,) * array.ndim)

    def each(array, base=0, stride=1):
        return pl.BlockSpec(
            (1, *array.shape[1:]), lambda i: (base + stride * i, *(0,) * (array.ndim - 1))
        )

    specs, arrays, sizes = [], [], []
    for item in [*ins, ("group", list(after))]:
        kind, item = item if isinstance(item, tuple) else ("vmem", item)
        group = item if kind == "group" else [item]
        sizes.append(len(group) if kind == "group" else None)
        if kind in ("group", "smem"):
            space = pl.ANY if kind == "group" else pltpu.SMEM
            specs += [pl.BlockSpec(memory_space=space)] * len(group)
        elif kind == "each":
            specs.append(each(item, steps[0], steps[1] - steps[0]))
        elif steps:
            specs.append(whole(item))
        else:
            specs.append(pl.BlockSpec(memory_space=pltpu.VMEM))
        arrays += group

    def grouped(*refs):
        given, at = [], 0
        for size in sizes:
            given.append(refs[at] if size is None else refs[at : at + size])
            at += 1 if size is None else size
        return kernel(*given[:-1], *refs[at:])

    out_shape = [jax.ShapeDtypeStruct(*out[:2]) for out in outs]
    if steps:
        out_specs = [
            each(shape) if len(out) > 2 else whole(shape) for out, shape in zip(outs, out_shape)
        ]
        grid = {"grid": (len(steps),)}
    else:
        out_specs = [pl.BlockSpec(memory_space=pltpu.VMEM)] * len(out_shape)
        grid = {}
    moved = sum(a.size * a.dtype.itemsize for a in arrays)
    moved += sum(s.size * s.dtype.itemsize for s in out_shape)
    return pl.pallas_call(
        grouped,
        out_shape=out_shape,
        in_specs=specs,
        out_specs=out_specs,
        **grid,
        scratch_shapes=scratch,
        compiler_params=pltpu.CompilerParams(vmem_limit_bytes=VMEM_LIMIT),
        cost_estimate=pl.CostEstimate(
            flops=BRIEF * FLOP_PER_US, bytes_accessed=moved, transcendentals=0
        ),
    )(*arrays)


def tie(values, *behind):
    if not behind:
        return values
    return lax.optimization_barrier((values, behind))[0]


def swap(values, axis, distance):
    size = lax.axis_size(axis)
    return lax.ppermute(values, axis, [(rank, rank ^ distance) for rank in range(size)])


class Gather:
    def __init__(self, near):
        self.near = near

    def square(self, *behind):
        near = tie(self.near, *behind)
        self.own = [near, swap(near, "mp", 1), swap(near, "mp", 2)]
        self.other = [swap(near, "teach", 1)]

    def corner(self, *behind):
        near, by_one, by_two = self.own
        cut = near.shape[0] // 2
        by_one, by_two = tie((by_one, by_two), *behind)
        self.own = [near, by_one, by_two, swap(by_two[:cut], "mp", 1), swap(by_one[cut:], "mp", 2)]
        self.other += [swap(by_one, "teach", 1), swap(by_two, "teach", 1)]

    def cores(self, *behind):
        far = tie(tuple(self.own[3:]), *behind)
        self.own[3:] = far
        self.other += [swap(piece, "teach", 1) for piece in far]

    def refs(self):
        return [("group", self.own), ("group", self.other)]


def add_low(left, right):
    return (left.astype(F32) + right.astype(F32)).astype(BF)


def sum_over(values, axis):
    distance = 1
    while distance < lax.axis_size(axis):
        values = values + swap(values, axis, distance)
        distance *= 2
    return values


def sum_all(values):
    for axis in ("teach", "mp", "dp"):
        values = sum_over(values, axis)
    return values


def gather_mp(values):
    size = lax.axis_size("mp")
    return jnp.stack([values] + [swap(values, "mp", step) for step in range(1, size)])


class Scatter:
    def __init__(self):
        self.waiting = []
        self.block = {}
        self.total = None

    def cores(self, steps, mine, other):
        self.waiting.append((steps, mine, swap(other, "teach", 1)))

    def added(self, *behind):
        for steps, mine, got in self.waiting:
            got = tie(got, *behind)
            for slot, step in enumerate(steps):
                self.block[step] = add_low(mine[slot], got[slot])
        self.waiting = []

    def corner(self, *behind):
        self.added(*behind)
        cut = self.block[FAR].shape[0] // 2
        sent = [self.block[FAR][:cut], self.block[FAR][cut:]]
        self.by_one = swap(sent[0], "mp", 1)
        self.by_two = swap(sent[1], "mp", 2)
        return sent

    def square(self, *behind):
        self.added(*behind)
        one, two = self.block[1], self.block[2]
        cut = one.shape[0] // 2
        by_one, by_two = tie((self.by_one, self.by_two), *behind)
        sent = [
            jnp.concatenate([one[:cut], add_low(one[cut:], by_two)]),
            jnp.concatenate([add_low(two[:cut], by_one), two[cut:]]),
        ]
        self.by_one = swap(sent[0], "mp", 1)
        self.by_two = swap(sent[1], "mp", 2)
        return sent

    def rows(self, *behind):
        by_one, by_two = tie((self.by_one, self.by_two), *behind)
        total = self.block[0].astype(F32) + (by_one.astype(F32) + by_two.astype(F32))
        total = total.astype(BF)
        self.total = lax.psum_scatter(total, "dp", scatter_dimension=0, tiled=True)
        return [total]

    def result(self):
        return self.total.astype(F32)


def adam_direction(gradient, first_moment, second_moment, correct_first, correct_second):
    new_first = BETA * first_moment + (1.0 - BETA) * gradient
    new_second = BETA * second_moment + (1.0 - BETA) * gradient * gradient
    return (
        new_first,
        new_second,
        new_first / correct_first / (jnp.sqrt(new_second / correct_second) + EPS_LAMB),
    )


def split_params(values):
    layered = values[1 : 1 + 6 * L].reshape(L, 6)
    return (
        values[0],
        layered[:, :4],
        layered[:, 4:],
        values[1 + 6 * L : 3 + 6 * L],
        values[3 + 6 * L],
        values[4 + 6 * L],
    )


def expand_params(pieces):
    return (
        pieces[0],
        pieces[1][:, :, None, None],
        pieces[2][:, :, None, None],
        pieces[3][:, None, None],
        pieces[4],
        pieces[5],
    )


def order_params(pieces):
    layered = jnp.concatenate([pieces[1], pieces[2]], axis=1).reshape(-1)
    return jnp.concatenate([pieces[0][None], layered, pieces[3], pieces[4][None], pieces[5][None]])


def squares_of(pieces, mp_first, data_first):
    return order_params(
        (
            jnp.sum(pieces[0] * pieces[0]) * mp_first,
            jnp.sum(pieces[1] * pieces[1], axis=(2, 3)),
            jnp.sum(pieces[2] * pieces[2], axis=(2, 3)),
            jnp.sum(pieces[3] * pieces[3], axis=(1, 2)),
            jnp.sum(pieces[4] * pieces[4]) * mp_first * data_first,
            jnp.sum(pieces[5] * pieces[5]) * data_first,
        )
    )


def per_device(
    patches,
    grid_sizes,
    label_ids,
    label_mix,
    image_weight,
    teacher_stem,
    teacher_head,
    patch_weight,
    attn_weight,
    mlp_weight,
    head_weight,
    vector_params,
    split_biases,
    patch_first,
    attn_first,
    mlp_first,
    head_first,
    vector_first,
    bias_first,
    patch_second,
    attn_second,
    mlp_second,
    head_second,
    vector_second,
    bias_second,
    decay_mask,
    layer_ids,
    step_count,
):
    dp, mp, teach = lax.axis_size("dp"), lax.axis_size("mp"), lax.axis_size("teach")
    here_mp = lax.axis_index("mp")
    here_teach = lax.axis_index("teach")
    place = ("smem", here_teach.astype(jnp.int32).reshape(1))
    mp_first = (here_mp == 0).astype(F32)
    data_first = (lax.axis_index(("dp", "teach")) == 0).astype(F32)
    rows_own = patch_weight.shape[0]
    half = dp * rows_own
    wl = attn_weight.shape[3]
    fl = mlp_weight.shape[3]
    cl = head_weight.shape[2]
    wc = -(-cl // 128) * 128
    head_row = 6 * L

    def inward(values):
        lead = values.shape[:-1]
        cut = values.reshape(*lead, dp, teach, rows_own)
        return jnp.swapaxes(cut, -3, -2).reshape(*lead, D)

    def outward(values):
        lead = values.shape[:-1]
        cut = values.reshape(*lead, teach, dp, rows_own)
        return jnp.swapaxes(cut, -3, -2).reshape(*lead, D)

    ni = patches.shape[0] // mp

    def take(array):
        return lax.dynamic_slice_in_dim(array, here_mp * ni, ni, 0)

    patches, grid_sizes, label_ids = take(patches), take(grid_sizes), take(label_ids)
    label_mix, image_weight = take(label_mix), take(image_weight)
    weight_sum = sum_all(jnp.sum(image_weight).reshape(1))[0]

    patch_low = inward(patch_weight).astype(BF)
    attn_low = [
        jnp.concatenate([attn_weight[layer, part] for part in range(4)], axis=1).astype(BF)
        for layer in range(L)
    ]
    mlp_low = [
        jnp.concatenate([mlp_weight[layer, 0], mlp_weight[layer, 1]], axis=1).astype(BF)
        for layer in range(L)
    ]
    head_pad = jnp.pad(head_weight, ((0, 0), (0, 0), (0, wc - cl)))
    head_low = jnp.concatenate([head_pad[0], head_pad[1]], axis=1).astype(BF)

    def gather_dp(*pieces):
        wide_piece = lax.all_gather(jnp.concatenate(pieces, axis=1), "dp", axis=0, tiled=True)
        cuts, at = [], 0
        for piece in pieces:
            cuts.append(wide_piece[:, at : at + piece.shape[1]])
            at += piece.shape[1]
        return cuts

    near = gather_dp(patch_low, attn_low[0]) + gather_dp(mlp_low[0])
    rest = [piece for layer in range(1, L) for piece in (attn_low[layer], mlp_low[layer])]
    near += gather_dp(*rest, head_low)
    teacher_all = gather_mp(jnp.pad(teacher_head, ((0, 0), (0, wc - cl))))
    bias_all = gather_mp(split_biases)
    near[0], near[1] = tie((near[0], near[1]), weight_sum, teacher_all, bias_all)
    patch_own = near[0]
    patch_other = swap(patch_own, "teach", 1)
    units = [Gather(piece) for piece in near[1:]]
    attn_units, mlp_units, head_unit = units[0:-1:2], units[1:-1:2], units[-1]

    vec_in = inward(vector_params)
    layer_vecs = [
        jnp.pad(vec_in[6 * layer : 6 * layer + 6], ((0, 2), (0, 0))) for layer in range(L)
    ]
    final_vec = jnp.pad(vec_in[head_row : head_row + 2], ((0, 6), (0, 0)))
    attn_bias, up_bias = [], []
    span = 2 * wl + fl
    for layer in range(L):
        part = bias_all[:, layer * span : (layer + 1) * span]
        zero = jnp.zeros((mp, wl), F32)
        attn_bias.append(
            jnp.concatenate([part[:, :wl], zero, part[:, wl : 2 * wl]], axis=1)[:, None]
        )
        up_bias.append(part[:, None, 2 * wl :])
    pad_class = ((0, 0), (0, wc - cl))
    head_bias = jnp.concatenate(
        [
            jnp.pad(bias_all[:, L * span : L * span + cl], pad_class),
            jnp.pad(bias_all[:, L * span + cl : L * span + 2 * cl], pad_class),
        ],
        axis=1,
    )[:, None]

    grid_rows, grid_cols = grid_sizes[:, 0:1], grid_sizes[:, 1:2]
    slot_ids = jnp.arange(PMAX, dtype=jnp.int32)[None, :]
    patch_live = slot_ids < grid_rows * grid_cols
    live_float = patch_live.astype(F32)
    live_rows = jnp.concatenate(
        [live_float, jnp.ones((ni, 2), F32), jnp.zeros((ni, RP - PMAX - 2), F32)], axis=1
    )[:, None, :]
    table = jnp.arange(G, dtype=jnp.int32)
    source_patch = jnp.concatenate(
        [
            jnp.ones((ni, PMAX, 1), F32),
            jnp.zeros((ni, PMAX, 2), F32),
            ((slot_ids // grid_cols)[..., None] == table).astype(F32),
            ((slot_ids % grid_cols)[..., None] == table).astype(F32),
        ],
        axis=2,
    )
    source_token = jnp.broadcast_to(jnp.eye(2, 3 + 2 * G, 1, dtype=F32), (ni, 2, 3 + 2 * G))
    sources = jnp.concatenate(
        [source_patch, source_token, jnp.zeros((ni, RP - PMAX - 2, 3 + 2 * G), F32)], axis=1
    ).reshape(ni * RP, 3 + 2 * G)

    stem_rows = gelu_erf(dot_nn(patches.reshape(ni * PMAX, -1), teacher_stem)).reshape(ni, PMAX, -1)
    pooled = (
        jnp.sum(stem_rows * live_float[..., None], axis=1)
        / jnp.sum(live_float, axis=1, keepdims=True)
    ).astype(BF)

    first_core = here_teach == 0
    patch_full = jnp.stack(
        [
            jnp.where(first_core, patch_own, patch_other).reshape(dp, rows_own, D),
            jnp.where(first_core, patch_other, patch_own).reshape(dp, rows_own, D),
        ],
        axis=1,
    ).reshape(D, D)
    patch_rows = jnp.pad(patches, ((0, 0), (0, RP - PMAX), (0, 0))).reshape(ni * RP, -1)
    residual = dot_nn(patch_rows, patch_full) + jnp.dot(
        sources, vec_in[head_row + 2 :], precision=HIGH
    )

    n = ni * RP
    parts = 2 * mp + 2
    saved = []
    def wide(values):
        return jnp.pad(values.reshape(ni, -1), ((0, HR - ni), (0, 0)))

    ranks = here_mp ^ jnp.arange(mp, dtype=jnp.int32)
    lanes = jnp.arange(wc, dtype=jnp.int32)
    class_ids = jnp.where(lanes[None] < cl, ranks[:, None] * cl + lanes[None], -1)[:, None]
    head_small = [
        class_ids,
        wide(label_ids),
        wide(label_mix),
        wide(0.5 * image_weight / weight_sum),
        wide(image_weight / weight_sum),
        wide(pooled),
    ]

    first_unit = units[0]
    first_unit.square()
    first_unit.corner(residual)
    units[1].square(*first_unit.own[3:])

    def arrive(at, done):
        here = units[at]
        ahead = units[at + 1 : at + 2] if at < len(units) - 3 else units[at + 1 :]
        if at == 0:
            here.cores()
            return [units[1].own[0], near[-1], *head_small, head_bias, *attn_bias, *up_bias]
        if at < len(units) - 2:
            here.corner(done)
            for unit in ahead:
                unit.square(*here.own[3:], done)
            here.cores(*[unit.own[0] for unit in ahead])
            return [unit.own[0] for unit in ahead]
        if at == len(units) - 2:
            here.corner(done)
            units[-1].corner(done)
            here.cores()
            units[-1].cores()
        return []

    for layer in range(L):
        sending = arrive(2 * layer, residual)
        first, qkv, attended, lse, middle = call(
            functools.partial(attn_forward_kernel, mp, ni, wl),
            [
                ((n, D), BF),
                ((mp, n, 3 * wl), BF, "each"),
                ((mp, n, wl), BF, "each"),
                ((mp, n, wl // HD), F32, "each"),
                ((n, D), F32),
            ],
            [pltpu.VMEM((mp, D, 4 * wl), BF), pltpu.SemaphoreType.DMA((parts,))],
            [place, residual, layer_vecs[layer], ("each", attn_bias[layer]), live_rows]
            + attn_units[layer].refs(),
            range(mp),
            sending,
        )
        sending = arrive(2 * layer + 1, middle)
        second, hidden, slope, output = call(
            functools.partial(mlp_forward_kernel, mp, n // 4),
            [((n, D), BF), ((mp, n, fl), BF, "each"), ((mp, n, fl), F32, "each"), ((n, D), F32)],
            [pltpu.VMEM((mp, D, 2 * fl), BF), pltpu.SemaphoreType.DMA((parts,))],
            [place, middle, layer_vecs[layer], ("each", up_bias[layer])]
            + mlp_units[layer].refs(),
            range(mp),
            sending,
        )
        saved.append((residual, first, qkv, attended, lse, middle, second, hidden, slope))
        residual = output

    head_mine, head_other, head_bgrad, grad, final_vgrad, loss_part = call(
        functools.partial(head_kernel, mp, ni, wc),
        [
            ((mp, half, 2 * wc), BF),
            ((mp, half, 2 * wc), BF),
            ((mp, 1, 2 * wc), F32),
            ((n, D), F32),
            ((8, D), F32),
            ((8, 128), F32),
        ],
        [
            pltpu.VMEM((mp, D, 2 * wc), BF),
            pltpu.VMEM((HR, D), F32),
            pltpu.VMEM((HR, D), F32),
            pltpu.VMEM((D, 2 * wc), BF),
            pltpu.SemaphoreType.DMA((parts,)),
        ],
        [
            place,
            residual,
            final_vec,
            head_bias,
            *head_small,
            teacher_all,
            *head_unit.refs(),
        ],
    )
    head_out = Scatter()
    head_out.cores(range(mp), head_mine, head_other)
    mlp_out, attn_out = [Scatter() for _ in range(L)], [Scatter() for _ in range(L)]
    agenda = {0: [], 1: [(head_out, "corner")], 2: [(head_out, "square")], 3: [(head_out, "rows")]}
    slot = 0
    for layer in reversed(range(L)):
        for at, unit in ((slot + 1, mlp_out[layer]), (slot + 3, attn_out[layer])):
            wait = 2 if unit is mlp_out[layer] else 1
            for moment, what in ((at + 1, "corner"), (at + 2, "square"), (at + 2 + wait, "rows")):
                agenda.setdefault(moment, []).append((unit, what))
        slot += 4
    final = slot

    def proceed(moment, done):
        sent = []
        for unit, what in agenda.pop(moment, []):
            sent += getattr(unit, what)(done)
        return sent

    sending = [head_other]
    gain_list, bias_list = [None] * L, [None] * L
    slot = 0
    for layer in reversed(range(L)):
        resid_in, first, qkv, attended, lse, middle, second, hidden, slope = saved[layer]
        part = []
        up_bgrad, qkv_bgrad = {}, {}
        for steps in PARTS:
            count = len(steps)
            gmid, mine, other, bgrad, mlp_vgrad = call(
                functools.partial(mlp_backward_kernel, steps, steps is PARTS[-1]),
                [
                    ((n, D), F32),
                    ((count, half, 2 * fl), BF, "each"),
                    ((count, half, 2 * fl), BF, "each"),
                    ((count, 1, fl), F32, "each"),
                    ((8, D), F32),
                ],
                [
                    pltpu.VMEM((count, D, 2 * fl), BF),
                    pltpu.VMEM((n, D), BF),
                    pltpu.VMEM((D, n), BF),
                    pltpu.VMEM((D, n), BF),
                    pltpu.VMEM((D, 2 * fl), BF),
                    pltpu.SemaphoreType.DMA((2 * count + 2,)),
                ],
                [place, grad, middle, layer_vecs[layer], second, ("each", hidden), ("each", slope)]
                + mlp_units[layer].refs()
                + part,
                steps,
                sending,
            )
            part = [gmid]
            up_bgrad.update({step: bgrad[at, 0] for at, step in enumerate(steps)})
            slot += 1
            mlp_out[layer].cores(steps, mine, other)
            sending = [other] + proceed(slot, gmid)
        part = []
        for steps in PARTS:
            count = len(steps)
            grad, mine, other, bgrad, attn_vgrad = call(
                functools.partial(attn_backward_kernel, ni, wl, steps, steps is PARTS[-1]),
                [
                    ((n, D), F32),
                    ((count, half, 4 * wl), BF, "each"),
                    ((count, half, 4 * wl), BF, "each"),
                    ((count, 1, 3 * wl), F32, "each"),
                    ((8, D), F32),
                ],
                [
                    pltpu.VMEM((count, D, 4 * wl), BF),
                    pltpu.VMEM((n, D), BF),
                    pltpu.VMEM((D, n), BF),
                    pltpu.VMEM((D, n), BF),
                    pltpu.VMEM((n, wl), BF),
                    pltpu.VMEM((n, 3 * wl), BF),
                    pltpu.VMEM((D, 4 * wl), BF),
                    pltpu.SemaphoreType.DMA((2 * count + 2,)),
                ],
                [place, gmid, resid_in, layer_vecs[layer], live_rows, first]
                + [("each", qkv), ("each", attended), ("each", lse)]
                + attn_units[layer].refs()
                + part,
                steps,
                sending,
            )
            part = [grad]
            qkv_bgrad.update({step: bgrad[at, 0] for at, step in enumerate(steps)})
            slot += 1
            attn_out[layer].cores(steps, mine, other)
            sending = [other] + proceed(slot, grad)
        gain_list[layer] = (attn_vgrad + mlp_vgrad)[:6]
        bias_list[layer] = jnp.stack(
            [
                jnp.concatenate(
                    [qkv_bgrad[step][:wl], qkv_bgrad[step][2 * wl :], up_bgrad[step]]
                )
                for step in range(mp)
            ]
        )
    for moment in sorted(agenda):
        proceed(moment, grad)

    patch_grad = dot_tn(patch_rows, grad.astype(BF)).astype(BF)
    patch_grad = patch_grad.reshape(dp, teach, rows_own, D)
    patch_mine = lax.dynamic_index_in_dim(patch_grad, here_teach, 1, False)
    patch_sent = lax.dynamic_index_in_dim(patch_grad, 1 - here_teach, 1, False)
    patch_grad = add_low(patch_mine, swap(patch_sent, "teach", 1)).reshape(dp * rows_own, D)
    patch_grad = lax.psum_scatter(patch_grad, "dp", scatter_dimension=0, tiled=True)
    patch_grad = outward(sum_over(patch_grad.astype(F32), "mp"))

    source_grads = lax.dot_general(
        sources, grad, (((0,), (0,)), ((), ())), precision=HIGH, preferred_element_type=F32
    )
    vector_grads = outward(
        jnp.concatenate(gain_list + [final_vgrad[:2], source_grads], axis=0)
    )
    bias_blocks = jnp.concatenate(
        bias_list + [head_bgrad[:, 0, :cl], head_bgrad[:, 0, wc : wc + cl]], axis=1
    )[ranks]
    bias_size = bias_blocks.shape[1]
    flat = jnp.concatenate([vector_grads.reshape(-1), bias_blocks.reshape(-1)])
    flat = jnp.pad(flat, (0, -flat.size % 1024)).reshape(-1, 128)
    flat = sum_all(flat).reshape(-1)
    vector_grads = flat[: vector_params.size].reshape(vector_params.shape)
    bias_grads = lax.dynamic_slice_in_dim(
        flat, vector_params.size + here_mp * bias_size, bias_size, 0
    )

    attn_list = [unit.result() for unit in attn_out]
    mlp_list = [unit.result() for unit in mlp_out]
    head_grads = head_out.result()
    attn_grads = jnp.stack(
        [
            jnp.stack([attn_list[layer][:, part * wl : (part + 1) * wl] for part in range(4)])
            for layer in range(L)
        ]
    )
    mlp_grads = jnp.stack(
        [jnp.stack([mlp_list[layer][:, :fl], mlp_list[layer][:, fl:]]) for layer in range(L)]
    )
    head_grads = jnp.stack([head_grads[:, :cl], head_grads[:, wc : wc + cl]])

    step_power = step_count[0].astype(F32)
    correct_first = 1.0 - jnp.power(BETA, step_power)
    correct_second = 1.0 - jnp.power(BETA, step_power)
    weights = (patch_weight, attn_weight, mlp_weight, head_weight, vector_params, split_biases)
    gradients = (patch_grad, attn_grads, mlp_grads, head_grads, vector_grads, bias_grads)
    firsts = (patch_first, attn_first, mlp_first, head_first, vector_first, bias_first)
    seconds = (patch_second, attn_second, mlp_second, head_second, vector_second, bias_second)
    decay_pieces = expand_params(split_params(decay_mask.astype(F32)))
    results = [
        adam_direction(gradients[slot], firsts[slot], seconds[slot], correct_first, correct_second)
        for slot in range(6)
    ]
    directions = [
        results[slot][2] + DECAY * decay_pieces[slot] * weights[slot] for slot in range(6)
    ]
    totals = sum_all(
        jnp.concatenate(
            [
                squares_of(weights, mp_first, data_first),
                squares_of(directions, mp_first, data_first),
                loss_part[0, :1],
            ]
        )
    )
    npar = (totals.size - 1) // 2
    weights_sq, direction_sq, loss_value = totals[:npar], totals[npar : 2 * npar], totals[2 * npar]
    weight_norm = jnp.sqrt(weights_sq)
    update_norm = jnp.sqrt(direction_sq)
    trust_ratio = weight_norm / update_norm
    rates = BASE_RATE * jnp.power(LAYER_DECAY, 2.0 - layer_ids.astype(F32)) * trust_ratio
    rate_pieces = expand_params(split_params(rates))
    updated = [weights[slot] - rate_pieces[slot] * directions[slot] for slot in range(6)]
    norm_table = jnp.stack([weight_norm, update_norm])
    return (
        *updated,
        *[results[slot][0] for slot in range(6)],
        *[results[slot][1] for slot in range(6)],
        norm_table,
        trust_ratio,
        loss_value,
    )


def solution(mesh):
    rows = ("dp", "teach")
    moments = (
        P(rows, None),
        P(None, None, rows, "mp"),
        P(None, None, rows, "mp"),
        P(None, rows, "mp"),
        P(),
        P("mp"),
    )
    placed = (
        P(rows, None, None),
        P(rows, None),
        P(rows, None),
        P(rows),
        P(rows),
        P(),
        P(None, "mp"),
        *moments,
        *moments,
        *moments,
        P(),
        P(),
        P(),
    )
    return jax.shard_map(
        per_device,
        mesh=mesh,
        in_specs=placed,
        out_specs=(*moments, *moments, *moments, P(), P(), P()),
        check_vma=False,
    )
```

```python
import functools

import jax
import jax.numpy as jnp
from jax import lax
from jax.experimental import pallas as pl
from jax.experimental.pallas import tpu as pltpu
from jax.sharding import PartitionSpec as P

D = 768
HD = 64
G = 24
PMAX = 280
L = 2
RP = 288
TOK = 280
HR = 16

EPS_NORM = 1e-06
EPS_LAMB = 1e-06
BETA = 0.5
DECAY = 0.05
BASE_RATE = 0.4
LAYER_DECAY = 0.8
SCALE = 0.125
MASKED = -1e30
HIGH = lax.Precision.HIGHEST
ROOT_HALF = 0.7071067811865476
DENSITY = 0.3989422804014327
BF = jnp.bfloat16
F32 = jnp.float32
ALL = ("dp", "mp", "teach")
VMEM_LIMIT = 56 * 1024 * 1024
FLOP_PER_US = 1_150_000_000
BRIEF = 2
FAR = 3
PARTS = ((3, 1), (2, 0))


def dot_nn(left, right):
    return lax.dot_general(
        left, right, (((1,), (0,)), ((), ())), preferred_element_type=F32
    )


def dot_nt(left, right):
    return lax.dot_general(
        left, right, (((1,), (1,)), ((), ())), preferred_element_type=F32
    )


def dot_tn(left, right):
    return lax.dot_general(
        left, right, (((0,), (0,)), ((), ())), preferred_element_type=F32
    )


def gelu_erf(values):
    return 0.5 * values * (1.0 + lax.erf(values * ROOT_HALF))


def norm_stats(values):
    centre = values - jnp.mean(values, axis=-1, keepdims=True)
    scaled = lax.rsqrt(jnp.mean(centre * centre, axis=-1, keepdims=True) + EPS_NORM)
    return centre * scaled, scaled


def norm_back(grad_out, normed, scaled, gain_row):
    grad_normed = grad_out * gain_row
    inner_sum = jnp.mean(grad_normed, axis=-1, keepdims=True)
    cross_term = jnp.mean(grad_normed * normed, axis=-1, keepdims=True)
    return scaled * (grad_normed - inner_sum - normed * cross_term)


def row_sum(values):
    return jnp.sum(values, axis=0, keepdims=True)


def weight_copies(place_ref, steps, own, other, buf, sems):
    half = own[0].shape[0]
    here = place_ref[0]
    slots, sem = [], 0
    for slot, step in enumerate(steps):
        pieces = (FAR, FAR + 1) if step == FAR else (step,)
        copies = []
        for piece in pieces:
            size = half // len(pieces)
            for source, core in ((own[piece], here), (other[piece], 1 - here)):
                at = pl.multiple_of(core * half + (piece - pieces[0]) * size, 64)
                copies.append(
                    pltpu.make_async_copy(source, buf.at[slot, pl.ds(at, size)], sems.at[sem])
                )
                sem += 1
        slots.append(copies)
    return slots


def start_all(slots):
    for copies in slots:
        for copy in copies:
            copy.start()


def wait_slot(slots, now):
    for slot, copies in enumerate(slots):

        @pl.when(now == slot)
        def _():
            for copy in copies:
                copy.wait()


def split_out(half, place_ref, grad_buf, mine_ref, other_ref, slot):
    mine = pl.multiple_of(place_ref[0] * half, 128)
    theirs = pl.multiple_of((1 - place_ref[0]) * half, 128)
    mine_ref[slot] = grad_buf[pl.ds(mine, half), :]
    other_ref[slot] = grad_buf[pl.ds(theirs, half), :]


def attn_forward_kernel(
    mp,
    ni,
    wl,
    place_ref,
    resid_ref,
    vec_ref,
    bias_ref,
    live_ref,
    own,
    other,
    first_ref,
    qkv_ref,
    att_ref,
    lse_ref,
    mid_ref,
    buf,
    sems,
):
    now = pl.program_id(0)
    slots = weight_copies(place_ref, range(mp), own, other, buf, sems)

    @pl.when(now == 0)
    def _():
        start_all(slots)
        resid = resid_ref[...]
        normed, _ = norm_stats(resid)
        first_ref[...] = (normed * vec_ref[0:1] + vec_ref[1:2]).astype(BF)
        mid_ref[...] = resid + vec_ref[4:5]

    wait_slot(slots, now)
    qkv = dot_nn(first_ref[...], buf[now, :, : 3 * wl]) + bias_ref[0]
    qkv_ref[0] = qkv.astype(BF)
    for image in range(ni):
        rows = slice(image * RP, (image + 1) * RP)
        live = live_ref[image] > 0.0
        for head in range(wl // HD):
            at = head * HD
            queries = qkv_ref[0, rows, at : at + HD]
            keys = qkv_ref[0, rows, wl + at : wl + at + HD]
            vals = qkv_ref[0, rows, 2 * wl + at : 2 * wl + at + HD]
            scores = jnp.where(live, dot_nt(queries, keys) * SCALE, MASKED)
            peak = jnp.max(scores, axis=-1, keepdims=True)
            expo = jnp.exp(scores - peak)
            total = jnp.sum(expo, axis=-1, keepdims=True)
            soft = (expo * (1.0 / total)).astype(BF)
            att_ref[0, rows, at : at + HD] = dot_nn(soft, vals).astype(BF)
            lse_ref[0, rows, head : head + 1] = peak + jnp.log(total)
    mid_ref[...] += dot_nt(att_ref[0], buf[now, :, 3 * wl :])


def mlp_forward_kernel(
    mp,
    chunk,
    place_ref,
    mid_ref,
    vec_ref,
    bias_ref,
    own,
    other,
    second_ref,
    hidden_ref,
    slope_ref,
    out_ref,
    buf,
    sems,
):
    now = pl.program_id(0)
    fl = hidden_ref.shape[2]
    slots = weight_copies(place_ref, range(mp), own, other, buf, sems)

    @pl.when(now == 0)
    def _():
        start_all(slots)
        middle = mid_ref[...]
        normed, _ = norm_stats(middle)
        second_ref[...] = (normed * vec_ref[2:3] + vec_ref[3:4]).astype(BF)
        out_ref[...] = middle + vec_ref[5:6]

    wait_slot(slots, now)
    for start in range(0, mid_ref.shape[0], chunk):
        rows = slice(start, start + chunk)
        upward = dot_nn(second_ref[rows, :], buf[now, :, :fl]) + bias_ref[0]
        share = 0.5 + 0.5 * lax.erf(upward * ROOT_HALF)
        hidden = (upward * share).astype(BF)
        hidden_ref[0, rows, :] = hidden
        slope_ref[0, rows, :] = share + upward * (DENSITY * jnp.exp(-0.5 * upward * upward))
        out_ref[rows, :] += dot_nt(hidden, buf[now, :, fl:])


def head_kernel(
    mp,
    ni,
    wc,
    place_ref,
    resid_ref,
    vec_ref,
    bias_ref,
    ids_ref,
    labels_ref,
    mix_ref,
    scale_ref,
    weight_ref,
    pooled_ref,
    teacher_ref,
    own,
    other,
    mine_ref,
    other_ref,
    hbias_ref,
    grad_ref,
    vgrad_ref,
    loss_ref,
    buf,
    cls_buf,
    dist_buf,
    gw_buf,
    sems,
):
    half = mine_ref.shape[1]
    slots = weight_copies(place_ref, range(mp), own, other, buf, sems)
    start_all(slots)
    cls_buf[...] = jnp.zeros_like(cls_buf)
    dist_buf[...] = jnp.zeros_like(dist_buf)
    for image in range(ni):
        at = image * RP + TOK
        cls_buf[image : image + 1, :] = resid_ref[at : at + 1, :]
        dist_buf[image : image + 1, :] = resid_ref[at + 1 : at + 2, :]
    grad_ref[...] = jnp.zeros_like(grad_ref)
    normed_c, scaled_c = norm_stats(cls_buf[...])
    normed_d, scaled_d = norm_stats(dist_buf[...])
    gain, shift = vec_ref[0:1], vec_ref[1:2]
    final_c = (normed_c * gain + shift).astype(BF)
    final_d = (normed_d * gain + shift).astype(BF)
    for copies in slots:
        for copy in copies:
            copy.wait()
    cls, dist, teach, goal = [], [], [], []
    mix = mix_ref[:, 0:1]
    for block in range(mp):
        ids = ids_ref[block]
        valid = ids >= 0
        both = bias_ref[block]
        cls.append(
            jnp.where(valid, dot_nn(final_c, buf[block, :, :wc]) + both[:, :wc], MASKED)
        )
        dist.append(
            jnp.where(valid, dot_nn(final_d, buf[block, :, wc:]) + both[:, wc:], MASKED)
        )
        teach.append(jnp.where(valid, dot_nn(pooled_ref[...], teacher_ref[block]), MASKED))
        first = (labels_ref[:, 0:1] == ids).astype(F32)
        second = (labels_ref[:, 1:2] == ids).astype(F32)
        goal.append(mix * first + (1.0 - mix) * second)

    def log_total(parts):
        peak = functools.reduce(
            jnp.maximum, [jnp.max(part, axis=-1, keepdims=True) for part in parts]
        )
        total = sum(jnp.sum(jnp.exp(part - peak), axis=-1, keepdims=True) for part in parts)
        return peak + jnp.log(total)

    log_c, log_d, log_t = log_total(cls), log_total(dist), log_total(teach)
    prob = [jnp.exp(part - log_t) for part in teach]
    dot_c = sum(jnp.sum(g * c, axis=-1, keepdims=True) for g, c in zip(goal, cls))
    dot_d = sum(jnp.sum(p * d, axis=-1, keepdims=True) for p, d in zip(prob, dist))
    loss_rows = 0.5 * (log_c - dot_c) + 0.5 * (log_d - dot_d)
    loss_ref[...] = jnp.broadcast_to(row_sum(weight_ref[:, 0:1] * loss_rows), loss_ref.shape)
    scale = scale_ref[:, 0:1]
    gfin_c = jnp.zeros(cls_buf.shape, F32)
    gfin_d = jnp.zeros(dist_buf.shape, F32)
    for block in range(mp):
        grad_c = scale * (jnp.exp(cls[block] - log_c) - goal[block])
        grad_d = scale * (jnp.exp(dist[block] - log_d) - prob[block])
        hbias_ref[block, :, :wc] = row_sum(grad_c)
        hbias_ref[block, :, wc:] = row_sum(grad_d)
        low_c, low_d = grad_c.astype(BF), grad_d.astype(BF)
        gw_buf[:, :wc] = dot_tn(final_c, low_c).astype(BF)
        gw_buf[:, wc:] = dot_tn(final_d, low_d).astype(BF)
        split_out(half, place_ref, gw_buf, mine_ref, other_ref, block)
        gfin_c += dot_nt(low_c, buf[block, :, :wc])
        gfin_d += dot_nt(low_d, buf[block, :, wc:])
    vgrad_ref[...] = jnp.zeros_like(vgrad_ref)
    vgrad_ref[0:1, :] = row_sum(gfin_c * normed_c) + row_sum(gfin_d * normed_d)
    vgrad_ref[1:2, :] = row_sum(gfin_c) + row_sum(gfin_d)
    cls_buf[...] = norm_back(gfin_c, normed_c, scaled_c, gain)
    dist_buf[...] = norm_back(gfin_d, normed_d, scaled_d, gain)
    for image in range(ni):
        at = image * RP + TOK
        grad_ref[at : at + 1, :] = cls_buf[image : image + 1, :]
        grad_ref[at + 1 : at + 2, :] = dist_buf[image : image + 1, :]


def mlp_backward_kernel(
    steps,
    last,
    place_ref,
    grad_ref,
    mid_ref,
    vec_ref,
    second_ref,
    hidden_ref,
    slope_ref,
    own,
    other,
    *rest,
):
    if steps[0] != FAR:
        part_ref, *rest = rest
    (
        gmid_ref,
        mine_ref,
        other_ref,
        gbias_ref,
        vgrad_ref,
        buf,
        branch_buf,
        branch_t,
        second_t,
        gw_buf,
        sems,
    ) = rest
    now = pl.program_id(0)
    fl = hidden_ref.shape[2]
    half = mine_ref.shape[1]
    slots = weight_copies(place_ref, steps, own, other, buf, sems)

    @pl.when(now == 0)
    def _():
        start_all(slots)
        branch_buf[...] = grad_ref[...].astype(BF)
        branch_t[...] = branch_buf[...].T
        second_t[...] = second_ref[...].T
        if steps[0] == FAR:
            gmid_ref[...] = jnp.zeros_like(gmid_ref)
        else:
            gmid_ref[...] = part_ref[...]
        vgrad_ref[...] = jnp.zeros_like(vgrad_ref)

    wait_slot(slots, now)
    gup = (dot_nn(branch_buf[...], buf[now, :, fl:]) * slope_ref[0]).astype(BF)
    gbias_ref[0] = row_sum(gup.astype(F32))
    gmid_ref[...] += dot_nt(gup, buf[now, :, :fl])
    gw_buf[:, :fl] = dot_nn(second_t[...], gup).astype(BF)
    gw_buf[:, fl:] = dot_nn(branch_t[...], hidden_ref[0]).astype(BF)
    split_out(half, place_ref, gw_buf, mine_ref, other_ref, 0)
    if last:

        @pl.when(now == len(steps) - 1)
        def _():
            normed, scaled = norm_stats(mid_ref[...])
            gsec = gmid_ref[...]
            grad = grad_ref[...]
            vgrad_ref[2:3, :] = row_sum(gsec * normed)
            vgrad_ref[3:4, :] = row_sum(gsec)
            vgrad_ref[5:6, :] = row_sum(grad)
            gmid = norm_back(gsec, normed, scaled, vec_ref[2:3]) + grad
            vgrad_ref[4:5, :] = row_sum(gmid)
            gmid_ref[...] = gmid


def attn_backward_kernel(
    ni,
    wl,
    steps,
    last,
    place_ref,
    gmid_ref,
    resid_ref,
    vec_ref,
    live_ref,
    first_ref,
    qkv_ref,
    att_ref,
    lse_ref,
    own,
    other,
    *rest,
):
    if steps[0] != FAR:
        part_ref, *rest = rest
    (
        gres_ref,
        mine_ref,
        other_ref,
        gbias_ref,
        vgrad_ref,
        buf,
        mixed_buf,
        mixed_t,
        first_t,
        gatt_buf,
        gqkv_buf,
        gw_buf,
        sems,
    ) = rest
    now = pl.program_id(0)
    half = mine_ref.shape[1]
    slots = weight_copies(place_ref, steps, own, other, buf, sems)

    @pl.when(now == 0)
    def _():
        start_all(slots)
        mixed_buf[...] = gmid_ref[...].astype(BF)
        mixed_t[...] = mixed_buf[...].T
        first_t[...] = first_ref[...].T
        if steps[0] == FAR:
            gres_ref[...] = jnp.zeros_like(gres_ref)
        else:
            gres_ref[...] = part_ref[...]
        vgrad_ref[...] = jnp.zeros_like(vgrad_ref)

    wait_slot(slots, now)
    gatt_buf[...] = dot_nn(mixed_buf[...], buf[now, :, 3 * wl :]).astype(BF)
    for image in range(ni):
        rows = slice(image * RP, (image + 1) * RP)
        live = live_ref[image] > 0.0
        for head in range(wl // HD):
            at = head * HD
            queries = qkv_ref[0, rows, at : at + HD]
            keys = qkv_ref[0, rows, wl + at : wl + at + HD]
            vals = qkv_ref[0, rows, 2 * wl + at : 2 * wl + at + HD]
            gatt = gatt_buf[rows, at : at + HD]
            scores = jnp.where(live, dot_nt(queries, keys) * SCALE, MASKED)
            soft = jnp.exp(scores - lse_ref[0, rows, head : head + 1])
            gsoft = dot_nt(gatt, vals)
            inner = jnp.sum(soft * gsoft, axis=-1, keepdims=True)
            gscore = (soft * (gsoft - inner)).astype(BF)
            gqkv_buf[rows, at : at + HD] = (dot_nn(gscore, keys) * SCALE).astype(BF)
            gqkv_buf[rows, wl + at : wl + at + HD] = (dot_tn(gscore, queries) * SCALE).astype(BF)
            gqkv_buf[rows, 2 * wl + at : 2 * wl + at + HD] = dot_tn(soft.astype(BF), gatt).astype(BF)
    gqkv = gqkv_buf[...]
    gbias_ref[0] = row_sum(gqkv.astype(F32))
    gres_ref[...] += dot_nt(gqkv, buf[now, :, : 3 * wl])
    gw_buf[:, : 3 * wl] = dot_nn(first_t[...], gqkv).astype(BF)
    gw_buf[:, 3 * wl :] = dot_nn(mixed_t[...], att_ref[0]).astype(BF)
    split_out(half, place_ref, gw_buf, mine_ref, other_ref, 0)
    if last:

        @pl.when(now == len(steps) - 1)
        def _():
            normed, scaled = norm_stats(resid_ref[...])
            gfirst = gres_ref[...]
            vgrad_ref[0:1, :] = row_sum(gfirst * normed)
            vgrad_ref[1:2, :] = row_sum(gfirst)
            gres_ref[...] = norm_back(gfirst, normed, scaled, vec_ref[0:1]) + gmid_ref[...]


def call(kernel, outs, scratch, ins, steps=None, after=()):
    def whole(array):
        return pl.BlockSpec(array.shape, lambda i: (0,) * array.ndim)

    def each(array, base=0, stride=1):
        return pl.BlockSpec(
            (1, *array.shape[1:]), lambda i: (base + stride * i, *(0,) * (array.ndim - 1))
        )

    specs, arrays, sizes = [], [], []
    for item in [*ins, ("group", list(after))]:
        kind, item = item if isinstance(item, tuple) else ("vmem", item)
        group = item if kind == "group" else [item]
        sizes.append(len(group) if kind == "group" else None)
        if kind in ("group", "smem"):
            space = pl.ANY if kind == "group" else pltpu.SMEM
            specs += [pl.BlockSpec(memory_space=space)] * len(group)
        elif kind == "each":
            specs.append(each(item, steps[0], steps[1] - steps[0]))
        elif steps:
            specs.append(whole(item))
        else:
            specs.append(pl.BlockSpec(memory_space=pltpu.VMEM))
        arrays += group

    def grouped(*refs):
        given, at = [], 0
        for size in sizes:
            given.append(refs[at] if size is None else refs[at : at + size])
            at += 1 if size is None else size
        return kernel(*given[:-1], *refs[at:])

    out_shape = [jax.ShapeDtypeStruct(*out[:2]) for out in outs]
    if steps:
        out_specs = [
            each(shape) if len(out) > 2 else whole(shape) for out, shape in zip(outs, out_shape)
        ]
        grid = {"grid": (len(steps),)}
    else:
        out_specs = [pl.BlockSpec(memory_space=pltpu.VMEM)] * len(out_shape)
        grid = {}
    moved = sum(a.size * a.dtype.itemsize for a in arrays)
    moved += sum(s.size * s.dtype.itemsize for s in out_shape)
    return pl.pallas_call(
        grouped,
        out_shape=out_shape,
        in_specs=specs,
        out_specs=out_specs,
        **grid,
        scratch_shapes=scratch,
        compiler_params=pltpu.CompilerParams(vmem_limit_bytes=VMEM_LIMIT),
        cost_estimate=pl.CostEstimate(
            flops=BRIEF * FLOP_PER_US, bytes_accessed=moved, transcendentals=0
        ),
    )(*arrays)


def tie(values, *behind):
    if not behind:
        return values
    return lax.optimization_barrier((values, behind))[0]


def swap(values, axis, distance):
    size = lax.axis_size(axis)
    return lax.ppermute(values, axis, [(rank, rank ^ distance) for rank in range(size)])


class Gather:
    def __init__(self, near):
        self.near = near

    def square(self, *behind):
        near = tie(self.near, *behind)
        self.own = [near, swap(near, "mp", 1), swap(near, "mp", 2)]
        self.other = [swap(near, "teach", 1)]

    def corner(self, *behind):
        near, by_one, by_two = self.own
        cut = near.shape[0] // 2
        by_one, by_two = tie((by_one, by_two), *behind)
        self.own = [near, by_one, by_two, swap(by_two[:cut], "mp", 1), swap(by_one[cut:], "mp", 2)]
        self.other += [swap(by_one, "teach", 1), swap(by_two, "teach", 1)]

    def cores(self, *behind):
        far = tie(tuple(self.own[3:]), *behind)
        self.own[3:] = far
        self.other += [swap(piece, "teach", 1) for piece in far]

    def refs(self):
        return [("group", self.own), ("group", self.other)]


def add_low(left, right):
    return (left.astype(F32) + right.astype(F32)).astype(BF)


def sum_over(values, axis):
    distance = 1
    while distance < lax.axis_size(axis):
        values = values + swap(values, axis, distance)
        distance *= 2
    return values


def sum_all(values):
    for axis in ("teach", "mp", "dp"):
        values = sum_over(values, axis)
    return values


def sum_and_gather(values, everywhere, cores, square):
    for axis in ("dp", "teach", "mp"):
        distance = 1
        while distance < lax.axis_size(axis):
            parts = [everywhere, square] if axis == "mp" else [everywhere, cores]
            sent = jnp.concatenate([values] + [part.reshape(-1) for part in parts])
            got = swap(sent, axis, distance)
            first = (lax.axis_index(axis) // distance) % 2 == 0
            at = values.size
            values = values + got[:at]
            doubled = []
            for part in parts:
                new = got[at : at + part.size].reshape(part.shape)
                at += part.size
                doubled.append(
                    jnp.concatenate([jnp.where(first, part, new), jnp.where(first, new, part)])
                )
            if axis == "mp":
                everywhere, square = doubled
            else:
                everywhere, cores = doubled
            distance *= 2
    return values, everywhere, cores, square


def gather_mp(values):
    size = lax.axis_size("mp")
    return jnp.stack([values] + [swap(values, "mp", step) for step in range(1, size)])


class Scatter:
    def __init__(self):
        self.waiting = []
        self.block = {}
        self.extra = None
        self.sections = []
        self.pieces = None

    def cores(self, steps, mine, other):
        self.waiting.append((steps, mine, swap(other, "teach", 1)))

    def attach(self, *sections):
        self.sections = [mine.shape[1] for mine, _ in sections]
        other = jnp.concatenate([other for _, other in sections], axis=1)
        self.extra = (
            jnp.concatenate([mine for mine, _ in sections], axis=1),
            swap(other, "teach", 1),
        )

    def added(self, *behind):
        for steps, mine, got in self.waiting:
            got = tie(got, *behind)
            for slot, step in enumerate(steps):
                block = add_low(mine[slot], got[slot])
                self.cuts = [block.shape[0], *self.sections]
                if self.extra:
                    more = add_low(self.extra[0][step], self.extra[1][step])
                    block = jnp.concatenate([block, more])
                self.block[step] = block
        self.waiting = []

    def corner(self, *behind):
        self.added(*behind)
        self.cut = cut = -(-self.block[FAR].shape[0] // 32) * 16
        sent = [self.block[FAR][:cut], self.block[FAR][cut:]]
        self.by_one = swap(sent[0], "mp", 1)
        self.by_two = swap(sent[1], "mp", 2)
        return sent

    def square(self, *behind):
        self.added(*behind)
        one, two = self.block[1], self.block[2]
        cut = self.cut
        by_one, by_two = tie((self.by_one, self.by_two), *behind)
        sent = [
            jnp.concatenate([one[:cut], add_low(one[cut:], by_two)]),
            jnp.concatenate([add_low(two[:cut], by_one), two[cut:]]),
        ]
        self.by_one = swap(sent[0], "mp", 1)
        self.by_two = swap(sent[1], "mp", 2)
        return sent

    def summed(self, *behind):
        by_one, by_two = tie((self.by_one, self.by_two), *behind)
        total = self.block[0].astype(F32) + (by_one.astype(F32) + by_two.astype(F32))
        dp = lax.axis_size("dp")
        width = total.shape[1]
        parts, at = [], 0
        for cut in self.cuts:
            parts.append(total[at : at + cut].reshape(dp, -1, width))
            at += cut
        return jnp.concatenate(parts, axis=1).astype(BF).reshape(total.shape)

    def rows(self, *behind):
        total = self.summed(*behind)
        self.pieces = lax.psum_scatter(total, "dp", scatter_dimension=0, tiled=True)
        return [total]

    def result(self):
        return self.pieces.astype(F32)


def adam_direction(gradient, first_moment, second_moment, correct_first, correct_second):
    new_first = BETA * first_moment + (1.0 - BETA) * gradient
    new_second = BETA * second_moment + (1.0 - BETA) * gradient * gradient
    return (
        new_first,
        new_second,
        new_first / correct_first / (jnp.sqrt(new_second / correct_second) + EPS_LAMB),
    )


def split_params(values):
    layered = values[1 : 1 + 6 * L].reshape(L, 6)
    return (
        values[0],
        layered[:, :4],
        layered[:, 4:],
        values[1 + 6 * L : 3 + 6 * L],
        values[3 + 6 * L],
        values[4 + 6 * L],
    )


def expand_params(pieces):
    return (
        pieces[0],
        pieces[1][:, :, None, None],
        pieces[2][:, :, None, None],
        pieces[3][:, None, None],
        pieces[4],
        pieces[5],
    )


def order_params(pieces):
    layered = jnp.concatenate([pieces[1], pieces[2]], axis=1).reshape(-1)
    return jnp.concatenate([pieces[0][None], layered, pieces[3], pieces[4][None], pieces[5][None]])


def squares_of(pieces, mp_first, data_first):
    return order_params(
        (
            jnp.sum(pieces[0] * pieces[0]) * mp_first,
            jnp.sum(pieces[1] * pieces[1], axis=(2, 3)),
            jnp.sum(pieces[2] * pieces[2], axis=(2, 3)),
            jnp.sum(pieces[3] * pieces[3], axis=(1, 2)),
            jnp.sum(pieces[4] * pieces[4]) * mp_first * data_first,
            jnp.sum(pieces[5] * pieces[5]) * data_first,
        )
    )


def per_device(
    patches,
    grid_sizes,
    label_ids,
    label_mix,
    image_weight,
    teacher_stem,
    teacher_head,
    patch_weight,
    attn_weight,
    mlp_weight,
    head_weight,
    vector_params,
    split_biases,
    patch_first,
    attn_first,
    mlp_first,
    head_first,
    vector_first,
    bias_first,
    patch_second,
    attn_second,
    mlp_second,
    head_second,
    vector_second,
    bias_second,
    decay_mask,
    layer_ids,
    step_count,
):
    dp, mp, teach = lax.axis_size("dp"), lax.axis_size("mp"), lax.axis_size("teach")
    here_mp = lax.axis_index("mp")
    here_teach = lax.axis_index("teach")
    place = ("smem", here_teach.astype(jnp.int32).reshape(1))
    mp_first = (here_mp == 0).astype(F32)
    data_first = (lax.axis_index(("dp", "teach")) == 0).astype(F32)
    rows_own = patch_weight.shape[0]
    half = dp * rows_own
    wl = attn_weight.shape[3]
    fl = mlp_weight.shape[3]
    cl = head_weight.shape[2]
    wc = -(-cl // 128) * 128
    head_row = 6 * L

    def inward(values):
        lead = values.shape[:-1]
        cut = values.reshape(*lead, dp, teach, rows_own)
        return jnp.swapaxes(cut, -3, -2).reshape(*lead, D)

    def outward(values):
        lead = values.shape[:-1]
        cut = values.reshape(*lead, teach, dp, rows_own)
        return jnp.swapaxes(cut, -3, -2).reshape(*lead, D)

    ni = patches.shape[0] // mp

    def take(array):
        return lax.dynamic_slice_in_dim(array, here_mp * ni, ni, 0)

    patches, grid_sizes, label_ids = take(patches), take(grid_sizes), take(label_ids)
    label_mix, image_weight = take(label_mix), take(image_weight)
    weight_sum = sum_all(jnp.sum(image_weight).reshape(1))[0]

    patch_low = inward(patch_weight).astype(BF)
    attn_low = [
        jnp.concatenate([attn_weight[layer, part] for part in range(4)], axis=1).astype(BF)
        for layer in range(L)
    ]
    mlp_low = [
        jnp.concatenate([mlp_weight[layer, 0], mlp_weight[layer, 1]], axis=1).astype(BF)
        for layer in range(L)
    ]
    head_pad = jnp.pad(head_weight, ((0, 0), (0, 0), (0, wc - cl)))
    head_low = jnp.concatenate([head_pad[0], head_pad[1]], axis=1).astype(BF)

    def gather_dp(*pieces):
        wide_piece = lax.all_gather(jnp.concatenate(pieces, axis=1), "dp", axis=0, tiled=True)
        cuts, at = [], 0
        for piece in pieces:
            cuts.append(wide_piece[:, at : at + piece.shape[1]])
            at += piece.shape[1]
        return cuts

    near = gather_dp(patch_low, attn_low[0]) + gather_dp(mlp_low[0])
    rest = [piece for layer in range(1, L) for piece in (attn_low[layer], mlp_low[layer])]
    near += gather_dp(*rest, head_low)
    teacher_all = gather_mp(jnp.pad(teacher_head, ((0, 0), (0, wc - cl))))
    bias_all = gather_mp(split_biases)
    near[0], near[1] = tie((near[0], near[1]), weight_sum, teacher_all, bias_all)
    patch_own = near[0]
    patch_other = swap(patch_own, "teach", 1)
    units = [Gather(piece) for piece in near[1:]]
    attn_units, mlp_units, head_unit = units[0:-1:2], units[1:-1:2], units[-1]

    vec_in = inward(vector_params)
    layer_vecs = [
        jnp.pad(vec_in[6 * layer : 6 * layer + 6], ((0, 2), (0, 0))) for layer in range(L)
    ]
    final_vec = jnp.pad(vec_in[head_row : head_row + 2], ((0, 6), (0, 0)))
    attn_bias, up_bias = [], []
    span = 2 * wl + fl
    for layer in range(L):
        part = bias_all[:, layer * span : (layer + 1) * span]
        zero = jnp.zeros((mp, wl), F32)
        attn_bias.append(
            jnp.concatenate([part[:, :wl], zero, part[:, wl : 2 * wl]], axis=1)[:, None]
        )
        up_bias.append(part[:, None, 2 * wl :])
    pad_class = ((0, 0), (0, wc - cl))
    head_bias = jnp.concatenate(
        [
            jnp.pad(bias_all[:, L * span : L * span + cl], pad_class),
            jnp.pad(bias_all[:, L * span + cl : L * span + 2 * cl], pad_class),
        ],
        axis=1,
    )[:, None]

    grid_rows, grid_cols = grid_sizes[:, 0:1], grid_sizes[:, 1:2]
    slot_ids = jnp.arange(PMAX, dtype=jnp.int32)[None, :]
    patch_live = slot_ids < grid_rows * grid_cols
    live_float = patch_live.astype(F32)
    live_rows = jnp.concatenate(
        [live_float, jnp.ones((ni, 2), F32), jnp.zeros((ni, RP - PMAX - 2), F32)], axis=1
    )[:, None, :]
    table = jnp.arange(G, dtype=jnp.int32)
    source_patch = jnp.concatenate(
        [
            jnp.ones((ni, PMAX, 1), F32),
            jnp.zeros((ni, PMAX, 2), F32),
            ((slot_ids // grid_cols)[..., None] == table).astype(F32),
            ((slot_ids % grid_cols)[..., None] == table).astype(F32),
        ],
        axis=2,
    )
    source_token = jnp.broadcast_to(jnp.eye(2, 3 + 2 * G, 1, dtype=F32), (ni, 2, 3 + 2 * G))
    sources = jnp.concatenate(
        [source_patch, source_token, jnp.zeros((ni, RP - PMAX - 2, 3 + 2 * G), F32)], axis=1
    ).reshape(ni * RP, 3 + 2 * G)

    stem_rows = gelu_erf(dot_nn(patches.reshape(ni * PMAX, -1), teacher_stem)).reshape(ni, PMAX, -1)
    pooled = (
        jnp.sum(stem_rows * live_float[..., None], axis=1)
        / jnp.sum(live_float, axis=1, keepdims=True)
    ).astype(BF)

    first_core = here_teach == 0
    patch_full = jnp.stack(
        [
            jnp.where(first_core, patch_own, patch_other).reshape(dp, rows_own, D),
            jnp.where(first_core, patch_other, patch_own).reshape(dp, rows_own, D),
        ],
        axis=1,
    ).reshape(D, D)
    patch_rows = jnp.pad(patches, ((0, 0), (0, RP - PMAX), (0, 0))).reshape(ni * RP, -1)
    residual = dot_nn(patch_rows, patch_full) + jnp.dot(
        sources, vec_in[head_row + 2 :], precision=HIGH
    )

    n = ni * RP
    parts = 2 * mp + 2
    saved = []
    def wide(values):
        return jnp.pad(values.reshape(ni, -1), ((0, HR - ni), (0, 0)))

    ranks = here_mp ^ jnp.arange(mp, dtype=jnp.int32)
    lanes = jnp.arange(wc, dtype=jnp.int32)
    class_ids = jnp.where(lanes[None] < cl, ranks[:, None] * cl + lanes[None], -1)[:, None]
    head_small = [
        class_ids,
        wide(label_ids),
        wide(label_mix),
        wide(0.5 * image_weight / weight_sum),
        wide(image_weight / weight_sum),
        wide(pooled),
    ]

    first_unit = units[0]
    first_unit.square()
    first_unit.corner(residual)
    units[1].square(*first_unit.own[3:])

    def arrive(at, done):
        here = units[at]
        ahead = units[at + 1 : at + 2] if at < len(units) - 3 else units[at + 1 :]
        if at == 0:
            here.cores()
            return [units[1].own[0], *head_small, head_bias, *attn_bias, *up_bias]
        if at < len(units) - 2:
            here.corner(done)
            for unit in ahead:
                unit.square(*here.own[3:], done)
            here.cores(*[unit.own[0] for unit in ahead])
            return [unit.own[0] for unit in ahead]
        if at == len(units) - 2:
            here.corner(done)
            units[-1].corner(done)
            here.cores()
            units[-1].cores()
        return []

    for layer in range(L):
        sending = arrive(2 * layer, residual)
        first, qkv, attended, lse, middle = call(
            functools.partial(attn_forward_kernel, mp, ni, wl),
            [
                ((n, D), BF),
                ((mp, n, 3 * wl), BF, "each"),
                ((mp, n, wl), BF, "each"),
                ((mp, n, wl // HD), F32, "each"),
                ((n, D), F32),
            ],
            [pltpu.VMEM((mp, D, 4 * wl), BF), pltpu.SemaphoreType.DMA((parts,))],
            [place, residual, layer_vecs[layer], ("each", attn_bias[layer]), live_rows]
            + attn_units[layer].refs(),
            range(mp),
            sending,
        )
        sending = arrive(2 * layer + 1, middle)
        second, hidden, slope, output = call(
            functools.partial(mlp_forward_kernel, mp, n // 4),
            [((n, D), BF), ((mp, n, fl), BF, "each"), ((mp, n, fl), F32, "each"), ((n, D), F32)],
            [pltpu.VMEM((mp, D, 2 * fl), BF), pltpu.SemaphoreType.DMA((parts,))],
            [place, middle, layer_vecs[layer], ("each", up_bias[layer])]
            + mlp_units[layer].refs(),
            range(mp),
            sending,
        )
        saved.append((residual, first, qkv, attended, lse, middle, second, hidden, slope))
        residual = output

    head_mine, head_other, head_bgrad, grad, final_vgrad, loss_part = call(
        functools.partial(head_kernel, mp, ni, wc),
        [
            ((mp, half, 2 * wc), BF),
            ((mp, half, 2 * wc), BF),
            ((mp, 1, 2 * wc), F32),
            ((n, D), F32),
            ((8, D), F32),
            ((8, 128), F32),
        ],
        [
            pltpu.VMEM((mp, D, 2 * wc), BF),
            pltpu.VMEM((HR, D), F32),
            pltpu.VMEM((HR, D), F32),
            pltpu.VMEM((D, 2 * wc), BF),
            pltpu.SemaphoreType.DMA((parts,)),
        ],
        [
            place,
            residual,
            final_vec,
            head_bias,
            *head_small,
            teacher_all,
            *head_unit.refs(),
        ],
    )
    head_out = Scatter()
    head_out.cores(range(mp), head_mine, head_other)
    mlp_out, attn_out = [Scatter() for _ in range(L)], [Scatter() for _ in range(L)]
    agenda = {0: [], 1: [(head_out, "corner")], 2: [(head_out, "square")], 3: [(head_out, "rows")]}
    slot = 0
    for layer in reversed(range(L)):
        plan = (
            (mlp_out[layer], "corner", 2),
            (mlp_out[layer], "square", 3),
            (mlp_out[layer], "rows", 5 if layer else 4),
            (attn_out[layer], "corner", 4),
            (attn_out[layer], "square", 5),
            (attn_out[layer], "rows", 6),
        )
        for unit, what, moment in plan:
            agenda.setdefault(slot + moment, []).append((unit, what))
        slot += 4
    final = slot

    def proceed(moment, done):
        sent = []
        for unit, what in agenda.pop(moment, []):
            sent += getattr(unit, what)(done)
        return sent

    sending = [head_other]
    gain_list, bias_list = [None] * L, [None] * L
    slot = 0
    for layer in reversed(range(L)):
        resid_in, first, qkv, attended, lse, middle, second, hidden, slope = saved[layer]
        part = []
        up_bgrad, qkv_bgrad = {}, {}
        for steps in PARTS:
            count = len(steps)
            gmid, mine, other, bgrad, mlp_vgrad = call(
                functools.partial(mlp_backward_kernel, steps, steps is PARTS[-1]),
                [
                    ((n, D), F32),
                    ((count, half, 2 * fl), BF, "each"),
                    ((count, half, 2 * fl), BF, "each"),
                    ((count, 1, fl), F32, "each"),
                    ((8, D), F32),
                ],
                [
                    pltpu.VMEM((count, D, 2 * fl), BF),
                    pltpu.VMEM((n, D), BF),
                    pltpu.VMEM((D, n), BF),
                    pltpu.VMEM((D, n), BF),
                    pltpu.VMEM((D, 2 * fl), BF),
                    pltpu.SemaphoreType.DMA((2 * count + 2,)),
                ],
                [place, grad, middle, layer_vecs[layer], second, ("each", hidden), ("each", slope)]
                + mlp_units[layer].refs()
                + part,
                steps,
                sending,
            )
            part = [gmid]
            up_bgrad.update({step: bgrad[at, 0] for at, step in enumerate(steps)})
            slot += 1
            mlp_out[layer].cores(steps, mine, other)
            sending = [other] + proceed(slot, gmid)
        part = []
        for steps in PARTS:
            count = len(steps)
            grad, mine, other, bgrad, attn_vgrad = call(
                functools.partial(attn_backward_kernel, ni, wl, steps, steps is PARTS[-1]),
                [
                    ((n, D), F32),
                    ((count, half, 4 * wl), BF, "each"),
                    ((count, half, 4 * wl), BF, "each"),
                    ((count, 1, 3 * wl), F32, "each"),
                    ((8, D), F32),
                ],
                [
                    pltpu.VMEM((count, D, 4 * wl), BF),
                    pltpu.VMEM((n, D), BF),
                    pltpu.VMEM((D, n), BF),
                    pltpu.VMEM((D, n), BF),
                    pltpu.VMEM((n, wl), BF),
                    pltpu.VMEM((n, 3 * wl), BF),
                    pltpu.VMEM((D, 4 * wl), BF),
                    pltpu.SemaphoreType.DMA((2 * count + 2,)),
                ],
                [place, gmid, resid_in, layer_vecs[layer], live_rows, first]
                + [("each", qkv), ("each", attended), ("each", lse)]
                + attn_units[layer].refs()
                + part,
                steps,
                sending,
            )
            part = [grad]
            qkv_bgrad.update({step: bgrad[at, 0] for at, step in enumerate(steps)})
            slot += 1
            attn_out[layer].cores(steps, mine, other)
            if slot < final:
                sending = [other] + proceed(slot, grad)
        gain_list[layer] = (attn_vgrad + mlp_vgrad)[:6]
        bias_list[layer] = jnp.stack(
            [
                jnp.concatenate(
                    [qkv_bgrad[step][:wl], qkv_bgrad[step][2 * wl :], up_bgrad[step]]
                )
                for step in range(mp)
            ]
        )
    quarter = rows_own // mp
    patch_grad = dot_tn(patch_rows, grad.astype(BF)).astype(BF)
    patch_grad = patch_grad.reshape(dp, teach, mp, quarter, D)

    def patch_half(core):
        kept = lax.dynamic_index_in_dim(patch_grad, core, 1, False)
        return kept.transpose(1, 0, 2, 3)[ranks].reshape(mp, dp * quarter, D)

    source_grads = lax.dot_general(
        sources, grad, (((0,), (0,)), ((), ())), precision=HIGH, preferred_element_type=F32
    )
    vector_grads = outward(
        jnp.concatenate(gain_list + [final_vgrad[:2], source_grads], axis=0)
    )
    bias_blocks = jnp.concatenate(
        bias_list + [head_bgrad[:, 0, :cl], head_bgrad[:, 0, wc : wc + cl]], axis=1
    )
    devices = dp * teach
    vector_piece = -(-vector_params.size // (mp * devices))
    bias_piece = -(-split_biases.size // devices)

    def padded(flat, size):
        return jnp.pad(flat, ((0, 0), (0, size - flat.shape[1])))

    more_rows = -(rows_own + quarter) % 16
    while more_rows * D < vector_piece + bias_piece:
        more_rows += 16
    vector_cut = padded(vector_grads.reshape(1, -1), vector_piece * mp * devices)
    small = jnp.concatenate(
        [
            vector_cut.reshape(mp, devices, vector_piece)[ranks],
            padded(bias_blocks, bias_piece * devices).reshape(mp, devices, bias_piece),
            jnp.zeros((mp, devices, more_rows * D - vector_piece - bias_piece), F32),
        ],
        axis=2,
    )
    small = small.astype(BF).reshape(mp, teach, dp * more_rows, D)

    def small_half(core):
        return lax.dynamic_index_in_dim(small, core, 1, False)

    attn_out[0].attach(
        (patch_half(here_teach), patch_half(1 - here_teach)),
        (small_half(here_teach), small_half(1 - here_teach)),
    )
    ahead = [grad]
    for moment in sorted(agenda):
        for unit, what in agenda[moment]:
            ahead += getattr(unit, what)(*ahead)
    first_rows = attn_out[0].result()
    patch_grad = outward(first_rows[rows_own : rows_own + quarter])
    small = first_rows[rows_own + quarter :].reshape(-1)
    vector_grads = small[:vector_piece]
    bias_grads = small[vector_piece : vector_piece + bias_piece]

    attn_list = [first_rows[:rows_own]] + [unit.result() for unit in attn_out[1:]]
    mlp_list = [unit.result() for unit in mlp_out]
    head_grads = head_out.result()
    attn_grads = jnp.stack(
        [
            jnp.stack([attn_list[layer][:, part * wl : (part + 1) * wl] for part in range(4)])
            for layer in range(L)
        ]
    )
    mlp_grads = jnp.stack(
        [jnp.stack([mlp_list[layer][:, :fl], mlp_list[layer][:, fl:]]) for layer in range(L)]
    )
    head_grads = jnp.stack([head_grads[:, :cl], head_grads[:, wc : wc + cl]])

    step_power = step_count[0].astype(F32)
    correct_first = 1.0 - jnp.power(BETA, step_power)
    correct_second = 1.0 - jnp.power(BETA, step_power)
    weights = (patch_weight, attn_weight, mlp_weight, head_weight, vector_params, split_biases)
    firsts = (patch_first, attn_first, mlp_first, head_first, vector_first, bias_first)
    seconds = (patch_second, attn_second, mlp_second, head_second, vector_second, bias_second)
    decay_pieces = expand_params(split_params(decay_mask.astype(F32)))

    def direct(gradient, first, second, weight, decay):
        new_first, new_second, direction = adam_direction(
            gradient, first, second, correct_first, correct_second
        )
        return new_first, new_second, direction + DECAY * decay * weight

    device = lax.axis_index(("teach", "dp"))

    def patch_cut(array):
        return lax.dynamic_slice_in_dim(array, here_mp * quarter, quarter, 0)

    def vector_part(array):
        flat = padded(array.reshape(1, -1), vector_piece * mp * devices)[0]
        at = (here_mp * devices + device) * vector_piece
        return lax.dynamic_slice_in_dim(flat, at, vector_piece, 0)

    def bias_part(array):
        flat = padded(array.reshape(1, -1), bias_piece * devices)[0]
        return lax.dynamic_slice_in_dim(flat, device * bias_piece, bias_piece, 0)

    pieces = (patch_grad, attn_grads, mlp_grads, head_grads, vector_grads, bias_grads)
    own_part = (patch_cut, None, None, None, vector_part, bias_part)
    results = []
    for slot, part in enumerate(own_part):
        others = (firsts[slot], seconds[slot], weights[slot])
        if part is not None:
            others = [part(array) for array in others]
        results.append(direct(pieces[slot], *others, decay_pieces[slot]))
    totals, vector_grads, bias_grads, patch_grad = sum_and_gather(
        jnp.concatenate(
            [
                squares_of(weights, mp_first, data_first),
                squares_of([result[2] for result in results], 1.0, 1.0),
                loss_part[0, :1],
            ]
        ),
        vector_grads,
        bias_grads,
        patch_grad,
    )
    gathered = {
        0: patch_grad,
        4: vector_grads[: vector_params.size].reshape(vector_params.shape),
        5: bias_grads[: split_biases.size],
    }
    for slot, gradient in gathered.items():
        results[slot] = direct(
            gradient, firsts[slot], seconds[slot], weights[slot], decay_pieces[slot]
        )
    directions = [result[2] for result in results]
    npar = (totals.size - 1) // 2
    weights_sq, direction_sq, loss_value = totals[:npar], totals[npar : 2 * npar], totals[2 * npar]
    weight_norm = jnp.sqrt(weights_sq)
    update_norm = jnp.sqrt(direction_sq)
    trust_ratio = weight_norm / update_norm
    rates = BASE_RATE * jnp.power(LAYER_DECAY, 2.0 - layer_ids.astype(F32)) * trust_ratio
    rate_pieces = expand_params(split_params(rates))
    updated = [weights[slot] - rate_pieces[slot] * directions[slot] for slot in range(6)]
    norm_table = jnp.stack([weight_norm, update_norm])
    return (
        *updated,
        *[results[slot][0] for slot in range(6)],
        *[results[slot][1] for slot in range(6)],
        norm_table,
        trust_ratio,
        loss_value,
    )


def solution(mesh):
    rows = ("dp", "teach")
    moments = (
        P(rows, None),
        P(None, None, rows, "mp"),
        P(None, None, rows, "mp"),
        P(None, rows, "mp"),
        P(),
        P("mp"),
    )
    placed = (
        P(rows, None, None),
        P(rows, None),
        P(rows, None),
        P(rows),
        P(rows),
        P(),
        P(None, "mp"),
        *moments,
        *moments,
        *moments,
        P(),
        P(),
        P(),
    )
    return jax.shard_map(
        per_device,
        mesh=mesh,
        in_specs=placed,
        out_specs=(*moments, *moments, *moments, P(), P(), P()),
        check_vma=False,
    )
```

```python
import functools

import jax
import jax.numpy as jnp
from jax import lax
from jax.experimental import pallas as pl
from jax.experimental.pallas import tpu as pltpu
from jax.sharding import PartitionSpec as P

D = 768
HD = 64
G = 24
PMAX = 280
L = 2
RP = 288
TOK = 280
HR = 16

EPS_NORM = 1e-06
EPS_LAMB = 1e-06
BETA = 0.5
DECAY = 0.05
BASE_RATE = 0.4
LAYER_DECAY = 0.8
SCALE = 0.125
MASKED = -1e30
HIGH = lax.Precision.HIGHEST
ROOT_HALF = 0.7071067811865476
DENSITY = 0.3989422804014327
BF = jnp.bfloat16
F32 = jnp.float32
ALL = ("dp", "mp", "teach")
VMEM_LIMIT = 56 * 1024 * 1024
FLOP_PER_US = 1_150_000_000
BRIEF = 2
FAR = 3
PARTS = ((3, 1), (2, 0))


def dot_nn(left, right):
    return lax.dot_general(
        left, right, (((1,), (0,)), ((), ())), preferred_element_type=F32
    )


def dot_nt(left, right):
    return lax.dot_general(
        left, right, (((1,), (1,)), ((), ())), preferred_element_type=F32
    )


def dot_tn(left, right):
    return lax.dot_general(
        left, right, (((0,), (0,)), ((), ())), preferred_element_type=F32
    )


def gelu_erf(values):
    return 0.5 * values * (1.0 + lax.erf(values * ROOT_HALF))


def norm_stats(values):
    centre = values - jnp.mean(values, axis=-1, keepdims=True)
    scaled = lax.rsqrt(jnp.mean(centre * centre, axis=-1, keepdims=True) + EPS_NORM)
    return centre * scaled, scaled


def norm_back(grad_out, normed, scaled, gain_row):
    grad_normed = grad_out * gain_row
    inner_sum = jnp.mean(grad_normed, axis=-1, keepdims=True)
    cross_term = jnp.mean(grad_normed * normed, axis=-1, keepdims=True)
    return scaled * (grad_normed - inner_sum - normed * cross_term)


def row_sum(values):
    return jnp.sum(values, axis=0, keepdims=True)


def tiled(half, rows):
    return rows if rows % 16 == 0 else half


def weight_copies(place_ref, run, steps, own, other, buf, sems, columns=(0, None)):
    half = own[0].shape[0]
    here = place_ref[0]
    low = columns[0]
    width = buf.shape[2]
    slots, sem = [], 0
    for slot, step in enumerate(steps):
        pieces = (FAR, FAR + 1) if step == FAR else (step,)
        copies = []
        for piece in pieces:
            size = half // len(pieces)
            unit = min(run, size)
            for at in range(0, size, unit):
                row = (piece - pieces[0]) * size + at
                for source, core in ((own[piece], here), (other[piece], 1 - here)):
                    target = (row // run) * 2 * run + core * run + row % run
                    copies.append(
                        pltpu.make_async_copy(
                            source.at[pl.ds(at, unit), pl.ds(low, width)],
                            buf.at[slot, pl.ds(pl.multiple_of(target, 16), unit)],
                            sems.at[sem],
                        )
                    )
                    sem += 1
        slots.append(copies)
    return slots


def copy_count(half, run, count):
    return 2 * count * max(half // run, 2)


def start_all(slots):
    for copies in slots:
        for copy in copies:
            copy.start()


def wait_slot(slots, now):
    for slot, copies in enumerate(slots):

        @pl.when(now == slot)
        def _():
            for copy in copies:
                copy.wait()


def split_out(half, run, place_ref, grad_buf, mine_ref, other_ref, slot):
    here = place_ref[0]
    for at in range(0, half, run):
        mine = pl.multiple_of(2 * at + here * run, 16)
        theirs = pl.multiple_of(2 * at + (1 - here) * run, 16)
        mine_ref[slot, at : at + run] = grad_buf[pl.ds(mine, run), :]
        other_ref[slot, at : at + run] = grad_buf[pl.ds(theirs, run), :]


def attn_forward_kernel(
    run,
    mp,
    ni,
    wl,
    place_ref,
    resid_ref,
    vec_ref,
    bias_ref,
    live_ref,
    own,
    other,
    first_ref,
    qkv_ref,
    att_ref,
    lse_ref,
    mid_ref,
    buf,
    sems,
):
    now = pl.program_id(0)
    slots = weight_copies(place_ref, run, range(mp), own, other, buf, sems)

    @pl.when(now == 0)
    def _():
        start_all(slots)
        resid = resid_ref[...]
        normed, _ = norm_stats(resid)
        first_ref[...] = (normed * vec_ref[0:1] + vec_ref[1:2]).astype(BF)
        mid_ref[...] = resid + vec_ref[4:5]

    wait_slot(slots, now)
    qkv = dot_nn(first_ref[...], buf[now, :, : 3 * wl]) + bias_ref[0]
    qkv_ref[0] = qkv.astype(BF)
    for image in range(ni):
        rows = slice(image * RP, (image + 1) * RP)
        live = live_ref[image] > 0.0
        for head in range(wl // HD):
            at = head * HD
            queries = qkv_ref[0, rows, at : at + HD]
            keys = qkv_ref[0, rows, wl + at : wl + at + HD]
            vals = qkv_ref[0, rows, 2 * wl + at : 2 * wl + at + HD]
            scores = jnp.where(live, dot_nt(queries, keys) * SCALE, MASKED)
            peak = jnp.max(scores, axis=-1, keepdims=True)
            expo = jnp.exp(scores - peak)
            total = jnp.sum(expo, axis=-1, keepdims=True)
            soft = (expo * (1.0 / total)).astype(BF)
            att_ref[0, rows, at : at + HD] = dot_nn(soft, vals).astype(BF)
            lse_ref[0, rows, head : head + 1] = peak + jnp.log(total)
    mid_ref[...] += dot_nt(att_ref[0], buf[now, :, 3 * wl :])


def mlp_forward_kernel(
    run,
    mp,
    chunk,
    place_ref,
    mid_ref,
    vec_ref,
    bias_ref,
    own,
    other,
    second_ref,
    hidden_ref,
    slope_ref,
    out_ref,
    buf,
    sems,
):
    now = pl.program_id(0)
    fl = hidden_ref.shape[2]
    slots = weight_copies(place_ref, run, range(mp), own, other, buf, sems)

    @pl.when(now == 0)
    def _():
        start_all(slots)
        middle = mid_ref[...]
        normed, _ = norm_stats(middle)
        second_ref[...] = (normed * vec_ref[2:3] + vec_ref[3:4]).astype(BF)
        out_ref[...] = middle + vec_ref[5:6]

    wait_slot(slots, now)
    for start in range(0, mid_ref.shape[0], chunk):
        rows = slice(start, start + chunk)
        upward = dot_nn(second_ref[rows, :], buf[now, :, :fl]) + bias_ref[0]
        share = 0.5 + 0.5 * lax.erf(upward * ROOT_HALF)
        hidden = (upward * share).astype(BF)
        hidden_ref[0, rows, :] = hidden
        slope_ref[0, rows, :] = share + upward * (DENSITY * jnp.exp(-0.5 * upward * upward))
        out_ref[rows, :] += dot_nt(hidden, buf[now, :, fl:])


def head_kernel(
    run,
    columns,
    mp,
    ni,
    wc,
    place_ref,
    resid_ref,
    vec_ref,
    bias_ref,
    ids_ref,
    labels_ref,
    mix_ref,
    scale_ref,
    weight_ref,
    pooled_ref,
    teacher_ref,
    own,
    other,
    mine_ref,
    other_ref,
    hbias_ref,
    grad_ref,
    vgrad_ref,
    loss_ref,
    buf,
    cls_buf,
    dist_buf,
    gw_buf,
    sems,
):
    half = mine_ref.shape[1]
    slots = weight_copies(place_ref, run, range(mp), own, other, buf, sems, columns)
    start_all(slots)
    cls_buf[...] = jnp.zeros_like(cls_buf)
    dist_buf[...] = jnp.zeros_like(dist_buf)
    for image in range(ni):
        at = image * RP + TOK
        cls_buf[image : image + 1, :] = resid_ref[at : at + 1, :]
        dist_buf[image : image + 1, :] = resid_ref[at + 1 : at + 2, :]
    grad_ref[...] = jnp.zeros_like(grad_ref)
    normed_c, scaled_c = norm_stats(cls_buf[...])
    normed_d, scaled_d = norm_stats(dist_buf[...])
    gain, shift = vec_ref[0:1], vec_ref[1:2]
    final_c = (normed_c * gain + shift).astype(BF)
    final_d = (normed_d * gain + shift).astype(BF)
    for copies in slots:
        for copy in copies:
            copy.wait()
    cls, dist, teach, goal = [], [], [], []
    mix = mix_ref[:, 0:1]
    for block in range(mp):
        ids = ids_ref[block]
        valid = ids >= 0
        both = bias_ref[block]
        cls.append(
            jnp.where(valid, dot_nn(final_c, buf[block, :, :wc]) + both[:, :wc], MASKED)
        )
        dist.append(
            jnp.where(valid, dot_nn(final_d, buf[block, :, wc:]) + both[:, wc:], MASKED)
        )
        teach.append(jnp.where(valid, dot_nn(pooled_ref[...], teacher_ref[block]), MASKED))
        first = (labels_ref[:, 0:1] == ids).astype(F32)
        second = (labels_ref[:, 1:2] == ids).astype(F32)
        goal.append(mix * first + (1.0 - mix) * second)

    def log_total(parts):
        peak = functools.reduce(
            jnp.maximum, [jnp.max(part, axis=-1, keepdims=True) for part in parts]
        )
        total = sum(jnp.sum(jnp.exp(part - peak), axis=-1, keepdims=True) for part in parts)
        return peak + jnp.log(total)

    log_c, log_d, log_t = log_total(cls), log_total(dist), log_total(teach)
    prob = [jnp.exp(part - log_t) for part in teach]
    dot_c = sum(jnp.sum(g * c, axis=-1, keepdims=True) for g, c in zip(goal, cls))
    dot_d = sum(jnp.sum(p * d, axis=-1, keepdims=True) for p, d in zip(prob, dist))
    loss_rows = 0.5 * (log_c - dot_c) + 0.5 * (log_d - dot_d)
    loss_ref[...] = jnp.broadcast_to(row_sum(weight_ref[:, 0:1] * loss_rows), loss_ref.shape)
    scale = scale_ref[:, 0:1]
    gfin_c = jnp.zeros(cls_buf.shape, F32)
    gfin_d = jnp.zeros(dist_buf.shape, F32)
    for block in range(mp):
        grad_c = scale * (jnp.exp(cls[block] - log_c) - goal[block])
        grad_d = scale * (jnp.exp(dist[block] - log_d) - prob[block])
        hbias_ref[block, :, :wc] = row_sum(grad_c)
        hbias_ref[block, :, wc:] = row_sum(grad_d)
        low_c, low_d = grad_c.astype(BF), grad_d.astype(BF)
        gw_buf[:, :wc] = dot_tn(final_c, low_c).astype(BF)
        gw_buf[:, wc:] = dot_tn(final_d, low_d).astype(BF)
        split_out(half, run, place_ref, gw_buf, mine_ref, other_ref, block)
        gfin_c += dot_nt(low_c, buf[block, :, :wc])
        gfin_d += dot_nt(low_d, buf[block, :, wc:])
    vgrad_ref[...] = jnp.zeros_like(vgrad_ref)
    vgrad_ref[0:1, :] = row_sum(gfin_c * normed_c) + row_sum(gfin_d * normed_d)
    vgrad_ref[1:2, :] = row_sum(gfin_c) + row_sum(gfin_d)
    cls_buf[...] = norm_back(gfin_c, normed_c, scaled_c, gain)
    dist_buf[...] = norm_back(gfin_d, normed_d, scaled_d, gain)
    for image in range(ni):
        at = image * RP + TOK
        grad_ref[at : at + 1, :] = cls_buf[image : image + 1, :]
        grad_ref[at + 1 : at + 2, :] = dist_buf[image : image + 1, :]


def mlp_backward_kernel(
    run,
    steps,
    last,
    place_ref,
    grad_ref,
    mid_ref,
    vec_ref,
    second_ref,
    hidden_ref,
    slope_ref,
    own,
    other,
    *rest,
):
    if steps[0] != FAR:
        part_ref, *rest = rest
    (
        gmid_ref,
        mine_ref,
        other_ref,
        gbias_ref,
        vgrad_ref,
        buf,
        branch_buf,
        branch_t,
        second_t,
        gw_buf,
        sems,
    ) = rest
    now = pl.program_id(0)
    fl = hidden_ref.shape[2]
    half = mine_ref.shape[1]
    slots = weight_copies(place_ref, run, steps, own, other, buf, sems)

    @pl.when(now == 0)
    def _():
        start_all(slots)
        branch_buf[...] = grad_ref[...].astype(BF)
        branch_t[...] = branch_buf[...].T
        second_t[...] = second_ref[...].T
        if steps[0] == FAR:
            gmid_ref[...] = jnp.zeros_like(gmid_ref)
        else:
            gmid_ref[...] = part_ref[...]
        vgrad_ref[...] = jnp.zeros_like(vgrad_ref)

    wait_slot(slots, now)
    gup = (dot_nn(branch_buf[...], buf[now, :, fl:]) * slope_ref[0]).astype(BF)
    gbias_ref[0] = row_sum(gup.astype(F32))
    gmid_ref[...] += dot_nt(gup, buf[now, :, :fl])
    gw_buf[:, :fl] = dot_nn(second_t[...], gup).astype(BF)
    gw_buf[:, fl:] = dot_nn(branch_t[...], hidden_ref[0]).astype(BF)
    split_out(half, run, place_ref, gw_buf, mine_ref, other_ref, 0)
    if last:

        @pl.when(now == len(steps) - 1)
        def _():
            normed, scaled = norm_stats(mid_ref[...])
            gsec = gmid_ref[...]
            grad = grad_ref[...]
            vgrad_ref[2:3, :] = row_sum(gsec * normed)
            vgrad_ref[3:4, :] = row_sum(gsec)
            vgrad_ref[5:6, :] = row_sum(grad)
            gmid = norm_back(gsec, normed, scaled, vec_ref[2:3]) + grad
            vgrad_ref[4:5, :] = row_sum(gmid)
            gmid_ref[...] = gmid


def attn_backward_kernel(
    run,
    ni,
    wl,
    steps,
    last,
    place_ref,
    gmid_ref,
    resid_ref,
    vec_ref,
    live_ref,
    first_ref,
    qkv_ref,
    att_ref,
    lse_ref,
    own,
    other,
    *rest,
):
    if steps[0] != FAR:
        part_ref, *rest = rest
    (
        gres_ref,
        mine_ref,
        other_ref,
        gbias_ref,
        vgrad_ref,
        buf,
        mixed_buf,
        mixed_t,
        first_t,
        gatt_buf,
        gqkv_buf,
        gw_buf,
        sems,
    ) = rest
    now = pl.program_id(0)
    half = mine_ref.shape[1]
    slots = weight_copies(place_ref, run, steps, own, other, buf, sems)

    @pl.when(now == 0)
    def _():
        start_all(slots)
        mixed_buf[...] = gmid_ref[...].astype(BF)
        mixed_t[...] = mixed_buf[...].T
        first_t[...] = first_ref[...].T
        if steps[0] == FAR:
            gres_ref[...] = jnp.zeros_like(gres_ref)
        else:
            gres_ref[...] = part_ref[...]
        vgrad_ref[...] = jnp.zeros_like(vgrad_ref)

    wait_slot(slots, now)
    gatt_buf[...] = dot_nn(mixed_buf[...], buf[now, :, 3 * wl :]).astype(BF)
    for image in range(ni):
        rows = slice(image * RP, (image + 1) * RP)
        live = live_ref[image] > 0.0
        for head in range(wl // HD):
            at = head * HD
            queries = qkv_ref[0, rows, at : at + HD]
            keys = qkv_ref[0, rows, wl + at : wl + at + HD]
            vals = qkv_ref[0, rows, 2 * wl + at : 2 * wl + at + HD]
            gatt = gatt_buf[rows, at : at + HD]
            scores = jnp.where(live, dot_nt(queries, keys) * SCALE, MASKED)
            soft = jnp.exp(scores - lse_ref[0, rows, head : head + 1])
            gsoft = dot_nt(gatt, vals)
            inner = jnp.sum(soft * gsoft, axis=-1, keepdims=True)
            gscore = (soft * (gsoft - inner)).astype(BF)
            gqkv_buf[rows, at : at + HD] = (dot_nn(gscore, keys) * SCALE).astype(BF)
            gqkv_buf[rows, wl + at : wl + at + HD] = (dot_tn(gscore, queries) * SCALE).astype(BF)
            gqkv_buf[rows, 2 * wl + at : 2 * wl + at + HD] = dot_tn(soft.astype(BF), gatt).astype(BF)
    gqkv = gqkv_buf[...]
    gbias_ref[0] = row_sum(gqkv.astype(F32))
    gres_ref[...] += dot_nt(gqkv, buf[now, :, : 3 * wl])
    gw_buf[:, : 3 * wl] = dot_nn(first_t[...], gqkv).astype(BF)
    gw_buf[:, 3 * wl :] = dot_nn(mixed_t[...], att_ref[0]).astype(BF)
    split_out(half, run, place_ref, gw_buf, mine_ref, other_ref, 0)
    if last:

        @pl.when(now == len(steps) - 1)
        def _():
            normed, scaled = norm_stats(resid_ref[...])
            gfirst = gres_ref[...]
            vgrad_ref[0:1, :] = row_sum(gfirst * normed)
            vgrad_ref[1:2, :] = row_sum(gfirst)
            gres_ref[...] = norm_back(gfirst, normed, scaled, vec_ref[0:1]) + gmid_ref[...]


def call(kernel, outs, scratch, ins, steps=None, after=()):
    def whole(array):
        return pl.BlockSpec(array.shape, lambda i: (0,) * array.ndim)

    def each(array, base=0, stride=1):
        return pl.BlockSpec(
            (1, *array.shape[1:]), lambda i: (base + stride * i, *(0,) * (array.ndim - 1))
        )

    specs, arrays, sizes = [], [], []
    for item in [*ins, ("group", list(after))]:
        kind, item = item if isinstance(item, tuple) else ("vmem", item)
        group = item if kind == "group" else [item]
        sizes.append(len(group) if kind == "group" else None)
        if kind in ("group", "smem"):
            space = pl.ANY if kind == "group" else pltpu.SMEM
            specs += [pl.BlockSpec(memory_space=space)] * len(group)
        elif kind == "each":
            specs.append(each(item, steps[0], steps[1] - steps[0]))
        elif steps:
            specs.append(whole(item))
        else:
            specs.append(pl.BlockSpec(memory_space=pltpu.VMEM))
        arrays += group

    def grouped(*refs):
        given, at = [], 0
        for size in sizes:
            given.append(refs[at] if size is None else refs[at : at + size])
            at += 1 if size is None else size
        return kernel(*given[:-1], *refs[at:])

    out_shape = [jax.ShapeDtypeStruct(*out[:2]) for out in outs]
    if steps:
        out_specs = [
            each(shape) if len(out) > 2 else whole(shape) for out, shape in zip(outs, out_shape)
        ]
        grid = {"grid": (len(steps),)}
    else:
        out_specs = [pl.BlockSpec(memory_space=pltpu.VMEM)] * len(out_shape)
        grid = {}
    moved = sum(a.size * a.dtype.itemsize for a in arrays)
    moved += sum(s.size * s.dtype.itemsize for s in out_shape)
    return pl.pallas_call(
        grouped,
        out_shape=out_shape,
        in_specs=specs,
        out_specs=out_specs,
        **grid,
        scratch_shapes=scratch,
        compiler_params=pltpu.CompilerParams(vmem_limit_bytes=VMEM_LIMIT),
        cost_estimate=pl.CostEstimate(
            flops=BRIEF * FLOP_PER_US, bytes_accessed=moved, transcendentals=0
        ),
    )(*arrays)


def tie(values, *behind):
    if not behind:
        return values
    return lax.optimization_barrier((values, behind))[0]


def swap(values, axis, distance):
    size = lax.axis_size(axis)
    return lax.ppermute(values, axis, [(rank, rank ^ distance) for rank in range(size)])


class Gather:
    def __init__(self, near):
        self.near = near

    def square(self, *behind):
        near = tie(self.near, *behind)
        self.own = [near, swap(near, "mp", 1), swap(near, "mp", 2)]
        self.other = [swap(near, "teach", 1)]
        return [near]

    def corner(self, *behind):
        near, by_one, by_two = self.own
        cut = near.shape[0] // 2
        by_one, by_two = tie((by_one, by_two), *behind)
        lower, upper = by_two[:cut], by_one[cut:]
        self.own = [near, by_one, by_two, swap(lower, "mp", 1), swap(upper, "mp", 2)]
        self.other += [swap(by_one, "teach", 1), swap(by_two, "teach", 1)]
        return [lower, upper]

    def cores(self, *behind):
        far = tie(tuple(self.own[3:]), *behind)
        self.own[3:] = far
        self.other += [swap(piece, "teach", 1) for piece in far]

    def refs(self):
        return [("group", self.own), ("group", self.other)]


def add_low(left, right):
    return (left.astype(F32) + right.astype(F32)).astype(BF)


def sum_over(values, axis):
    distance = 1
    while distance < lax.axis_size(axis):
        values = values + swap(values, axis, distance)
        distance *= 2
    return values


def sum_all(values):
    for axis in ("teach", "mp", "dp"):
        values = sum_over(values, axis)
    return values


def join_kernel(sizes, bit_ref, own_ref, got_ref, out_ref):
    first = bit_ref[0] == 0
    size = sizes[0]
    out_ref[:size] = own_ref[:size] + got_ref[:size]
    at, to = size, size
    for size in sizes[1:]:
        own, got = own_ref[at : at + size], got_ref[at : at + size]
        out_ref[to : to + size] = jnp.where(first, own, got)
        out_ref[to + size : to + 2 * size] = jnp.where(first, got, own)
        at, to = at + size, to + 2 * size


def sum_and_gather(values, everywhere, cores, square):
    parts = jnp.concatenate([values, everywhere, cores])
    sizes = [values.shape[0], everywhere.shape[0], cores.shape[0]]
    for axis in ("dp", "teach", "mp"):
        distance = 1
        if axis == "mp":
            cores = parts[sizes[0] + sizes[1] :]
            parts, sizes = parts[: sizes[0] + sizes[1]], sizes[:2]
        while distance < lax.axis_size(axis):
            got = swap(parts, axis, distance)
            bit = (lax.axis_index(axis) // distance) % 2
            new_sizes = [sizes[0], *[2 * size for size in sizes[1:]]]
            parts = call(
                functools.partial(join_kernel, sizes),
                [((sum(new_sizes), 128), F32)],
                [],
                [("smem", bit.astype(jnp.int32).reshape(1)), parts, got],
            )[0]
            sizes = new_sizes
            if axis == "mp":
                other = swap(square, axis, distance)
                pair = [jnp.where(bit == 0, square, other), jnp.where(bit == 0, other, square)]
                square = jnp.concatenate(pair)
            distance *= 2
    return parts[: sizes[0]], parts[sizes[0] :], cores, square


def gather_mp(values):
    size = lax.axis_size("mp")
    return jnp.stack([values] + [swap(values, "mp", step) for step in range(1, size)])


class Scatter:
    def __init__(self):
        self.waiting = []
        self.block = {}
        self.extra = None
        self.sections = []
        self.pieces = None

    def cores(self, steps, mine, other):
        self.waiting.append((steps, mine, swap(other, "teach", 1)))

    def attach(self, *sections):
        self.sections = [mine.shape[1] for mine, _ in sections]
        other = jnp.concatenate([other for _, other in sections], axis=1)
        self.extra = (
            jnp.concatenate([mine for mine, _ in sections], axis=1),
            swap(other, "teach", 1),
        )

    def added(self, *behind):
        for steps, mine, got in self.waiting:
            got = tie(got, *behind)
            for slot, step in enumerate(steps):
                block = add_low(mine[slot], got[slot])
                self.cuts = [block.shape[0], *self.sections]
                if self.extra:
                    more = add_low(self.extra[0][step], self.extra[1][step])
                    block = jnp.concatenate([block, more])
                self.block[step] = block
        self.waiting = []

    def corner(self, *behind):
        self.added(*behind)
        self.cut = cut = -(-self.block[FAR].shape[0] // 32) * 16
        sent = [self.block[FAR][:cut], self.block[FAR][cut:]]
        self.by_one = swap(sent[0], "mp", 1)
        self.by_two = swap(sent[1], "mp", 2)
        return sent

    def square(self, *behind):
        self.added(*behind)
        one, two = self.block[1], self.block[2]
        cut = self.cut
        by_one, by_two = tie((self.by_one, self.by_two), *behind)
        sent = [
            jnp.concatenate([one[:cut], add_low(one[cut:], by_two)]),
            jnp.concatenate([add_low(two[:cut], by_one), two[cut:]]),
        ]
        self.by_one = swap(sent[0], "mp", 1)
        self.by_two = swap(sent[1], "mp", 2)
        return sent

    def summed(self, *behind):
        by_one, by_two = tie((self.by_one, self.by_two), *behind)
        total = self.block[0].astype(F32) + (by_one.astype(F32) + by_two.astype(F32))
        dp = lax.axis_size("dp")
        width = total.shape[1]
        parts, at = [], 0
        for cut in self.cuts:
            parts.append(total[at : at + cut].reshape(dp, -1, width))
            at += cut
        return jnp.concatenate(parts, axis=1).astype(BF).reshape(total.shape)

    def rows(self, *behind):
        total = self.summed(*behind)
        self.pieces = lax.psum_scatter(total, "dp", scatter_dimension=0, tiled=True)
        return [total]

    def result(self):
        return self.pieces.astype(F32)


def adam_direction(gradient, first_moment, second_moment, correct_first, correct_second):
    new_first = BETA * first_moment + (1.0 - BETA) * gradient
    new_second = BETA * second_moment + (1.0 - BETA) * gradient * gradient
    return (
        new_first,
        new_second,
        new_first / correct_first / (jnp.sqrt(new_second / correct_second) + EPS_LAMB),
    )


def split_params(values):
    layered = values[1 : 1 + 6 * L].reshape(L, 6)
    return (
        values[0],
        layered[:, :4],
        layered[:, 4:],
        values[1 + 6 * L : 3 + 6 * L],
        values[3 + 6 * L],
        values[4 + 6 * L],
    )


def expand_params(pieces):
    return (
        pieces[0],
        pieces[1][:, :, None, None],
        pieces[2][:, :, None, None],
        pieces[3][:, None, None],
        pieces[4],
        pieces[5],
    )


def order_params(pieces):
    layered = jnp.concatenate([pieces[1], pieces[2]], axis=1).reshape(-1)
    return jnp.concatenate([pieces[0][None], layered, pieces[3], pieces[4][None], pieces[5][None]])


def squares_of(pieces, mp_first, data_first):
    return order_params(
        (
            jnp.sum(pieces[0] * pieces[0]) * mp_first,
            jnp.sum(pieces[1] * pieces[1], axis=(2, 3)),
            jnp.sum(pieces[2] * pieces[2], axis=(2, 3)),
            jnp.sum(pieces[3] * pieces[3], axis=(1, 2)),
            jnp.sum(pieces[4] * pieces[4]) * mp_first * data_first,
            jnp.sum(pieces[5] * pieces[5]) * data_first,
        )
    )


def per_device(
    patches,
    grid_sizes,
    label_ids,
    label_mix,
    image_weight,
    teacher_stem,
    teacher_head,
    patch_weight,
    attn_weight,
    mlp_weight,
    head_weight,
    vector_params,
    split_biases,
    patch_first,
    attn_first,
    mlp_first,
    head_first,
    vector_first,
    bias_first,
    patch_second,
    attn_second,
    mlp_second,
    head_second,
    vector_second,
    bias_second,
    decay_mask,
    layer_ids,
    step_count,
):
    dp, mp, teach = lax.axis_size("dp"), lax.axis_size("mp"), lax.axis_size("teach")
    here_mp = lax.axis_index("mp")
    here_teach = lax.axis_index("teach")
    place = ("smem", here_teach.astype(jnp.int32).reshape(1))
    mp_first = (here_mp == 0).astype(F32)
    data_first = (lax.axis_index(("dp", "teach")) == 0).astype(F32)
    rows_own = patch_weight.shape[0]
    half = dp * rows_own
    wl = attn_weight.shape[3]
    fl = mlp_weight.shape[3]
    cl = head_weight.shape[2]
    wc = -(-cl // 128) * 128
    head_row = 6 * L

    run = tiled(half, rows_own)

    def inward(values):
        if run == rows_own:
            return values
        lead = values.shape[:-1]
        cut = values.reshape(*lead, dp, teach, rows_own)
        return jnp.swapaxes(cut, -3, -2).reshape(*lead, D)

    def outward(values):
        if run == rows_own:
            return values
        lead = values.shape[:-1]
        cut = values.reshape(*lead, teach, dp, rows_own)
        return jnp.swapaxes(cut, -3, -2).reshape(*lead, D)

    ni = patches.shape[0] // mp

    def take(array):
        return lax.dynamic_slice_in_dim(array, here_mp * ni, ni, 0)

    weight_part = jnp.sum(image_weight).reshape(1)
    patches, grid_sizes, label_ids = take(patches), take(grid_sizes), take(label_ids)
    label_mix, image_weight = take(label_mix), take(image_weight)

    patch_low = inward(patch_weight).astype(BF)
    attn_low = [
        jnp.concatenate([attn_weight[layer, part] for part in range(4)], axis=1).astype(BF)
        for layer in range(L)
    ]
    mlp_low = [
        jnp.concatenate([mlp_weight[layer, 0], mlp_weight[layer, 1]], axis=1).astype(BF)
        for layer in range(L)
    ]
    head_pad = jnp.pad(head_weight, ((0, 0), (0, 0), (0, wc - cl)))
    head_low = jnp.concatenate([head_pad[0], head_pad[1]], axis=1).astype(BF)

    def gather_dp(*pieces):
        wide_piece = lax.all_gather(jnp.concatenate(pieces, axis=1), "dp", axis=0, tiled=True)
        cuts, at = [], 0
        for piece in pieces:
            cuts.append(wide_piece[:, at : at + piece.shape[1]])
            at += piece.shape[1]
        return cuts

    near = gather_dp(patch_low, attn_low[0]) + gather_dp(mlp_low[0])
    mlp_low[-1] = jnp.concatenate([mlp_low[-1], head_low], axis=1)
    head_columns = (2 * fl, 2 * wc)
    rest = [piece for layer in range(1, L) for piece in (attn_low[layer], mlp_low[layer])]
    near += gather_dp(*rest)
    bias_all = gather_mp(split_biases)
    teacher_all = gather_mp(jnp.pad(teacher_head, ((0, 0), (0, wc - cl))))

    vec_in = inward(vector_params)
    layer_vecs = [
        jnp.pad(vec_in[6 * layer : 6 * layer + 6], ((0, 2), (0, 0))) for layer in range(L)
    ]
    final_vec = jnp.pad(vec_in[head_row : head_row + 2], ((0, 6), (0, 0)))
    attn_bias, up_bias = [], []
    span = 2 * wl + fl
    for layer in range(L):
        part = bias_all[:, layer * span : (layer + 1) * span]
        zero = jnp.zeros((mp, wl), F32)
        attn_bias.append(
            jnp.concatenate([part[:, :wl], zero, part[:, wl : 2 * wl]], axis=1)[:, None]
        )
        up_bias.append(part[:, None, 2 * wl :])
    pad_class = ((0, 0), (0, wc - cl))
    head_bias = jnp.concatenate(
        [
            jnp.pad(bias_all[:, L * span : L * span + cl], pad_class),
            jnp.pad(bias_all[:, L * span + cl : L * span + 2 * cl], pad_class),
        ],
        axis=1,
    )[:, None]

    grid_rows, grid_cols = grid_sizes[:, 0:1], grid_sizes[:, 1:2]
    slot_ids = jnp.arange(PMAX, dtype=jnp.int32)[None, :]
    patch_live = slot_ids < grid_rows * grid_cols
    live_float = patch_live.astype(F32)
    live_rows = jnp.concatenate(
        [live_float, jnp.ones((ni, 2), F32), jnp.zeros((ni, RP - PMAX - 2), F32)], axis=1
    )[:, None, :]
    table = jnp.arange(G, dtype=jnp.int32)
    source_patch = jnp.concatenate(
        [
            jnp.ones((ni, PMAX, 1), F32),
            jnp.zeros((ni, PMAX, 2), F32),
            ((slot_ids // grid_cols)[..., None] == table).astype(F32),
            ((slot_ids % grid_cols)[..., None] == table).astype(F32),
        ],
        axis=2,
    )
    source_token = jnp.broadcast_to(jnp.eye(2, 3 + 2 * G, 1, dtype=F32), (ni, 2, 3 + 2 * G))
    sources = jnp.concatenate(
        [source_patch, source_token, jnp.zeros((ni, RP - PMAX - 2, 3 + 2 * G), F32)], axis=1
    ).reshape(ni * RP, 3 + 2 * G)

    stem_rows = gelu_erf(dot_nn(patches.reshape(ni * PMAX, -1), teacher_stem)).reshape(ni, PMAX, -1)
    pooled = (
        jnp.sum(stem_rows * live_float[..., None], axis=1)
        / jnp.sum(live_float, axis=1, keepdims=True)
    ).astype(BF)

    ranks = here_mp ^ jnp.arange(mp, dtype=jnp.int32)
    quarter = rows_own // mp
    patch_rows = jnp.pad(patches, ((0, 0), (0, RP - PMAX), (0, 0))).reshape(ni * RP, -1)
    sides = here_teach ^ jnp.arange(teach, dtype=jnp.int32)
    patches_t = patch_rows.T.reshape(dp, teach, mp, quarter, ni * RP).transpose(1, 2, 0, 3, 4)
    patches_t = patches_t[sides][:, ranks].reshape(-1, ni * RP)

    def wide(values):
        return jnp.pad(values.reshape(ni, -1), ((0, HR - ni), (0, 0)))

    lanes = jnp.arange(wc, dtype=jnp.int32)
    class_ids = jnp.where(lanes[None] < cl, ranks[:, None] * cl + lanes[None], -1)[:, None]
    head_small = [class_ids, wide(label_ids), wide(label_mix), wide(pooled)]

    near[0], near[1] = tie(
        (near[0], near[1]),
        *attn_bias,
        *up_bias,
        head_bias,
        *layer_vecs,
        final_vec,
        live_rows,
        sources,
        patches_t,
        *head_small,
        teacher_all,
    )
    patch_own = near[0]
    patch_other = swap(patch_own, "teach", 1)
    units = [Gather(piece) for piece in near[1:]]
    attn_units, mlp_units, head_unit = units[0::2], units[1::2], units[-1]

    first_core = here_teach == 0
    patch_full = jnp.stack(
        [
            jnp.where(first_core, patch_own, patch_other).reshape(dp, rows_own, D),
            jnp.where(first_core, patch_other, patch_own).reshape(dp, rows_own, D),
        ],
        axis=1,
    ).reshape(D, D)
    residual = dot_nn(patch_rows, patch_full) + jnp.dot(
        sources, vec_in[head_row + 2 :], precision=HIGH
    )

    n = ni * RP
    parts = copy_count(half, run, mp)
    saved = []
    units[0].square()
    units[0].corner(residual)
    units[1].square(*units[0].own[3:])

    def arrive(at, done):
        here = units[at]
        ahead = units[at + 1 : at + 2]
        if at > 0:
            here.corner(done)
            for unit in ahead:
                unit.square(*here.own[3:], done)
        here.cores(*[unit.own[0] for unit in ahead])
        return [unit.own[0] for unit in ahead]

    for layer in range(L):
        sending = arrive(2 * layer, residual)
        first, qkv, attended, lse, middle = call(
            functools.partial(attn_forward_kernel, run, mp, ni, wl),
            [
                ((n, D), BF),
                ((mp, n, 3 * wl), BF, "each"),
                ((mp, n, wl), BF, "each"),
                ((mp, n, wl // HD), F32, "each"),
                ((n, D), F32),
            ],
            [pltpu.VMEM((mp, D, 4 * wl), BF), pltpu.SemaphoreType.DMA((parts,))],
            [place, residual, layer_vecs[layer], ("each", attn_bias[layer]), live_rows]
            + attn_units[layer].refs(),
            range(mp),
            sending,
        )
        if layer == 0:
            weight_sum = sum_over(sum_over(tie(weight_part, middle), "teach"), "dp")[0]
            shares = [
                wide(0.5 * image_weight / weight_sum),
                wide(image_weight / weight_sum),
            ]
            for unit in units[2:]:
                unit.near = tie(unit.near, *shares)
        sending = arrive(2 * layer + 1, middle)
        second, hidden, slope, output = call(
            functools.partial(mlp_forward_kernel, run, mp, n // 4),
            [((n, D), BF), ((mp, n, fl), BF, "each"), ((mp, n, fl), F32, "each"), ((n, D), F32)],
            [pltpu.VMEM((mp, D, 2 * fl), BF), pltpu.SemaphoreType.DMA((parts,))],
            [place, middle, layer_vecs[layer], ("each", up_bias[layer])]
            + mlp_units[layer].refs(),
            range(mp),
            sending,
        )
        saved.append((residual, first, qkv, attended, lse, middle, second, hidden, slope))
        residual = output

    head_mine, head_other, head_bgrad, grad, final_vgrad, loss_part = call(
        functools.partial(head_kernel, run, head_columns, mp, ni, wc),
        [
            ((mp, half, 2 * wc), BF),
            ((mp, half, 2 * wc), BF),
            ((mp, 1, 2 * wc), F32),
            ((n, D), F32),
            ((8, D), F32),
            ((8, 128), F32),
        ],
        [
            pltpu.VMEM((mp, D, 2 * wc), BF),
            pltpu.VMEM((HR, D), F32),
            pltpu.VMEM((HR, D), F32),
            pltpu.VMEM((D, 2 * wc), BF),
            pltpu.SemaphoreType.DMA((parts,)),
        ],
        [
            place,
            residual,
            final_vec,
            head_bias,
            *head_small[:3],
            *shares,
            head_small[3],
            teacher_all,
            *head_unit.refs(),
        ],
    )
    head_out = Scatter()
    head_out.cores(range(mp), head_mine, head_other)
    mlp_out, attn_out = [Scatter() for _ in range(L)], [Scatter() for _ in range(L)]
    agenda = {0: [], 1: [(head_out, "corner")], 2: [(head_out, "square")], 3: [(head_out, "rows")]}
    slot = 0
    for layer in reversed(range(L)):
        plan = (
            (mlp_out[layer], "corner", 2),
            (mlp_out[layer], "square", 3),
            (mlp_out[layer], "rows", 5 if layer else 4),
            (attn_out[layer], "corner", 4),
            (attn_out[layer], "square", 5),
            (attn_out[layer], "rows", 6),
        )
        for unit, what, moment in plan:
            agenda.setdefault(slot + moment, []).append((unit, what))
        slot += 4
    final = slot

    def proceed(moment, done):
        sent = []
        for unit, what in agenda.pop(moment, []):
            sent += getattr(unit, what)(done)
        return sent

    sending = [head_other]
    gain_list, bias_list = [None] * L, [None] * L
    slot = 0
    for layer in reversed(range(L)):
        resid_in, first, qkv, attended, lse, middle, second, hidden, slope = saved[layer]
        part = []
        up_bgrad, qkv_bgrad = {}, {}
        for steps in PARTS:
            count = len(steps)
            gmid, mine, other, bgrad, mlp_vgrad = call(
                functools.partial(mlp_backward_kernel, run, steps, steps is PARTS[-1]),
                [
                    ((n, D), F32),
                    ((count, half, 2 * fl), BF, "each"),
                    ((count, half, 2 * fl), BF, "each"),
                    ((count, 1, fl), F32, "each"),
                    ((8, D), F32),
                ],
                [
                    pltpu.VMEM((count, D, 2 * fl), BF),
                    pltpu.VMEM((n, D), BF),
                    pltpu.VMEM((D, n), BF),
                    pltpu.VMEM((D, n), BF),
                    pltpu.VMEM((D, 2 * fl), BF),
                    pltpu.SemaphoreType.DMA((copy_count(half, run, count),)),
                ],
                [place, grad, middle, layer_vecs[layer], second, ("each", hidden), ("each", slope)]
                + mlp_units[layer].refs()
                + part,
                steps,
                sending,
            )
            part = [gmid]
            up_bgrad.update({step: bgrad[at] for at, step in enumerate(steps)})
            slot += 1
            mlp_out[layer].cores(steps, mine, other)
            sending = [other] + proceed(slot, gmid)
        part = []
        for steps in PARTS:
            count = len(steps)
            grad, mine, other, bgrad, attn_vgrad = call(
                functools.partial(attn_backward_kernel, run, ni, wl, steps, steps is PARTS[-1]),
                [
                    ((n, D), F32),
                    ((count, half, 4 * wl), BF, "each"),
                    ((count, half, 4 * wl), BF, "each"),
                    ((count, 1, 3 * wl), F32, "each"),
                    ((8, D), F32),
                ],
                [
                    pltpu.VMEM((count, D, 4 * wl), BF),
                    pltpu.VMEM((n, D), BF),
                    pltpu.VMEM((D, n), BF),
                    pltpu.VMEM((D, n), BF),
                    pltpu.VMEM((n, wl), BF),
                    pltpu.VMEM((n, 3 * wl), BF),
                    pltpu.VMEM((D, 4 * wl), BF),
                    pltpu.SemaphoreType.DMA((copy_count(half, run, count),)),
                ],
                [place, gmid, resid_in, layer_vecs[layer], live_rows, first]
                + [("each", qkv), ("each", attended), ("each", lse)]
                + attn_units[layer].refs()
                + part,
                steps,
                sending,
            )
            part = [grad]
            qkv_bgrad.update({step: bgrad[at] for at, step in enumerate(steps)})
            slot += 1
            attn_out[layer].cores(steps, mine, other)
            if slot < final:
                sending = [other] + proceed(slot, grad)
        gain_list[layer] = (attn_vgrad + mlp_vgrad)[:6]
        bias_list[layer] = jnp.concatenate(
            [
                jnp.concatenate([qkv_bgrad[step][:, :wl] for step in range(mp)]),
                jnp.concatenate([qkv_bgrad[step][:, 2 * wl :] for step in range(mp)]),
                jnp.concatenate([up_bgrad[step] for step in range(mp)]),
            ],
            axis=1,
        )
    ahead = mlp_out[0].rows(grad)
    agenda[final].remove((mlp_out[0], "rows"))
    grad = tie(grad, *ahead)
    patch_grad = dot_nn(patches_t, grad.astype(BF)).astype(BF)
    patch_grad = patch_grad.reshape(teach, mp, dp * quarter, D)

    source_grads = lax.dot_general(
        sources, grad, (((0,), (0,)), ((), ())), precision=HIGH, preferred_element_type=F32
    )
    vector_grads = jnp.concatenate(gain_list + [final_vgrad[:2], source_grads], axis=0)
    bias_blocks = jnp.concatenate(
        bias_list + [head_bgrad[:, 0, :cl], head_bgrad[:, 0, wc : wc + cl]], axis=1
    )
    devices = dp * teach
    vector_piece = -(-vector_params.size // (mp * devices * 1024)) * 1024
    bias_piece = -(-split_biases.size // (devices * 1024)) * 1024

    def padded(flat, size):
        return jnp.pad(flat, ((0, 0), (0, size - flat.shape[1])))

    more_rows = -(rows_own + quarter) % 16
    while more_rows * D < vector_piece + bias_piece:
        more_rows += 16
    vector_cut = padded(vector_grads.reshape(1, -1), vector_piece * mp * devices)
    small = jnp.concatenate(
        [
            vector_cut.reshape(mp, devices, vector_piece)[ranks],
            padded(bias_blocks, bias_piece * devices).reshape(mp, devices, bias_piece),
            jnp.zeros((mp, devices, more_rows * D - vector_piece - bias_piece), F32),
        ],
        axis=2,
    )
    small = small.astype(BF).reshape(mp, teach, dp * more_rows, D)

    def small_half(core):
        return lax.dynamic_index_in_dim(small, core, 1, False)

    attn_out[0].attach(
        (patch_grad[0], patch_grad[1]),
        (small_half(here_teach), small_half(1 - here_teach)),
    )
    for moment in sorted(agenda):
        for unit, what in agenda[moment]:
            ahead += getattr(unit, what)(*ahead)
    first_rows = attn_out[0].result()
    patch_grad = outward(first_rows[rows_own : rows_own + quarter])
    small = first_rows[rows_own + quarter :].reshape(-1, 128)
    vector_grads = small[: vector_piece // 128]
    bias_grads = small[vector_piece // 128 : (vector_piece + bias_piece) // 128]

    attn_list = [first_rows[:rows_own]] + [unit.result() for unit in attn_out[1:]]
    mlp_list = [unit.result() for unit in mlp_out]
    head_grads = head_out.result()
    attn_grads = jnp.stack(
        [
            jnp.stack([attn_list[layer][:, part * wl : (part + 1) * wl] for part in range(4)])
            for layer in range(L)
        ]
    )
    mlp_grads = jnp.stack(
        [jnp.stack([mlp_list[layer][:, :fl], mlp_list[layer][:, fl:]]) for layer in range(L)]
    )
    head_grads = jnp.stack([head_grads[:, :cl], head_grads[:, wc : wc + cl]])

    step_power = step_count[0].astype(F32)
    correct_first = 1.0 - jnp.power(BETA, step_power)
    correct_second = 1.0 - jnp.power(BETA, step_power)
    weights = (patch_weight, attn_weight, mlp_weight, head_weight, vector_params, split_biases)
    firsts = (patch_first, attn_first, mlp_first, head_first, vector_first, bias_first)
    seconds = (patch_second, attn_second, mlp_second, head_second, vector_second, bias_second)
    decay_pieces = expand_params(split_params(decay_mask.astype(F32)))

    def direct(gradient, first, second, weight, decay):
        new_first, new_second, direction = adam_direction(
            gradient, first, second, correct_first, correct_second
        )
        return new_first, new_second, direction + DECAY * decay * weight

    device = lax.axis_index(("teach", "dp"))

    def patch_cut(array):
        return lax.dynamic_slice_in_dim(array, here_mp * quarter, quarter, 0)

    def vector_part(array):
        flat = padded(inward(array).reshape(1, -1), vector_piece * mp * devices)[0]
        at = (here_mp * devices + device) * vector_piece
        return lax.dynamic_slice_in_dim(flat, at, vector_piece, 0).reshape(-1, 128)

    def bias_part(array):
        flat = padded(array.reshape(1, -1), bias_piece * devices)[0]
        part = lax.dynamic_slice_in_dim(flat, device * bias_piece, bias_piece, 0)
        return part.reshape(-1, 128)

    pieces = (patch_grad, attn_grads, mlp_grads, head_grads, vector_grads, bias_grads)
    own_part = (patch_cut, None, None, None, vector_part, bias_part)
    results = []
    for slot, part in enumerate(own_part):
        others = (firsts[slot], seconds[slot], weights[slot])
        if part is not None:
            others = [part(array) for array in others]
        results.append(direct(pieces[slot], *others, decay_pieces[slot]))
    totals = jnp.concatenate(
        [
            squares_of(weights, mp_first, data_first),
            squares_of([result[2] for result in results], 1.0, 1.0),
            loss_part[0, :1],
        ]
    )
    npar = (totals.size - 1) // 2
    totals, vector_grads, bias_grads, patch_grad = sum_and_gather(
        jnp.pad(totals, (0, -totals.size % 1024)).reshape(-1, 128),
        vector_grads,
        bias_grads,
        patch_grad,
    )
    gathered = {
        0: patch_grad,
        4: outward(vector_grads.reshape(-1)[: vector_params.size].reshape(vector_params.shape)),
        5: bias_grads.reshape(-1)[: split_biases.size],
    }
    for slot, gradient in gathered.items():
        results[slot] = direct(
            gradient, firsts[slot], seconds[slot], weights[slot], decay_pieces[slot]
        )
    directions = [result[2] for result in results]
    totals = totals.reshape(-1)
    weights_sq, direction_sq, loss_value = totals[:npar], totals[npar : 2 * npar], totals[2 * npar]
    weight_norm = jnp.sqrt(weights_sq)
    update_norm = jnp.sqrt(direction_sq)
    trust_ratio = weight_norm / update_norm
    rates = BASE_RATE * jnp.power(LAYER_DECAY, 2.0 - layer_ids.astype(F32)) * trust_ratio
    rate_pieces = expand_params(split_params(rates))
    updated = [weights[slot] - rate_pieces[slot] * directions[slot] for slot in range(6)]
    norm_table = jnp.stack([weight_norm, update_norm])
    return (
        *updated,
        *[results[slot][0] for slot in range(6)],
        *[results[slot][1] for slot in range(6)],
        norm_table,
        trust_ratio,
        loss_value,
    )


def solution(mesh):
    rows = ("dp", "teach")
    moments = (
        P(rows, None),
        P(None, None, rows, "mp"),
        P(None, None, rows, "mp"),
        P(None, rows, "mp"),
        P(),
        P("mp"),
    )
    placed = (
        P(rows, None, None),
        P(rows, None),
        P(rows, None),
        P(rows),
        P(rows),
        P(),
        P(None, "mp"),
        *moments,
        *moments,
        *moments,
        P(),
        P(),
        P(),
    )
    return jax.shard_map(
        per_device,
        mesh=mesh,
        in_specs=placed,
        out_specs=(*moments, *moments, *moments, P(), P(), P()),
        check_vma=False,
    )
```

```python
import functools

import jax
import jax.numpy as jnp
from jax import lax
from jax.experimental import pallas as pl
from jax.experimental.pallas import tpu as pltpu
from jax.sharding import PartitionSpec as P

D = 768
HD = 64
G = 24
PMAX = 280
L = 2
RP = 288
TOK = 280
HR = 16

EPS_NORM = 1e-06
EPS_LAMB = 1e-06
BETA = 0.5
DECAY = 0.05
BASE_RATE = 0.4
LAYER_DECAY = 0.8
SCALE = 0.125
MASKED = -1e30
HIGH = lax.Precision.HIGHEST
ROOT_HALF = 0.7071067811865476
DENSITY = 0.3989422804014327
BF = jnp.bfloat16
F32 = jnp.float32
ALL = ("dp", "mp", "teach")
VMEM_LIMIT = 56 * 1024 * 1024
FLOP_PER_US = 1_150_000_000
BRIEF = 2
FAR = 3
PARTS = ((3, 1), (2, 0))


def dot_nn(left, right):
    return lax.dot_general(
        left, right, (((1,), (0,)), ((), ())), preferred_element_type=F32
    )


def dot_nt(left, right):
    return lax.dot_general(
        left, right, (((1,), (1,)), ((), ())), preferred_element_type=F32
    )


def dot_tn(left, right):
    return lax.dot_general(
        left, right, (((0,), (0,)), ((), ())), preferred_element_type=F32
    )


def gelu_erf(values):
    return 0.5 * values * (1.0 + lax.erf(values * ROOT_HALF))


def norm_stats(values):
    centre = values - jnp.mean(values, axis=-1, keepdims=True)
    scaled = lax.rsqrt(jnp.mean(centre * centre, axis=-1, keepdims=True) + EPS_NORM)
    return centre * scaled, scaled


def norm_back(grad_out, normed, scaled, gain_row):
    grad_normed = grad_out * gain_row
    inner_sum = jnp.mean(grad_normed, axis=-1, keepdims=True)
    cross_term = jnp.mean(grad_normed * normed, axis=-1, keepdims=True)
    return scaled * (grad_normed - inner_sum - normed * cross_term)


def row_sum(values):
    return jnp.sum(values, axis=0, keepdims=True)


def tiled(half, rows):
    return rows if rows % 16 == 0 else half


def weight_copies(place_ref, run, steps, own, other, buf, sems, columns=(0, None)):
    half = own[0].shape[0]
    here = place_ref[0]
    low = columns[0]
    width = buf.shape[2]
    slots, sem = [], 0
    for slot, step in enumerate(steps):
        pieces = (FAR, FAR + 1) if step == FAR else (step,)
        copies = []
        for piece in pieces:
            size = half // len(pieces)
            unit = min(run, size)
            for at in range(0, size, unit):
                row = (piece - pieces[0]) * size + at
                for source, core in ((own[piece], here), (other[piece], 1 - here)):
                    target = (row // run) * 2 * run + core * run + row % run
                    copies.append(
                        pltpu.make_async_copy(
                            source.at[pl.ds(at, unit), pl.ds(low, width)],
                            buf.at[slot, pl.ds(pl.multiple_of(target, 16), unit)],
                            sems.at[sem],
                        )
                    )
                    sem += 1
        slots.append(copies)
    return slots


def copy_count(half, run, count):
    return 2 * count * max(half // run, 2)


def start_all(slots):
    for copies in slots:
        for copy in copies:
            copy.start()


def wait_slot(slots, now):
    for slot, copies in enumerate(slots):

        @pl.when(now == slot)
        def _():
            for copy in copies:
                copy.wait()


def split_out(half, run, place_ref, grad_buf, mine_ref, other_ref, slot):
    here = place_ref[0]
    for at in range(0, half, run):
        mine = pl.multiple_of(2 * at + here * run, 16)
        theirs = pl.multiple_of(2 * at + (1 - here) * run, 16)
        mine_ref[slot, at : at + run] = grad_buf[pl.ds(mine, run), :]
        other_ref[slot, at : at + run] = grad_buf[pl.ds(theirs, run), :]


def attn_forward_kernel(
    run,
    mp,
    ni,
    wl,
    place_ref,
    resid_ref,
    vec_ref,
    bias_ref,
    live_ref,
    own,
    other,
    first_ref,
    qkv_ref,
    att_ref,
    lse_ref,
    mid_ref,
    buf,
    sems,
):
    now = pl.program_id(0)
    slots = weight_copies(place_ref, run, range(mp), own, other, buf, sems)

    @pl.when(now == 0)
    def _():
        start_all(slots)
        resid = resid_ref[...]
        normed, _ = norm_stats(resid)
        first_ref[...] = (normed * vec_ref[0:1] + vec_ref[1:2]).astype(BF)
        mid_ref[...] = resid + vec_ref[4:5]

    wait_slot(slots, now)
    qkv = dot_nn(first_ref[...], buf[now, :, : 3 * wl]) + bias_ref[0]
    qkv_ref[0] = qkv.astype(BF)
    for image in range(ni):
        rows = slice(image * RP, (image + 1) * RP)
        live = live_ref[image] > 0.0
        for head in range(wl // HD):
            at = head * HD
            queries = qkv_ref[0, rows, at : at + HD]
            keys = qkv_ref[0, rows, wl + at : wl + at + HD]
            vals = qkv_ref[0, rows, 2 * wl + at : 2 * wl + at + HD]
            scores = jnp.where(live, dot_nt(queries, keys) * SCALE, MASKED)
            peak = jnp.max(scores, axis=-1, keepdims=True)
            expo = jnp.exp(scores - peak)
            total = jnp.sum(expo, axis=-1, keepdims=True)
            soft = (expo * (1.0 / total)).astype(BF)
            att_ref[0, rows, at : at + HD] = dot_nn(soft, vals).astype(BF)
            lse_ref[0, rows, head : head + 1] = peak + jnp.log(total)
    mid_ref[...] += dot_nt(att_ref[0], buf[now, :, 3 * wl :])


def mlp_forward_kernel(
    run,
    mp,
    chunk,
    place_ref,
    mid_ref,
    vec_ref,
    bias_ref,
    own,
    other,
    second_ref,
    hidden_ref,
    slope_ref,
    out_ref,
    buf,
    sems,
):
    now = pl.program_id(0)
    fl = hidden_ref.shape[2]
    slots = weight_copies(place_ref, run, range(mp), own, other, buf, sems)

    @pl.when(now == 0)
    def _():
        start_all(slots)
        middle = mid_ref[...]
        normed, _ = norm_stats(middle)
        second_ref[...] = (normed * vec_ref[2:3] + vec_ref[3:4]).astype(BF)
        out_ref[...] = middle + vec_ref[5:6]

    wait_slot(slots, now)
    for start in range(0, mid_ref.shape[0], chunk):
        rows = slice(start, start + chunk)
        upward = dot_nn(second_ref[rows, :], buf[now, :, :fl]) + bias_ref[0]
        share = 0.5 + 0.5 * lax.erf(upward * ROOT_HALF)
        hidden = (upward * share).astype(BF)
        hidden_ref[0, rows, :] = hidden
        slope_ref[0, rows, :] = share + upward * (DENSITY * jnp.exp(-0.5 * upward * upward))
        out_ref[rows, :] += dot_nt(hidden, buf[now, :, fl:])


def head_kernel(
    run,
    columns,
    mp,
    ni,
    wc,
    place_ref,
    resid_ref,
    vec_ref,
    bias_ref,
    ids_ref,
    labels_ref,
    mix_ref,
    total_ref,
    weight_ref,
    pooled_ref,
    teacher_ref,
    own,
    other,
    mine_ref,
    other_ref,
    hbias_ref,
    grad_ref,
    vgrad_ref,
    loss_ref,
    buf,
    cls_buf,
    dist_buf,
    gw_buf,
    sems,
):
    half = mine_ref.shape[1]
    slots = weight_copies(place_ref, run, range(mp), own, other, buf, sems, columns)
    start_all(slots)
    cls_buf[...] = jnp.zeros_like(cls_buf)
    dist_buf[...] = jnp.zeros_like(dist_buf)
    for image in range(ni):
        at = image * RP + TOK
        cls_buf[image : image + 1, :] = resid_ref[at : at + 1, :]
        dist_buf[image : image + 1, :] = resid_ref[at + 1 : at + 2, :]
    grad_ref[...] = jnp.zeros_like(grad_ref)
    normed_c, scaled_c = norm_stats(cls_buf[...])
    normed_d, scaled_d = norm_stats(dist_buf[...])
    gain, shift = vec_ref[0:1], vec_ref[1:2]
    final_c = (normed_c * gain + shift).astype(BF)
    final_d = (normed_d * gain + shift).astype(BF)
    for copies in slots:
        for copy in copies:
            copy.wait()
    cls, dist, teach, goal = [], [], [], []
    mix = mix_ref[:, 0:1]
    for block in range(mp):
        ids = ids_ref[block]
        valid = ids >= 0
        both = bias_ref[block]
        cls.append(
            jnp.where(valid, dot_nn(final_c, buf[block, :, :wc]) + both[:, :wc], MASKED)
        )
        dist.append(
            jnp.where(valid, dot_nn(final_d, buf[block, :, wc:]) + both[:, wc:], MASKED)
        )
        teach.append(jnp.where(valid, dot_nn(pooled_ref[...], teacher_ref[block]), MASKED))
        first = (labels_ref[:, 0:1] == ids).astype(F32)
        second = (labels_ref[:, 1:2] == ids).astype(F32)
        goal.append(mix * first + (1.0 - mix) * second)

    def log_total(parts):
        peak = functools.reduce(
            jnp.maximum, [jnp.max(part, axis=-1, keepdims=True) for part in parts]
        )
        total = sum(jnp.sum(jnp.exp(part - peak), axis=-1, keepdims=True) for part in parts)
        return peak + jnp.log(total)

    log_c, log_d, log_t = log_total(cls), log_total(dist), log_total(teach)
    prob = [jnp.exp(part - log_t) for part in teach]
    dot_c = sum(jnp.sum(g * c, axis=-1, keepdims=True) for g, c in zip(goal, cls))
    dot_d = sum(jnp.sum(p * d, axis=-1, keepdims=True) for p, d in zip(prob, dist))
    loss_rows = 0.5 * (log_c - dot_c) + 0.5 * (log_d - dot_d)
    share = weight_ref[:, 0:1] / total_ref[0]
    loss_ref[...] = jnp.broadcast_to(row_sum(share * loss_rows), loss_ref.shape)
    scale = 0.5 * weight_ref[:, 0:1] / total_ref[0]
    gfin_c = jnp.zeros(cls_buf.shape, F32)
    gfin_d = jnp.zeros(dist_buf.shape, F32)
    for block in range(mp):
        grad_c = scale * (jnp.exp(cls[block] - log_c) - goal[block])
        grad_d = scale * (jnp.exp(dist[block] - log_d) - prob[block])
        hbias_ref[block, :, :wc] = row_sum(grad_c)
        hbias_ref[block, :, wc:] = row_sum(grad_d)
        low_c, low_d = grad_c.astype(BF), grad_d.astype(BF)
        gw_buf[:, :wc] = dot_tn(final_c, low_c).astype(BF)
        gw_buf[:, wc:] = dot_tn(final_d, low_d).astype(BF)
        split_out(half, run, place_ref, gw_buf, mine_ref, other_ref, block)
        gfin_c += dot_nt(low_c, buf[block, :, :wc])
        gfin_d += dot_nt(low_d, buf[block, :, wc:])
    vgrad_ref[...] = jnp.zeros_like(vgrad_ref)
    vgrad_ref[0:1, :] = row_sum(gfin_c * normed_c) + row_sum(gfin_d * normed_d)
    vgrad_ref[1:2, :] = row_sum(gfin_c) + row_sum(gfin_d)
    cls_buf[...] = norm_back(gfin_c, normed_c, scaled_c, gain)
    dist_buf[...] = norm_back(gfin_d, normed_d, scaled_d, gain)
    for image in range(ni):
        at = image * RP + TOK
        grad_ref[at : at + 1, :] = cls_buf[image : image + 1, :]
        grad_ref[at + 1 : at + 2, :] = dist_buf[image : image + 1, :]


def mlp_backward_kernel(
    run,
    steps,
    last,
    place_ref,
    grad_ref,
    mid_ref,
    vec_ref,
    second_ref,
    hidden_ref,
    slope_ref,
    own,
    other,
    *rest,
):
    if steps[0] != FAR:
        part_ref, *rest = rest
    (
        gmid_ref,
        mine_ref,
        other_ref,
        gbias_ref,
        vgrad_ref,
        buf,
        branch_buf,
        branch_t,
        second_t,
        gw_buf,
        sems,
    ) = rest
    now = pl.program_id(0)
    fl = hidden_ref.shape[2]
    half = mine_ref.shape[1]
    slots = weight_copies(place_ref, run, steps, own, other, buf, sems)

    @pl.when(now == 0)
    def _():
        start_all(slots)
        branch_buf[...] = grad_ref[...].astype(BF)
        branch_t[...] = branch_buf[...].T
        second_t[...] = second_ref[...].T
        if steps[0] == FAR:
            gmid_ref[...] = jnp.zeros_like(gmid_ref)
        else:
            gmid_ref[...] = part_ref[...]
        vgrad_ref[...] = jnp.zeros_like(vgrad_ref)

    wait_slot(slots, now)
    gup = (dot_nn(branch_buf[...], buf[now, :, fl:]) * slope_ref[0]).astype(BF)
    gbias_ref[0] = row_sum(gup.astype(F32))
    gmid_ref[...] += dot_nt(gup, buf[now, :, :fl])
    gw_buf[:, :fl] = dot_nn(second_t[...], gup).astype(BF)
    gw_buf[:, fl:] = dot_nn(branch_t[...], hidden_ref[0]).astype(BF)
    split_out(half, run, place_ref, gw_buf, mine_ref, other_ref, 0)
    if last:

        @pl.when(now == len(steps) - 1)
        def _():
            normed, scaled = norm_stats(mid_ref[...])
            gsec = gmid_ref[...]
            grad = grad_ref[...]
            vgrad_ref[2:3, :] = row_sum(gsec * normed)
            vgrad_ref[3:4, :] = row_sum(gsec)
            vgrad_ref[5:6, :] = row_sum(grad)
            gmid = norm_back(gsec, normed, scaled, vec_ref[2:3]) + grad
            vgrad_ref[4:5, :] = row_sum(gmid)
            gmid_ref[...] = gmid


def attn_backward_kernel(
    run,
    ni,
    wl,
    steps,
    last,
    place_ref,
    gmid_ref,
    resid_ref,
    vec_ref,
    live_ref,
    first_ref,
    qkv_ref,
    att_ref,
    lse_ref,
    own,
    other,
    *rest,
):
    if steps[0] != FAR:
        part_ref, *rest = rest
    (
        gres_ref,
        mine_ref,
        other_ref,
        gbias_ref,
        vgrad_ref,
        buf,
        mixed_buf,
        mixed_t,
        first_t,
        gatt_buf,
        gqkv_buf,
        gw_buf,
        sems,
    ) = rest
    now = pl.program_id(0)
    half = mine_ref.shape[1]
    slots = weight_copies(place_ref, run, steps, own, other, buf, sems)

    @pl.when(now == 0)
    def _():
        start_all(slots)
        mixed_buf[...] = gmid_ref[...].astype(BF)
        mixed_t[...] = mixed_buf[...].T
        first_t[...] = first_ref[...].T
        if steps[0] == FAR:
            gres_ref[...] = jnp.zeros_like(gres_ref)
        else:
            gres_ref[...] = part_ref[...]
        vgrad_ref[...] = jnp.zeros_like(vgrad_ref)

    wait_slot(slots, now)
    gatt_buf[...] = dot_nn(mixed_buf[...], buf[now, :, 3 * wl :]).astype(BF)
    for image in range(ni):
        rows = slice(image * RP, (image + 1) * RP)
        live = live_ref[image] > 0.0
        for head in range(wl // HD):
            at = head * HD
            queries = qkv_ref[0, rows, at : at + HD]
            keys = qkv_ref[0, rows, wl + at : wl + at + HD]
            vals = qkv_ref[0, rows, 2 * wl + at : 2 * wl + at + HD]
            gatt = gatt_buf[rows, at : at + HD]
            scores = jnp.where(live, dot_nt(queries, keys) * SCALE, MASKED)
            soft = jnp.exp(scores - lse_ref[0, rows, head : head + 1])
            gsoft = dot_nt(gatt, vals)
            inner = jnp.sum(soft * gsoft, axis=-1, keepdims=True)
            gscore = (soft * (gsoft - inner)).astype(BF)
            gqkv_buf[rows, at : at + HD] = (dot_nn(gscore, keys) * SCALE).astype(BF)
            gqkv_buf[rows, wl + at : wl + at + HD] = (dot_tn(gscore, queries) * SCALE).astype(BF)
            gqkv_buf[rows, 2 * wl + at : 2 * wl + at + HD] = dot_tn(soft.astype(BF), gatt).astype(BF)
    gqkv = gqkv_buf[...]
    gbias_ref[0] = row_sum(gqkv.astype(F32))
    gres_ref[...] += dot_nt(gqkv, buf[now, :, : 3 * wl])
    gw_buf[:, : 3 * wl] = dot_nn(first_t[...], gqkv).astype(BF)
    gw_buf[:, 3 * wl :] = dot_nn(mixed_t[...], att_ref[0]).astype(BF)
    split_out(half, run, place_ref, gw_buf, mine_ref, other_ref, 0)
    if last:

        @pl.when(now == len(steps) - 1)
        def _():
            normed, scaled = norm_stats(resid_ref[...])
            gfirst = gres_ref[...]
            vgrad_ref[0:1, :] = row_sum(gfirst * normed)
            vgrad_ref[1:2, :] = row_sum(gfirst)
            gres_ref[...] = norm_back(gfirst, normed, scaled, vec_ref[0:1]) + gmid_ref[...]


def call(kernel, outs, scratch, ins, steps=None, after=()):
    def whole(array):
        return pl.BlockSpec(array.shape, lambda i: (0,) * array.ndim)

    def each(array, base=0, stride=1):
        return pl.BlockSpec(
            (1, *array.shape[1:]), lambda i: (base + stride * i, *(0,) * (array.ndim - 1))
        )

    specs, arrays, sizes = [], [], []
    for item in [*ins, ("group", list(after))]:
        kind, item = item if isinstance(item, tuple) else ("vmem", item)
        group = item if kind == "group" else [item]
        sizes.append(len(group) if kind == "group" else None)
        if kind in ("group", "smem"):
            space = pl.ANY if kind == "group" else pltpu.SMEM
            specs += [pl.BlockSpec(memory_space=space)] * len(group)
        elif kind == "each":
            specs.append(each(item, steps[0], steps[1] - steps[0]))
        elif steps:
            specs.append(whole(item))
        else:
            specs.append(pl.BlockSpec(memory_space=pltpu.VMEM))
        arrays += group

    def grouped(*refs):
        given, at = [], 0
        for size in sizes:
            given.append(refs[at] if size is None else refs[at : at + size])
            at += 1 if size is None else size
        return kernel(*given[:-1], *refs[at:])

    out_shape = [jax.ShapeDtypeStruct(*out[:2]) for out in outs]
    if steps:
        out_specs = [
            each(shape) if len(out) > 2 else whole(shape) for out, shape in zip(outs, out_shape)
        ]
        grid = {"grid": (len(steps),)}
    else:
        out_specs = [pl.BlockSpec(memory_space=pltpu.VMEM)] * len(out_shape)
        grid = {}
    moved = sum(a.size * a.dtype.itemsize for a in arrays)
    moved += sum(s.size * s.dtype.itemsize for s in out_shape)
    return pl.pallas_call(
        grouped,
        out_shape=out_shape,
        in_specs=specs,
        out_specs=out_specs,
        **grid,
        scratch_shapes=scratch,
        compiler_params=pltpu.CompilerParams(vmem_limit_bytes=VMEM_LIMIT),
        cost_estimate=pl.CostEstimate(
            flops=BRIEF * FLOP_PER_US, bytes_accessed=moved, transcendentals=0
        ),
    )(*arrays)


def tie(values, *behind):
    if not behind:
        return values
    return lax.optimization_barrier((values, behind))[0]


def swap(values, axis, distance):
    size = lax.axis_size(axis)
    return lax.ppermute(values, axis, [(rank, rank ^ distance) for rank in range(size)])


class Gather:
    def __init__(self, near):
        self.near = near

    def square(self, *behind):
        near = tie(self.near, *behind)
        self.own = [near, swap(near, "mp", 1), swap(near, "mp", 2)]
        self.other = [swap(near, "teach", 1)]
        return [near]

    def corner(self, *behind):
        near, by_one, by_two = self.own
        cut = near.shape[0] // 2
        by_one, by_two = tie((by_one, by_two), *behind)
        lower, upper = by_two[:cut], by_one[cut:]
        self.own = [near, by_one, by_two, swap(lower, "mp", 1), swap(upper, "mp", 2)]
        self.other += [swap(by_one, "teach", 1), swap(by_two, "teach", 1)]
        return [lower, upper]

    def cores(self, *behind):
        far = tie(tuple(self.own[3:]), *behind)
        self.own[3:] = far
        self.other += [swap(piece, "teach", 1) for piece in far]

    def refs(self):
        return [("group", self.own), ("group", self.other)]


def add_low(left, right):
    return (left.astype(F32) + right.astype(F32)).astype(BF)


def sum_over(values, axis):
    distance = 1
    while distance < lax.axis_size(axis):
        values = values + swap(values, axis, distance)
        distance *= 2
    return values


def sum_all(values):
    for axis in ("teach", "mp", "dp"):
        values = sum_over(values, axis)
    return values


def join_kernel(sizes, bit_ref, own_ref, got_ref, out_ref):
    first = bit_ref[0] == 0
    size = sizes[0]
    out_ref[:size] = own_ref[:size] + got_ref[:size]
    at, to = size, size
    for size in sizes[1:]:
        own, got = own_ref[at : at + size], got_ref[at : at + size]
        out_ref[to : to + size] = jnp.where(first, own, got)
        out_ref[to + size : to + 2 * size] = jnp.where(first, got, own)
        at, to = at + size, to + 2 * size


def sum_and_gather(values, everywhere, cores, square):
    parts = jnp.concatenate([values, everywhere, cores])
    sizes = [values.shape[0], everywhere.shape[0], cores.shape[0]]
    for axis in ("dp", "teach", "mp"):
        distance = 1
        if axis == "mp":
            cores = parts[sizes[0] + sizes[1] :]
            parts, sizes = parts[: sizes[0] + sizes[1]], sizes[:2]
        while distance < lax.axis_size(axis):
            got = swap(parts, axis, distance)
            bit = (lax.axis_index(axis) // distance) % 2
            new_sizes = [sizes[0], *[2 * size for size in sizes[1:]]]
            parts = call(
                functools.partial(join_kernel, sizes),
                [((sum(new_sizes), 128), F32)],
                [],
                [("smem", bit.astype(jnp.int32).reshape(1)), parts, got],
            )[0]
            sizes = new_sizes
            if axis == "mp":
                other = swap(square, axis, distance)
                pair = [jnp.where(bit == 0, square, other), jnp.where(bit == 0, other, square)]
                square = jnp.concatenate(pair)
            distance *= 2
    return parts[: sizes[0]], parts[sizes[0] :], cores, square


def gather_mp(values):
    size = lax.axis_size("mp")
    return jnp.stack([values] + [swap(values, "mp", step) for step in range(1, size)])


class Scatter:
    def __init__(self):
        self.waiting = []
        self.block = {}
        self.extra = None
        self.sections = []
        self.pieces = None

    def cores(self, steps, mine, other):
        self.waiting.append((steps, mine, swap(other, "teach", 1)))

    def attach(self, *sections):
        self.sections = [mine.shape[1] for mine, _ in sections]
        other = jnp.concatenate([other for _, other in sections], axis=1)
        self.extra = (
            jnp.concatenate([mine for mine, _ in sections], axis=1),
            swap(other, "teach", 1),
        )

    def added(self, *behind):
        for steps, mine, got in self.waiting:
            got = tie(got, *behind)
            for slot, step in enumerate(steps):
                block = add_low(mine[slot], got[slot])
                self.cuts = [block.shape[0], *self.sections]
                if self.extra:
                    more = add_low(self.extra[0][step], self.extra[1][step])
                    block = jnp.concatenate([block, more])
                self.block[step] = block
        self.waiting = []

    def corner(self, *behind):
        self.added(*behind)
        self.cut = cut = -(-self.block[FAR].shape[0] // 32) * 16
        sent = [self.block[FAR][:cut], self.block[FAR][cut:]]
        self.by_one = swap(sent[0], "mp", 1)
        self.by_two = swap(sent[1], "mp", 2)
        return sent

    def square(self, *behind):
        self.added(*behind)
        one, two = self.block[1], self.block[2]
        cut = self.cut
        by_one, by_two = tie((self.by_one, self.by_two), *behind)
        sent = [
            jnp.concatenate([one[:cut], add_low(one[cut:], by_two)]),
            jnp.concatenate([add_low(two[:cut], by_one), two[cut:]]),
        ]
        self.by_one = swap(sent[0], "mp", 1)
        self.by_two = swap(sent[1], "mp", 2)
        return sent

    def summed(self, *behind):
        by_one, by_two = tie((self.by_one, self.by_two), *behind)
        total = self.block[0].astype(F32) + (by_one.astype(F32) + by_two.astype(F32))
        dp = lax.axis_size("dp")
        width = total.shape[1]
        parts, at = [], 0
        for cut in self.cuts:
            parts.append(total[at : at + cut].reshape(dp, -1, width))
            at += cut
        return jnp.concatenate(parts, axis=1).astype(BF).reshape(total.shape)

    def rows(self, *behind):
        total = self.summed(*behind)
        self.pieces = lax.psum_scatter(total, "dp", scatter_dimension=0, tiled=True)
        return [total]

    def result(self):
        return self.pieces.astype(F32)


def adam_direction(gradient, first_moment, second_moment, correct_first, correct_second):
    new_first = BETA * first_moment + (1.0 - BETA) * gradient
    new_second = BETA * second_moment + (1.0 - BETA) * gradient * gradient
    return (
        new_first,
        new_second,
        new_first / correct_first / (jnp.sqrt(new_second / correct_second) + EPS_LAMB),
    )


def split_params(values):
    layered = values[1 : 1 + 6 * L].reshape(L, 6)
    return (
        values[0],
        layered[:, :4],
        layered[:, 4:],
        values[1 + 6 * L : 3 + 6 * L],
        values[3 + 6 * L],
        values[4 + 6 * L],
    )


def expand_params(pieces):
    return (
        pieces[0],
        pieces[1][:, :, None, None],
        pieces[2][:, :, None, None],
        pieces[3][:, None, None],
        pieces[4],
        pieces[5],
    )


def order_params(pieces):
    layered = jnp.concatenate([pieces[1], pieces[2]], axis=1).reshape(-1)
    return jnp.concatenate([pieces[0][None], layered, pieces[3], pieces[4][None], pieces[5][None]])


def squares_of(pieces, mp_first, data_first):
    return order_params(
        (
            jnp.sum(pieces[0] * pieces[0]) * mp_first,
            jnp.sum(pieces[1] * pieces[1], axis=(2, 3)),
            jnp.sum(pieces[2] * pieces[2], axis=(2, 3)),
            jnp.sum(pieces[3] * pieces[3], axis=(1, 2)),
            jnp.sum(pieces[4] * pieces[4]) * mp_first * data_first,
            jnp.sum(pieces[5] * pieces[5]) * data_first,
        )
    )


def per_device(
    patches,
    grid_sizes,
    label_ids,
    label_mix,
    image_weight,
    teacher_stem,
    teacher_head,
    patch_weight,
    attn_weight,
    mlp_weight,
    head_weight,
    vector_params,
    split_biases,
    patch_first,
    attn_first,
    mlp_first,
    head_first,
    vector_first,
    bias_first,
    patch_second,
    attn_second,
    mlp_second,
    head_second,
    vector_second,
    bias_second,
    decay_mask,
    layer_ids,
    step_count,
):
    dp, mp, teach = lax.axis_size("dp"), lax.axis_size("mp"), lax.axis_size("teach")
    here_mp = lax.axis_index("mp")
    here_teach = lax.axis_index("teach")
    place = ("smem", here_teach.astype(jnp.int32).reshape(1))
    mp_first = (here_mp == 0).astype(F32)
    data_first = (lax.axis_index(("dp", "teach")) == 0).astype(F32)
    rows_own = patch_weight.shape[0]
    half = dp * rows_own
    wl = attn_weight.shape[3]
    fl = mlp_weight.shape[3]
    cl = head_weight.shape[2]
    wc = -(-cl // 128) * 128
    head_row = 6 * L

    run = tiled(half, rows_own)

    def inward(values):
        if run == rows_own:
            return values
        lead = values.shape[:-1]
        cut = values.reshape(*lead, dp, teach, rows_own)
        return jnp.swapaxes(cut, -3, -2).reshape(*lead, D)

    def outward(values):
        if run == rows_own:
            return values
        lead = values.shape[:-1]
        cut = values.reshape(*lead, teach, dp, rows_own)
        return jnp.swapaxes(cut, -3, -2).reshape(*lead, D)

    ni = patches.shape[0] // mp

    def take(array):
        return lax.dynamic_slice_in_dim(array, here_mp * ni, ni, 0)

    weight_part = jnp.sum(image_weight).reshape(1)
    patches, grid_sizes, label_ids = take(patches), take(grid_sizes), take(label_ids)
    label_mix, image_weight = take(label_mix), take(image_weight)

    patch_low = inward(patch_weight).astype(BF)
    attn_low = [
        jnp.concatenate([attn_weight[layer, part] for part in range(4)], axis=1).astype(BF)
        for layer in range(L)
    ]
    mlp_low = [
        jnp.concatenate([mlp_weight[layer, 0], mlp_weight[layer, 1]], axis=1).astype(BF)
        for layer in range(L)
    ]
    head_pad = jnp.pad(head_weight, ((0, 0), (0, 0), (0, wc - cl)))
    head_low = jnp.concatenate([head_pad[0], head_pad[1]], axis=1).astype(BF)

    def gather_dp(*pieces):
        wide_piece = lax.all_gather(jnp.concatenate(pieces, axis=1), "dp", axis=0, tiled=True)
        cuts, at = [], 0
        for piece in pieces:
            cuts.append(wide_piece[:, at : at + piece.shape[1]])
            at += piece.shape[1]
        return cuts

    near = gather_dp(patch_low, attn_low[0]) + gather_dp(mlp_low[0])
    mlp_low[-1] = jnp.concatenate([mlp_low[-1], head_low], axis=1)
    head_columns = (2 * fl, 2 * wc)
    rest = [piece for layer in range(1, L) for piece in (attn_low[layer], mlp_low[layer])]
    near += gather_dp(*rest)
    bias_all = gather_mp(split_biases)
    teacher_all = gather_mp(jnp.pad(teacher_head, ((0, 0), (0, wc - cl))))

    vec_in = inward(vector_params)
    layer_vecs = [
        jnp.pad(vec_in[6 * layer : 6 * layer + 6], ((0, 2), (0, 0))) for layer in range(L)
    ]
    final_vec = jnp.pad(vec_in[head_row : head_row + 2], ((0, 6), (0, 0)))
    attn_bias, up_bias = [], []
    span = 2 * wl + fl
    for layer in range(L):
        part = bias_all[:, layer * span : (layer + 1) * span]
        zero = jnp.zeros((mp, wl), F32)
        attn_bias.append(
            jnp.concatenate([part[:, :wl], zero, part[:, wl : 2 * wl]], axis=1)[:, None]
        )
        up_bias.append(part[:, None, 2 * wl :])
    pad_class = ((0, 0), (0, wc - cl))
    head_bias = jnp.concatenate(
        [
            jnp.pad(bias_all[:, L * span : L * span + cl], pad_class),
            jnp.pad(bias_all[:, L * span + cl : L * span + 2 * cl], pad_class),
        ],
        axis=1,
    )[:, None]

    grid_rows, grid_cols = grid_sizes[:, 0:1], grid_sizes[:, 1:2]
    slot_ids = jnp.arange(PMAX, dtype=jnp.int32)[None, :]
    patch_live = slot_ids < grid_rows * grid_cols
    live_float = patch_live.astype(F32)
    live_rows = jnp.concatenate(
        [live_float, jnp.ones((ni, 2), F32), jnp.zeros((ni, RP - PMAX - 2), F32)], axis=1
    )[:, None, :]
    table = jnp.arange(G, dtype=jnp.int32)
    source_patch = jnp.concatenate(
        [
            jnp.ones((ni, PMAX, 1), F32),
            jnp.zeros((ni, PMAX, 2), F32),
            ((slot_ids // grid_cols)[..., None] == table).astype(F32),
            ((slot_ids % grid_cols)[..., None] == table).astype(F32),
        ],
        axis=2,
    )
    source_token = jnp.broadcast_to(jnp.eye(2, 3 + 2 * G, 1, dtype=F32), (ni, 2, 3 + 2 * G))
    sources = jnp.concatenate(
        [source_patch, source_token, jnp.zeros((ni, RP - PMAX - 2, 3 + 2 * G), F32)], axis=1
    ).reshape(ni * RP, 3 + 2 * G)

    stem_rows = gelu_erf(dot_nn(patches.reshape(ni * PMAX, -1), teacher_stem)).reshape(ni, PMAX, -1)
    pooled = (
        jnp.sum(stem_rows * live_float[..., None], axis=1)
        / jnp.sum(live_float, axis=1, keepdims=True)
    ).astype(BF)

    ranks = here_mp ^ jnp.arange(mp, dtype=jnp.int32)
    quarter = rows_own // mp
    patch_rows = jnp.pad(patches, ((0, 0), (0, RP - PMAX), (0, 0))).reshape(ni * RP, -1)
    sides = here_teach ^ jnp.arange(teach, dtype=jnp.int32)
    patches_t = patch_rows.T.reshape(dp, teach, mp, quarter, ni * RP).transpose(1, 2, 0, 3, 4)
    patches_t = patches_t[sides][:, ranks].reshape(-1, ni * RP)

    def wide(values):
        return jnp.pad(values.reshape(ni, -1), ((0, HR - ni), (0, 0)))

    lanes = jnp.arange(wc, dtype=jnp.int32)
    class_ids = jnp.where(lanes[None] < cl, ranks[:, None] * cl + lanes[None], -1)[:, None]
    head_small = [class_ids, wide(label_ids), wide(label_mix), wide(image_weight), wide(pooled)]

    near[0], near[1] = tie(
        (near[0], near[1]),
        *attn_bias,
        *up_bias,
        head_bias,
        *layer_vecs,
        final_vec,
        live_rows,
        sources,
        patches_t,
        *head_small,
        teacher_all,
    )
    patch_own = near[0]
    patch_other = swap(patch_own, "teach", 1)
    units = [Gather(piece) for piece in near[1:]]
    attn_units, mlp_units, head_unit = units[0::2], units[1::2], units[-1]

    first_core = here_teach == 0
    patch_full = jnp.stack(
        [
            jnp.where(first_core, patch_own, patch_other).reshape(dp, rows_own, D),
            jnp.where(first_core, patch_other, patch_own).reshape(dp, rows_own, D),
        ],
        axis=1,
    ).reshape(D, D)
    residual = dot_nn(patch_rows, patch_full) + jnp.dot(
        sources, vec_in[head_row + 2 :], precision=HIGH
    )

    n = ni * RP
    parts = copy_count(half, run, mp)
    saved = []
    units[0].square()
    units[0].corner(residual)
    units[1].square(*units[0].own[3:])

    def arrive(at, done):
        here = units[at]
        ahead = units[at + 1 : at + 2]
        if at > 0:
            here.corner(done)
            for unit in ahead:
                unit.square(*here.own[3:], done)
        here.cores(*[unit.own[0] for unit in ahead])
        return [unit.own[0] for unit in ahead]

    for layer in range(L):
        sending = arrive(2 * layer, residual)
        first, qkv, attended, lse, middle = call(
            functools.partial(attn_forward_kernel, run, mp, ni, wl),
            [
                ((n, D), BF),
                ((mp, n, 3 * wl), BF, "each"),
                ((mp, n, wl), BF, "each"),
                ((mp, n, wl // HD), F32, "each"),
                ((n, D), F32),
            ],
            [pltpu.VMEM((mp, D, 4 * wl), BF), pltpu.SemaphoreType.DMA((parts,))],
            [place, residual, layer_vecs[layer], ("each", attn_bias[layer]), live_rows]
            + attn_units[layer].refs(),
            range(mp),
            sending,
        )
        if layer == 0:
            weight_sum = sum_over(sum_over(tie(weight_part, middle), "teach"), "dp")
            for unit in units[2:]:
                unit.near = tie(unit.near, weight_sum)
        sending = arrive(2 * layer + 1, middle)
        second, hidden, slope, output = call(
            functools.partial(mlp_forward_kernel, run, mp, n // 4),
            [((n, D), BF), ((mp, n, fl), BF, "each"), ((mp, n, fl), F32, "each"), ((n, D), F32)],
            [pltpu.VMEM((mp, D, 2 * fl), BF), pltpu.SemaphoreType.DMA((parts,))],
            [place, middle, layer_vecs[layer], ("each", up_bias[layer])]
            + mlp_units[layer].refs(),
            range(mp),
            sending,
        )
        saved.append((residual, first, qkv, attended, lse, middle, second, hidden, slope))
        residual = output

    head_mine, head_other, head_bgrad, grad, final_vgrad, loss_part = call(
        functools.partial(head_kernel, run, head_columns, mp, ni, wc),
        [
            ((mp, half, 2 * wc), BF),
            ((mp, half, 2 * wc), BF),
            ((mp, 1, 2 * wc), F32),
            ((n, D), F32),
            ((8, D), F32),
            ((8, 128), F32),
        ],
        [
            pltpu.VMEM((mp, D, 2 * wc), BF),
            pltpu.VMEM((HR, D), F32),
            pltpu.VMEM((HR, D), F32),
            pltpu.VMEM((D, 2 * wc), BF),
            pltpu.SemaphoreType.DMA((parts,)),
        ],
        [
            place,
            residual,
            final_vec,
            head_bias,
            *head_small[:3],
            ("smem", weight_sum),
            *head_small[3:],
            teacher_all,
            *head_unit.refs(),
        ],
    )
    head_out = Scatter()
    head_out.cores(range(mp), head_mine, head_other)
    mlp_out, attn_out = [Scatter() for _ in range(L)], [Scatter() for _ in range(L)]
    agenda = {0: [], 1: [(head_out, "corner")], 2: [(head_out, "square")], 3: [(head_out, "rows")]}
    slot = 0
    for layer in reversed(range(L)):
        plan = (
            (mlp_out[layer], "corner", 2),
            (mlp_out[layer], "square", 3),
            (mlp_out[layer], "rows", 5 if layer else 4),
            (attn_out[layer], "corner", 4),
            (attn_out[layer], "square", 5),
            (attn_out[layer], "rows", 6),
        )
        for unit, what, moment in plan:
            agenda.setdefault(slot + moment, []).append((unit, what))
        slot += 4
    final = slot

    def proceed(moment, done):
        sent = []
        for unit, what in agenda.pop(moment, []):
            sent += getattr(unit, what)(done)
        return sent

    sending = [head_other]
    gain_list, bias_list = [None] * L, [None] * L
    slot = 0
    for layer in reversed(range(L)):
        resid_in, first, qkv, attended, lse, middle, second, hidden, slope = saved[layer]
        part = []
        up_bgrad, qkv_bgrad = {}, {}
        for steps in PARTS:
            count = len(steps)
            gmid, mine, other, bgrad, mlp_vgrad = call(
                functools.partial(mlp_backward_kernel, run, steps, steps is PARTS[-1]),
                [
                    ((n, D), F32),
                    ((count, half, 2 * fl), BF, "each"),
                    ((count, half, 2 * fl), BF, "each"),
                    ((count, 1, fl), F32, "each"),
                    ((8, D), F32),
                ],
                [
                    pltpu.VMEM((count, D, 2 * fl), BF),
                    pltpu.VMEM((n, D), BF),
                    pltpu.VMEM((D, n), BF),
                    pltpu.VMEM((D, n), BF),
                    pltpu.VMEM((D, 2 * fl), BF),
                    pltpu.SemaphoreType.DMA((copy_count(half, run, count),)),
                ],
                [place, grad, middle, layer_vecs[layer], second, ("each", hidden), ("each", slope)]
                + mlp_units[layer].refs()
                + part,
                steps,
                sending,
            )
            part = [gmid]
            up_bgrad.update({step: bgrad[at] for at, step in enumerate(steps)})
            slot += 1
            mlp_out[layer].cores(steps, mine, other)
            sending = [other] + proceed(slot, gmid)
        part = []
        for steps in PARTS:
            count = len(steps)
            grad, mine, other, bgrad, attn_vgrad = call(
                functools.partial(attn_backward_kernel, run, ni, wl, steps, steps is PARTS[-1]),
                [
                    ((n, D), F32),
                    ((count, half, 4 * wl), BF, "each"),
                    ((count, half, 4 * wl), BF, "each"),
                    ((count, 1, 3 * wl), F32, "each"),
                    ((8, D), F32),
                ],
                [
                    pltpu.VMEM((count, D, 4 * wl), BF),
                    pltpu.VMEM((n, D), BF),
                    pltpu.VMEM((D, n), BF),
                    pltpu.VMEM((D, n), BF),
                    pltpu.VMEM((n, wl), BF),
                    pltpu.VMEM((n, 3 * wl), BF),
                    pltpu.VMEM((D, 4 * wl), BF),
                    pltpu.SemaphoreType.DMA((copy_count(half, run, count),)),
                ],
                [place, gmid, resid_in, layer_vecs[layer], live_rows, first]
                + [("each", qkv), ("each", attended), ("each", lse)]
                + attn_units[layer].refs()
                + part,
                steps,
                sending,
            )
            part = [grad]
            qkv_bgrad.update({step: bgrad[at] for at, step in enumerate(steps)})
            slot += 1
            attn_out[layer].cores(steps, mine, other)
            if slot < final:
                sending = [other] + proceed(slot, grad)
        gain_list[layer] = (attn_vgrad + mlp_vgrad)[:6]
        bias_list[layer] = jnp.concatenate(
            [
                jnp.concatenate([qkv_bgrad[step][:, :wl] for step in range(mp)]),
                jnp.concatenate([qkv_bgrad[step][:, 2 * wl :] for step in range(mp)]),
                jnp.concatenate([up_bgrad[step] for step in range(mp)]),
            ],
            axis=1,
        )
    ahead = mlp_out[0].rows(grad)
    agenda[final].remove((mlp_out[0], "rows"))
    grad = tie(grad, *ahead)
    patch_grad = dot_nn(patches_t, grad.astype(BF)).astype(BF)
    patch_grad = patch_grad.reshape(teach, mp, dp * quarter, D)

    source_grads = lax.dot_general(
        sources, grad, (((0,), (0,)), ((), ())), precision=HIGH, preferred_element_type=F32
    )
    vector_grads = jnp.concatenate(gain_list + [final_vgrad[:2], source_grads], axis=0)
    bias_blocks = jnp.concatenate(
        bias_list + [head_bgrad[:, 0, :cl], head_bgrad[:, 0, wc : wc + cl]], axis=1
    )
    devices = dp * teach
    vector_piece = -(-vector_params.size // (mp * devices * 1024)) * 1024
    bias_piece = -(-split_biases.size // (devices * 1024)) * 1024

    def padded(flat, size):
        return jnp.pad(flat, ((0, 0), (0, size - flat.shape[1])))

    more_rows = -(rows_own + quarter) % 16
    while more_rows * D < vector_piece + bias_piece:
        more_rows += 16
    vector_cut = padded(vector_grads.reshape(1, -1), vector_piece * mp * devices)
    small = jnp.concatenate(
        [
            vector_cut.reshape(mp, devices, vector_piece)[ranks],
            padded(bias_blocks, bias_piece * devices).reshape(mp, devices, bias_piece),
            jnp.zeros((mp, devices, more_rows * D - vector_piece - bias_piece), F32),
        ],
        axis=2,
    )
    small = small.astype(BF).reshape(mp, teach, dp * more_rows, D)

    def small_half(core):
        return lax.dynamic_index_in_dim(small, core, 1, False)

    attn_out[0].attach(
        (patch_grad[0], patch_grad[1]),
        (small_half(here_teach), small_half(1 - here_teach)),
    )
    for moment in sorted(agenda):
        for unit, what in agenda[moment]:
            ahead += getattr(unit, what)(*ahead)
    first_rows = attn_out[0].result()
    patch_grad = outward(first_rows[rows_own : rows_own + quarter])
    small = first_rows[rows_own + quarter :].reshape(-1, 128)
    vector_grads = small[: vector_piece // 128]
    bias_grads = small[vector_piece // 128 : (vector_piece + bias_piece) // 128]

    attn_list = [first_rows[:rows_own]] + [unit.result() for unit in attn_out[1:]]
    mlp_list = [unit.result() for unit in mlp_out]
    head_grads = head_out.result()
    attn_grads = jnp.stack(
        [
            jnp.stack([attn_list[layer][:, part * wl : (part + 1) * wl] for part in range(4)])
            for layer in range(L)
        ]
    )
    mlp_grads = jnp.stack(
        [jnp.stack([mlp_list[layer][:, :fl], mlp_list[layer][:, fl:]]) for layer in range(L)]
    )
    head_grads = jnp.stack([head_grads[:, :cl], head_grads[:, wc : wc + cl]])

    step_power = step_count[0].astype(F32)
    correct_first = 1.0 - jnp.power(BETA, step_power)
    correct_second = 1.0 - jnp.power(BETA, step_power)
    weights = (patch_weight, attn_weight, mlp_weight, head_weight, vector_params, split_biases)
    firsts = (patch_first, attn_first, mlp_first, head_first, vector_first, bias_first)
    seconds = (patch_second, attn_second, mlp_second, head_second, vector_second, bias_second)
    decay_pieces = expand_params(split_params(decay_mask.astype(F32)))

    def direct(gradient, first, second, weight, decay):
        new_first, new_second, direction = adam_direction(
            gradient, first, second, correct_first, correct_second
        )
        return new_first, new_second, direction + DECAY * decay * weight

    device = lax.axis_index(("teach", "dp"))

    def patch_cut(array):
        return lax.dynamic_slice_in_dim(array, here_mp * quarter, quarter, 0)

    def vector_part(array):
        flat = padded(inward(array).reshape(1, -1), vector_piece * mp * devices)[0]
        at = (here_mp * devices + device) * vector_piece
        return lax.dynamic_slice_in_dim(flat, at, vector_piece, 0).reshape(-1, 128)

    def bias_part(array):
        flat = padded(array.reshape(1, -1), bias_piece * devices)[0]
        part = lax.dynamic_slice_in_dim(flat, device * bias_piece, bias_piece, 0)
        return part.reshape(-1, 128)

    pieces = (patch_grad, attn_grads, mlp_grads, head_grads, vector_grads, bias_grads)
    own_part = (patch_cut, None, None, None, vector_part, bias_part)
    results = []
    for slot, part in enumerate(own_part):
        others = (firsts[slot], seconds[slot], weights[slot])
        if part is not None:
            others = [part(array) for array in others]
        results.append(direct(pieces[slot], *others, decay_pieces[slot]))
    totals = jnp.concatenate(
        [
            squares_of(weights, mp_first, data_first),
            squares_of([result[2] for result in results], 1.0, 1.0),
            loss_part[0, :1],
        ]
    )
    npar = (totals.size - 1) // 2
    totals, vector_grads, bias_grads, patch_grad = sum_and_gather(
        jnp.pad(totals, (0, -totals.size % 1024)).reshape(-1, 128),
        vector_grads,
        bias_grads,
        patch_grad,
    )
    gathered = {
        0: patch_grad,
        4: outward(vector_grads.reshape(-1)[: vector_params.size].reshape(vector_params.shape)),
        5: bias_grads.reshape(-1)[: split_biases.size],
    }
    for slot, gradient in gathered.items():
        results[slot] = direct(
            gradient, firsts[slot], seconds[slot], weights[slot], decay_pieces[slot]
        )
    directions = [result[2] for result in results]
    totals = totals.reshape(-1)
    weights_sq, direction_sq, loss_value = totals[:npar], totals[npar : 2 * npar], totals[2 * npar]
    weight_norm = jnp.sqrt(weights_sq)
    update_norm = jnp.sqrt(direction_sq)
    trust_ratio = weight_norm / update_norm
    rates = BASE_RATE * jnp.power(LAYER_DECAY, 2.0 - layer_ids.astype(F32)) * trust_ratio
    rate_pieces = expand_params(split_params(rates))
    updated = [weights[slot] - rate_pieces[slot] * directions[slot] for slot in range(6)]
    norm_table = jnp.stack([weight_norm, update_norm])
    return (
        *updated,
        *[results[slot][0] for slot in range(6)],
        *[results[slot][1] for slot in range(6)],
        norm_table,
        trust_ratio,
        loss_value,
    )


def solution(mesh):
    rows = ("dp", "teach")
    moments = (
        P(rows, None),
        P(None, None, rows, "mp"),
        P(None, None, rows, "mp"),
        P(None, rows, "mp"),
        P(),
        P("mp"),
    )
    placed = (
        P(rows, None, None),
        P(rows, None),
        P(rows, None),
        P(rows),
        P(rows),
        P(),
        P(None, "mp"),
        *moments,
        *moments,
        *moments,
        P(),
        P(),
        P(),
    )
    return jax.shard_map(
        per_device,
        mesh=mesh,
        in_specs=placed,
        out_specs=(*moments, *moments, *moments, P(), P(), P()),
        check_vma=False,
    )
```

```python
import functools

import jax
import jax.numpy as jnp
from jax import lax
from jax.experimental import pallas as pl
from jax.experimental.pallas import tpu as pltpu
from jax.sharding import PartitionSpec as P

D = 768
HD = 64
G = 24
PMAX = 280
L = 2
RP = 288
TOK = 280
HR = 16

EPS_NORM = 1e-06
EPS_LAMB = 1e-06
BETA = 0.5
DECAY = 0.05
BASE_RATE = 0.4
LAYER_DECAY = 0.8
SCALE = 0.125
MASKED = -1e30
HIGH = lax.Precision.HIGHEST
ROOT_HALF = 0.7071067811865476
DENSITY = 0.3989422804014327
BF = jnp.bfloat16
F32 = jnp.float32
ALL = ("dp", "mp", "teach")
VMEM_LIMIT = 56 * 1024 * 1024
FLOP_PER_US = 1_150_000_000
BRIEF = 2
FAR = 3
PARTS = ((3, 1), (2, 0))


def dot_nn(left, right):
    return lax.dot_general(
        left, right, (((1,), (0,)), ((), ())), preferred_element_type=F32
    )


def dot_nt(left, right):
    return lax.dot_general(
        left, right, (((1,), (1,)), ((), ())), preferred_element_type=F32
    )


def dot_tn(left, right):
    return lax.dot_general(
        left, right, (((0,), (0,)), ((), ())), preferred_element_type=F32
    )


def gelu_erf(values):
    return 0.5 * values * (1.0 + lax.erf(values * ROOT_HALF))


def norm_stats(values):
    centre = values - jnp.mean(values, axis=-1, keepdims=True)
    scaled = lax.rsqrt(jnp.mean(centre * centre, axis=-1, keepdims=True) + EPS_NORM)
    return centre * scaled, scaled


def norm_back(grad_out, normed, scaled, gain_row):
    grad_normed = grad_out * gain_row
    inner_sum = jnp.mean(grad_normed, axis=-1, keepdims=True)
    cross_term = jnp.mean(grad_normed * normed, axis=-1, keepdims=True)
    return scaled * (grad_normed - inner_sum - normed * cross_term)


def row_sum(values):
    return jnp.sum(values, axis=0, keepdims=True)


def tiled(half, rows):
    return rows if rows % 16 == 0 else half


def weight_copies(place_ref, run, steps, own, other, buf, sems, columns=(0, None)):
    half = own[0].shape[0]
    here = place_ref[0]
    low = columns[0]
    width = buf.shape[2]
    slots, sem = [], 0
    for slot, step in enumerate(steps):
        pieces = (FAR, FAR + 1) if step == FAR else (step,)
        copies = []
        for piece in pieces:
            size = half // len(pieces)
            unit = min(run, size)
            for at in range(0, size, unit):
                row = (piece - pieces[0]) * size + at
                for source, core in ((own[piece], here), (other[piece], 1 - here)):
                    target = (row // run) * 2 * run + core * run + row % run
                    copies.append(
                        pltpu.make_async_copy(
                            source.at[pl.ds(at, unit), pl.ds(low, width)],
                            buf.at[slot, pl.ds(pl.multiple_of(target, 16), unit)],
                            sems.at[sem],
                        )
                    )
                    sem += 1
        slots.append(copies)
    return slots


def copy_count(half, run, count):
    return 2 * count * max(half // run, 2)


def start_all(slots):
    for copies in slots:
        for copy in copies:
            copy.start()


def wait_slot(slots, now):
    for slot, copies in enumerate(slots):

        @pl.when(now == slot)
        def _():
            for copy in copies:
                copy.wait()


def split_out(half, run, place_ref, grad_buf, mine_ref, other_ref, slot):
    here = place_ref[0]
    for at in range(0, half, run):
        mine = pl.multiple_of(2 * at + here * run, 16)
        theirs = pl.multiple_of(2 * at + (1 - here) * run, 16)
        mine_ref[slot, at : at + run] = grad_buf[pl.ds(mine, run), :]
        other_ref[slot, at : at + run] = grad_buf[pl.ds(theirs, run), :]


def attn_forward_kernel(
    run,
    mp,
    ni,
    wl,
    place_ref,
    resid_ref,
    vec_ref,
    bias_ref,
    live_ref,
    own,
    other,
    first_ref,
    qkv_ref,
    att_ref,
    lse_ref,
    mid_ref,
    buf,
    sems,
):
    now = pl.program_id(0)
    slots = weight_copies(place_ref, run, range(mp), own, other, buf, sems)

    @pl.when(now == 0)
    def _():
        start_all(slots)
        resid = resid_ref[...]
        normed, _ = norm_stats(resid)
        first_ref[...] = (normed * vec_ref[0:1] + vec_ref[1:2]).astype(BF)
        mid_ref[...] = resid + vec_ref[4:5]

    wait_slot(slots, now)
    qkv = dot_nn(first_ref[...], buf[now, :, : 3 * wl]) + bias_ref[0]
    qkv_ref[0] = qkv.astype(BF)
    for image in range(ni):
        rows = slice(image * RP, (image + 1) * RP)
        live = live_ref[image] > 0.0
        for head in range(wl // HD):
            at = head * HD
            queries = qkv_ref[0, rows, at : at + HD]
            keys = qkv_ref[0, rows, wl + at : wl + at + HD]
            vals = qkv_ref[0, rows, 2 * wl + at : 2 * wl + at + HD]
            scores = jnp.where(live, dot_nt(queries, keys) * SCALE, MASKED)
            peak = jnp.max(scores, axis=-1, keepdims=True)
            expo = jnp.exp(scores - peak)
            total = jnp.sum(expo, axis=-1, keepdims=True)
            soft = (expo * (1.0 / total)).astype(BF)
            att_ref[0, rows, at : at + HD] = dot_nn(soft, vals).astype(BF)
            lse_ref[0, rows, head : head + 1] = peak + jnp.log(total)
    mid_ref[...] += dot_nt(att_ref[0], buf[now, :, 3 * wl :])


def mlp_forward_kernel(
    run,
    mp,
    chunk,
    place_ref,
    mid_ref,
    vec_ref,
    bias_ref,
    own,
    other,
    second_ref,
    hidden_ref,
    slope_ref,
    out_ref,
    buf,
    sems,
):
    now = pl.program_id(0)
    fl = hidden_ref.shape[2]
    slots = weight_copies(place_ref, run, range(mp), own, other, buf, sems)

    @pl.when(now == 0)
    def _():
        start_all(slots)
        middle = mid_ref[...]
        normed, _ = norm_stats(middle)
        second_ref[...] = (normed * vec_ref[2:3] + vec_ref[3:4]).astype(BF)
        out_ref[...] = middle + vec_ref[5:6]

    wait_slot(slots, now)
    for start in range(0, mid_ref.shape[0], chunk):
        rows = slice(start, start + chunk)
        upward = dot_nn(second_ref[rows, :], buf[now, :, :fl]) + bias_ref[0]
        share = 0.5 + 0.5 * lax.erf(upward * ROOT_HALF)
        hidden = (upward * share).astype(BF)
        hidden_ref[0, rows, :] = hidden
        slope_ref[0, rows, :] = share + upward * (DENSITY * jnp.exp(-0.5 * upward * upward))
        out_ref[rows, :] += dot_nt(hidden, buf[now, :, fl:])


def head_kernel(
    run,
    columns,
    mp,
    ni,
    wc,
    place_ref,
    resid_ref,
    vec_ref,
    bias_ref,
    ids_ref,
    labels_ref,
    mix_ref,
    total_ref,
    weight_ref,
    pooled_ref,
    teacher_ref,
    own,
    other,
    mine_ref,
    other_ref,
    hbias_ref,
    grad_ref,
    vgrad_ref,
    loss_ref,
    buf,
    cls_buf,
    dist_buf,
    gw_buf,
    sems,
):
    half = mine_ref.shape[1]
    slots = weight_copies(place_ref, run, range(mp), own, other, buf, sems, columns)
    start_all(slots)
    cls_buf[...] = jnp.zeros_like(cls_buf)
    dist_buf[...] = jnp.zeros_like(dist_buf)
    for image in range(ni):
        at = image * RP + TOK
        cls_buf[image : image + 1, :] = resid_ref[at : at + 1, :]
        dist_buf[image : image + 1, :] = resid_ref[at + 1 : at + 2, :]
    grad_ref[...] = jnp.zeros_like(grad_ref)
    normed_c, scaled_c = norm_stats(cls_buf[...])
    normed_d, scaled_d = norm_stats(dist_buf[...])
    gain, shift = vec_ref[0:1], vec_ref[1:2]
    final_c = (normed_c * gain + shift).astype(BF)
    final_d = (normed_d * gain + shift).astype(BF)
    for copies in slots:
        for copy in copies:
            copy.wait()
    cls, dist, teach, goal = [], [], [], []
    mix = mix_ref[:, 0:1]
    for block in range(mp):
        ids = ids_ref[block]
        valid = ids >= 0
        both = bias_ref[block]
        cls.append(
            jnp.where(valid, dot_nn(final_c, buf[block, :, :wc]) + both[:, :wc], MASKED)
        )
        dist.append(
            jnp.where(valid, dot_nn(final_d, buf[block, :, wc:]) + both[:, wc:], MASKED)
        )
        teach.append(jnp.where(valid, dot_nn(pooled_ref[...], teacher_ref[block]), MASKED))
        first = (labels_ref[:, 0:1] == ids).astype(F32)
        second = (labels_ref[:, 1:2] == ids).astype(F32)
        goal.append(mix * first + (1.0 - mix) * second)

    def log_total(parts):
        peak = functools.reduce(
            jnp.maximum, [jnp.max(part, axis=-1, keepdims=True) for part in parts]
        )
        total = sum(jnp.sum(jnp.exp(part - peak), axis=-1, keepdims=True) for part in parts)
        return peak + jnp.log(total)

    log_c, log_d, log_t = log_total(cls), log_total(dist), log_total(teach)
    prob = [jnp.exp(part - log_t) for part in teach]
    dot_c = sum(jnp.sum(g * c, axis=-1, keepdims=True) for g, c in zip(goal, cls))
    dot_d = sum(jnp.sum(p * d, axis=-1, keepdims=True) for p, d in zip(prob, dist))
    loss_rows = 0.5 * (log_c - dot_c) + 0.5 * (log_d - dot_d)
    share = weight_ref[:, 0:1] / total_ref[0]
    loss_ref[...] = jnp.broadcast_to(row_sum(share * loss_rows), loss_ref.shape)
    scale = 0.5 * weight_ref[:, 0:1] / total_ref[0]
    gfin_c = jnp.zeros(cls_buf.shape, F32)
    gfin_d = jnp.zeros(dist_buf.shape, F32)
    for block in range(mp):
        grad_c = scale * (jnp.exp(cls[block] - log_c) - goal[block])
        grad_d = scale * (jnp.exp(dist[block] - log_d) - prob[block])
        hbias_ref[block, :, :wc] = row_sum(grad_c)
        hbias_ref[block, :, wc:] = row_sum(grad_d)
        low_c, low_d = grad_c.astype(BF), grad_d.astype(BF)
        gw_buf[:, :wc] = dot_tn(final_c, low_c).astype(BF)
        gw_buf[:, wc:] = dot_tn(final_d, low_d).astype(BF)
        split_out(half, run, place_ref, gw_buf, mine_ref, other_ref, block)
        gfin_c += dot_nt(low_c, buf[block, :, :wc])
        gfin_d += dot_nt(low_d, buf[block, :, wc:])
    vgrad_ref[...] = jnp.zeros_like(vgrad_ref)
    vgrad_ref[0:1, :] = row_sum(gfin_c * normed_c) + row_sum(gfin_d * normed_d)
    vgrad_ref[1:2, :] = row_sum(gfin_c) + row_sum(gfin_d)
    cls_buf[...] = norm_back(gfin_c, normed_c, scaled_c, gain)
    dist_buf[...] = norm_back(gfin_d, normed_d, scaled_d, gain)
    for image in range(ni):
        at = image * RP + TOK
        grad_ref[at : at + 1, :] = cls_buf[image : image + 1, :]
        grad_ref[at + 1 : at + 2, :] = dist_buf[image : image + 1, :]


def mlp_backward_kernel(
    run,
    steps,
    last,
    place_ref,
    grad_ref,
    mid_ref,
    vec_ref,
    second_ref,
    hidden_ref,
    slope_ref,
    own,
    other,
    *rest,
):
    if steps[0] != FAR:
        part_ref, *rest = rest
    (
        gmid_ref,
        mine_ref,
        other_ref,
        gbias_ref,
        vgrad_ref,
        buf,
        branch_buf,
        branch_t,
        second_t,
        gw_buf,
        sems,
    ) = rest
    now = pl.program_id(0)
    fl = hidden_ref.shape[2]
    half = mine_ref.shape[1]
    slots = weight_copies(place_ref, run, steps, own, other, buf, sems)

    @pl.when(now == 0)
    def _():
        start_all(slots)
        branch_buf[...] = grad_ref[...].astype(BF)
        branch_t[...] = branch_buf[...].T
        second_t[...] = second_ref[...].T
        if steps[0] == FAR:
            gmid_ref[...] = jnp.zeros_like(gmid_ref)
        else:
            gmid_ref[...] = part_ref[...]
        vgrad_ref[...] = jnp.zeros_like(vgrad_ref)

    wait_slot(slots, now)
    gup = (dot_nn(branch_buf[...], buf[now, :, fl:]) * slope_ref[0]).astype(BF)
    gbias_ref[0] = row_sum(gup.astype(F32))
    gmid_ref[...] += dot_nt(gup, buf[now, :, :fl])
    gw_buf[:, :fl] = dot_nn(second_t[...], gup).astype(BF)
    gw_buf[:, fl:] = dot_nn(branch_t[...], hidden_ref[0]).astype(BF)
    split_out(half, run, place_ref, gw_buf, mine_ref, other_ref, 0)
    if last:

        @pl.when(now == len(steps) - 1)
        def _():
            normed, scaled = norm_stats(mid_ref[...])
            gsec = gmid_ref[...]
            grad = grad_ref[...]
            vgrad_ref[2:3, :] = row_sum(gsec * normed)
            vgrad_ref[3:4, :] = row_sum(gsec)
            vgrad_ref[5:6, :] = row_sum(grad)
            gmid = norm_back(gsec, normed, scaled, vec_ref[2:3]) + grad
            vgrad_ref[4:5, :] = row_sum(gmid)
            gmid_ref[...] = gmid


def attn_backward_kernel(
    run,
    ni,
    wl,
    steps,
    last,
    place_ref,
    gmid_ref,
    resid_ref,
    vec_ref,
    live_ref,
    first_ref,
    qkv_ref,
    att_ref,
    lse_ref,
    own,
    other,
    *rest,
):
    if steps[0] != FAR:
        part_ref, *rest = rest
    (
        gres_ref,
        mine_ref,
        other_ref,
        gbias_ref,
        vgrad_ref,
        buf,
        mixed_buf,
        mixed_t,
        first_t,
        gatt_buf,
        gqkv_buf,
        gw_buf,
        sems,
    ) = rest
    now = pl.program_id(0)
    half = mine_ref.shape[1]
    slots = weight_copies(place_ref, run, steps, own, other, buf, sems)

    @pl.when(now == 0)
    def _():
        start_all(slots)
        mixed_buf[...] = gmid_ref[...].astype(BF)
        mixed_t[...] = mixed_buf[...].T
        first_t[...] = first_ref[...].T
        if steps[0] == FAR:
            gres_ref[...] = jnp.zeros_like(gres_ref)
        else:
            gres_ref[...] = part_ref[...]
        vgrad_ref[...] = jnp.zeros_like(vgrad_ref)

    wait_slot(slots, now)
    gatt_buf[...] = dot_nn(mixed_buf[...], buf[now, :, 3 * wl :]).astype(BF)
    for image in range(ni):
        rows = slice(image * RP, (image + 1) * RP)
        live = live_ref[image] > 0.0
        for head in range(wl // HD):
            at = head * HD
            queries = qkv_ref[0, rows, at : at + HD]
            keys = qkv_ref[0, rows, wl + at : wl + at + HD]
            vals = qkv_ref[0, rows, 2 * wl + at : 2 * wl + at + HD]
            gatt = gatt_buf[rows, at : at + HD]
            scores = jnp.where(live, dot_nt(queries, keys) * SCALE, MASKED)
            soft = jnp.exp(scores - lse_ref[0, rows, head : head + 1])
            gsoft = dot_nt(gatt, vals)
            inner = jnp.sum(soft * gsoft, axis=-1, keepdims=True)
            gscore = (soft * (gsoft - inner)).astype(BF)
            gqkv_buf[rows, at : at + HD] = (dot_nn(gscore, keys) * SCALE).astype(BF)
            gqkv_buf[rows, wl + at : wl + at + HD] = (dot_tn(gscore, queries) * SCALE).astype(BF)
            gqkv_buf[rows, 2 * wl + at : 2 * wl + at + HD] = dot_tn(soft.astype(BF), gatt).astype(BF)
    gqkv = gqkv_buf[...]
    gbias_ref[0] = row_sum(gqkv.astype(F32))
    gres_ref[...] += dot_nt(gqkv, buf[now, :, : 3 * wl])
    gw_buf[:, : 3 * wl] = dot_nn(first_t[...], gqkv).astype(BF)
    gw_buf[:, 3 * wl :] = dot_nn(mixed_t[...], att_ref[0]).astype(BF)
    split_out(half, run, place_ref, gw_buf, mine_ref, other_ref, 0)
    if last:

        @pl.when(now == len(steps) - 1)
        def _():
            normed, scaled = norm_stats(resid_ref[...])
            gfirst = gres_ref[...]
            vgrad_ref[0:1, :] = row_sum(gfirst * normed)
            vgrad_ref[1:2, :] = row_sum(gfirst)
            gres_ref[...] = norm_back(gfirst, normed, scaled, vec_ref[0:1]) + gmid_ref[...]


def call(kernel, outs, scratch, ins, steps=None, after=()):
    def whole(array):
        return pl.BlockSpec(array.shape, lambda i: (0,) * array.ndim)

    def each(array, base=0, stride=1):
        return pl.BlockSpec(
            (1, *array.shape[1:]), lambda i: (base + stride * i, *(0,) * (array.ndim - 1))
        )

    specs, arrays, sizes = [], [], []
    for item in [*ins, ("group", list(after))]:
        kind, item = item if isinstance(item, tuple) else ("vmem", item)
        group = item if kind == "group" else [item]
        sizes.append(len(group) if kind == "group" else None)
        if kind in ("group", "smem"):
            space = pl.ANY if kind == "group" else pltpu.SMEM
            specs += [pl.BlockSpec(memory_space=space)] * len(group)
        elif kind == "each":
            specs.append(each(item, steps[0], steps[1] - steps[0]))
        elif steps:
            specs.append(whole(item))
        else:
            specs.append(pl.BlockSpec(memory_space=pltpu.VMEM))
        arrays += group

    def grouped(*refs):
        given, at = [], 0
        for size in sizes:
            given.append(refs[at] if size is None else refs[at : at + size])
            at += 1 if size is None else size
        return kernel(*given[:-1], *refs[at:])

    out_shape = [jax.ShapeDtypeStruct(*out[:2]) for out in outs]
    if steps:
        out_specs = [
            each(shape) if len(out) > 2 else whole(shape) for out, shape in zip(outs, out_shape)
        ]
        grid = {"grid": (len(steps),)}
    else:
        out_specs = [pl.BlockSpec(memory_space=pltpu.VMEM)] * len(out_shape)
        grid = {}
    moved = sum(a.size * a.dtype.itemsize for a in arrays)
    moved += sum(s.size * s.dtype.itemsize for s in out_shape)
    return pl.pallas_call(
        grouped,
        out_shape=out_shape,
        in_specs=specs,
        out_specs=out_specs,
        **grid,
        scratch_shapes=scratch,
        compiler_params=pltpu.CompilerParams(vmem_limit_bytes=VMEM_LIMIT),
        cost_estimate=pl.CostEstimate(
            flops=BRIEF * FLOP_PER_US, bytes_accessed=moved, transcendentals=0
        ),
    )(*arrays)


def tie(values, *behind):
    if not behind:
        return values
    return lax.optimization_barrier((values, behind))[0]


def swap(values, axis, distance):
    size = lax.axis_size(axis)
    return lax.ppermute(values, axis, [(rank, rank ^ distance) for rank in range(size)])


class Gather:
    def __init__(self, near):
        self.near = near

    def square(self, *behind):
        near = tie(self.near, *behind)
        self.own = [near, swap(near, "mp", 1), swap(near, "mp", 2)]
        self.other = [swap(near, "teach", 1)]
        return [near]

    def corner(self, *behind):
        near, by_one, by_two = self.own
        cut = near.shape[0] // 2
        by_one, by_two = tie((by_one, by_two), *behind)
        lower, upper = by_two[:cut], by_one[cut:]
        self.own = [near, by_one, by_two, swap(lower, "mp", 1), swap(upper, "mp", 2)]
        self.other += [swap(by_one, "teach", 1), swap(by_two, "teach", 1)]
        return [lower, upper]

    def cores(self, *behind):
        far = tie(tuple(self.own[3:]), *behind)
        self.own[3:] = far
        self.other += [swap(piece, "teach", 1) for piece in far]

    def refs(self):
        return [("group", self.own), ("group", self.other)]


def add_low(left, right):
    return (left.astype(F32) + right.astype(F32)).astype(BF)


def sum_over(values, axis):
    distance = 1
    while distance < lax.axis_size(axis):
        values = values + swap(values, axis, distance)
        distance *= 2
    return values


def sum_all(values):
    for axis in ("teach", "mp", "dp"):
        values = sum_over(values, axis)
    return values


def join_kernel(sizes, bit_ref, own_ref, got_ref, out_ref):
    first = bit_ref[0] == 0
    size = sizes[0]
    out_ref[:size] = own_ref[:size] + got_ref[:size]
    at, to = size, size
    for size in sizes[1:]:
        own, got = own_ref[at : at + size], got_ref[at : at + size]
        out_ref[to : to + size] = jnp.where(first, own, got)
        out_ref[to + size : to + 2 * size] = jnp.where(first, got, own)
        at, to = at + size, to + 2 * size


def sum_and_gather(values, everywhere, cores, square):
    parts = jnp.concatenate([values, everywhere, cores])
    sizes = [values.shape[0], everywhere.shape[0], cores.shape[0]]
    for axis in ("dp", "teach", "mp"):
        distance = 1
        if axis == "mp":
            cores = parts[sizes[0] + sizes[1] :]
            parts, sizes = parts[: sizes[0] + sizes[1]], sizes[:2]
        while distance < lax.axis_size(axis):
            got = swap(parts, axis, distance)
            bit = (lax.axis_index(axis) // distance) % 2
            new_sizes = [sizes[0], *[2 * size for size in sizes[1:]]]
            parts = call(
                functools.partial(join_kernel, sizes),
                [((sum(new_sizes), 128), F32)],
                [],
                [("smem", bit.astype(jnp.int32).reshape(1)), parts, got],
            )[0]
            sizes = new_sizes
            if axis == "mp":
                other = swap(square, axis, distance)
                pair = [jnp.where(bit == 0, square, other), jnp.where(bit == 0, other, square)]
                square = jnp.concatenate(pair)
            distance *= 2
    return parts[: sizes[0]], parts[sizes[0] :], cores, square


def gather_mp(values):
    size = lax.axis_size("mp")
    return jnp.stack([values] + [swap(values, "mp", step) for step in range(1, size)])


class Scatter:
    def __init__(self):
        self.waiting = []
        self.block = {}
        self.extra = None
        self.sections = []
        self.pieces = None

    def cores(self, steps, mine, other):
        self.waiting.append((steps, mine, swap(other, "teach", 1)))

    def attach(self, *sections):
        self.sections = [mine.shape[1] for mine, _ in sections]
        other = jnp.concatenate([other for _, other in sections], axis=1)
        self.extra = (
            jnp.concatenate([mine for mine, _ in sections], axis=1),
            swap(other, "teach", 1),
        )

    def added(self, *behind):
        for steps, mine, got in self.waiting:
            got = tie(got, *behind)
            for slot, step in enumerate(steps):
                block = add_low(mine[slot], got[slot])
                self.cuts = [block.shape[0], *self.sections]
                if self.extra:
                    more = add_low(self.extra[0][step], self.extra[1][step])
                    block = jnp.concatenate([block, more])
                self.block[step] = block
        self.waiting = []

    def corner(self, *behind):
        self.added(*behind)
        self.cut = cut = -(-self.block[FAR].shape[0] // 32) * 16
        sent = [self.block[FAR][:cut], self.block[FAR][cut:]]
        self.by_one = swap(sent[0], "mp", 1)
        self.by_two = swap(sent[1], "mp", 2)
        return sent

    def square(self, *behind):
        self.added(*behind)
        one, two = self.block[1], self.block[2]
        cut = self.cut
        by_one, by_two = tie((self.by_one, self.by_two), *behind)
        sent = [
            jnp.concatenate([one[:cut], add_low(one[cut:], by_two)]),
            jnp.concatenate([add_low(two[:cut], by_one), two[cut:]]),
        ]
        self.by_one = swap(sent[0], "mp", 1)
        self.by_two = swap(sent[1], "mp", 2)
        return sent

    def summed(self, *behind):
        by_one, by_two = tie((self.by_one, self.by_two), *behind)
        total = self.block[0].astype(F32) + (by_one.astype(F32) + by_two.astype(F32))
        dp = lax.axis_size("dp")
        width = total.shape[1]
        parts, at = [], 0
        for cut in self.cuts:
            parts.append(total[at : at + cut].reshape(dp, -1, width))
            at += cut
        return jnp.concatenate(parts, axis=1).astype(BF).reshape(total.shape)

    def rows(self, *behind):
        total = self.summed(*behind)
        self.pieces = lax.psum_scatter(total, "dp", scatter_dimension=0, tiled=True)
        return [total]

    def result(self):
        return self.pieces.astype(F32)


def adam_direction(gradient, first_moment, second_moment, correct_first, correct_second):
    new_first = BETA * first_moment + (1.0 - BETA) * gradient
    new_second = BETA * second_moment + (1.0 - BETA) * gradient * gradient
    return (
        new_first,
        new_second,
        new_first / correct_first / (jnp.sqrt(new_second / correct_second) + EPS_LAMB),
    )


def split_params(values):
    layered = values[1 : 1 + 6 * L].reshape(L, 6)
    return (
        values[0],
        layered[:, :4],
        layered[:, 4:],
        values[1 + 6 * L : 3 + 6 * L],
        values[3 + 6 * L],
        values[4 + 6 * L],
    )


def expand_params(pieces):
    return (
        pieces[0],
        pieces[1][:, :, None, None],
        pieces[2][:, :, None, None],
        pieces[3][:, None, None],
        pieces[4],
        pieces[5],
    )


def order_params(pieces):
    layered = jnp.concatenate([pieces[1], pieces[2]], axis=1).reshape(-1)
    return jnp.concatenate([pieces[0][None], layered, pieces[3], pieces[4][None], pieces[5][None]])


def squares_of(pieces, mp_first, data_first):
    return order_params(
        (
            jnp.sum(pieces[0] * pieces[0]) * mp_first,
            jnp.sum(pieces[1] * pieces[1], axis=(2, 3)),
            jnp.sum(pieces[2] * pieces[2], axis=(2, 3)),
            jnp.sum(pieces[3] * pieces[3], axis=(1, 2)),
            jnp.sum(pieces[4] * pieces[4]) * mp_first * data_first,
            jnp.sum(pieces[5] * pieces[5]) * data_first,
        )
    )


def per_device(
    patches,
    grid_sizes,
    label_ids,
    label_mix,
    image_weight,
    teacher_stem,
    teacher_head,
    patch_weight,
    attn_weight,
    mlp_weight,
    head_weight,
    vector_params,
    split_biases,
    patch_first,
    attn_first,
    mlp_first,
    head_first,
    vector_first,
    bias_first,
    patch_second,
    attn_second,
    mlp_second,
    head_second,
    vector_second,
    bias_second,
    decay_mask,
    layer_ids,
    step_count,
):
    dp, mp, teach = lax.axis_size("dp"), lax.axis_size("mp"), lax.axis_size("teach")
    here_mp = lax.axis_index("mp")
    here_teach = lax.axis_index("teach")
    place = ("smem", here_teach.astype(jnp.int32).reshape(1))
    mp_first = (here_mp == 0).astype(F32)
    data_first = (lax.axis_index(("dp", "teach")) == 0).astype(F32)
    rows_own = patch_weight.shape[0]
    half = dp * rows_own
    wl = attn_weight.shape[3]
    fl = mlp_weight.shape[3]
    cl = head_weight.shape[2]
    wc = -(-cl // 128) * 128
    head_row = 6 * L

    run = tiled(half, rows_own)

    def inward(values):
        if run == rows_own:
            return values
        lead = values.shape[:-1]
        cut = values.reshape(*lead, dp, teach, rows_own)
        return jnp.swapaxes(cut, -3, -2).reshape(*lead, D)

    def outward(values):
        if run == rows_own:
            return values
        lead = values.shape[:-1]
        cut = values.reshape(*lead, teach, dp, rows_own)
        return jnp.swapaxes(cut, -3, -2).reshape(*lead, D)

    ni = patches.shape[0] // mp

    def take(array):
        return lax.dynamic_slice_in_dim(array, here_mp * ni, ni, 0)

    weight_part = jnp.sum(image_weight).reshape(1)
    patches, grid_sizes, label_ids = take(patches), take(grid_sizes), take(label_ids)
    label_mix, image_weight = take(label_mix), take(image_weight)

    patch_low = inward(patch_weight).astype(BF)
    attn_low = [
        jnp.concatenate([attn_weight[layer, part] for part in range(4)], axis=1).astype(BF)
        for layer in range(L)
    ]
    mlp_low = [
        jnp.concatenate([mlp_weight[layer, 0], mlp_weight[layer, 1]], axis=1).astype(BF)
        for layer in range(L)
    ]
    head_pad = jnp.pad(head_weight, ((0, 0), (0, 0), (0, wc - cl)))
    head_low = jnp.concatenate([head_pad[0], head_pad[1]], axis=1).astype(BF)

    def gather_dp(*pieces):
        wide_piece = lax.all_gather(jnp.concatenate(pieces, axis=1), "dp", axis=0, tiled=True)
        cuts, at = [], 0
        for piece in pieces:
            cuts.append(wide_piece[:, at : at + piece.shape[1]])
            at += piece.shape[1]
        return cuts

    near = gather_dp(patch_low, attn_low[0]) + gather_dp(mlp_low[0])
    mlp_low[-1] = jnp.concatenate([mlp_low[-1], head_low], axis=1)
    head_columns = (2 * fl, 2 * wc)
    rest = [piece for layer in range(1, L) for piece in (attn_low[layer], mlp_low[layer])]
    near += gather_dp(*rest)
    bias_all = gather_mp(split_biases)
    teacher_all = gather_mp(jnp.pad(teacher_head, ((0, 0), (0, wc - cl))))

    vec_in = inward(vector_params)
    layer_vecs = [
        jnp.pad(vec_in[6 * layer : 6 * layer + 6], ((0, 2), (0, 0))) for layer in range(L)
    ]
    final_vec = jnp.pad(vec_in[head_row : head_row + 2], ((0, 6), (0, 0)))
    attn_bias, up_bias = [], []
    span = 2 * wl + fl
    for layer in range(L):
        part = bias_all[:, layer * span : (layer + 1) * span]
        zero = jnp.zeros((mp, wl), F32)
        attn_bias.append(
            jnp.concatenate([part[:, :wl], zero, part[:, wl : 2 * wl]], axis=1)[:, None]
        )
        up_bias.append(part[:, None, 2 * wl :])
    pad_class = ((0, 0), (0, wc - cl))
    head_bias = jnp.concatenate(
        [
            jnp.pad(bias_all[:, L * span : L * span + cl], pad_class),
            jnp.pad(bias_all[:, L * span + cl : L * span + 2 * cl], pad_class),
        ],
        axis=1,
    )[:, None]

    grid_rows, grid_cols = grid_sizes[:, 0:1], grid_sizes[:, 1:2]
    slot_ids = jnp.arange(PMAX, dtype=jnp.int32)[None, :]
    patch_live = slot_ids < grid_rows * grid_cols
    live_float = patch_live.astype(F32)
    live_rows = jnp.concatenate(
        [live_float, jnp.ones((ni, 2), F32), jnp.zeros((ni, RP - PMAX - 2), F32)], axis=1
    )[:, None, :]
    table = jnp.arange(G, dtype=jnp.int32)
    source_patch = jnp.concatenate(
        [
            jnp.ones((ni, PMAX, 1), F32),
            jnp.zeros((ni, PMAX, 2), F32),
            ((slot_ids // grid_cols)[..., None] == table).astype(F32),
            ((slot_ids % grid_cols)[..., None] == table).astype(F32),
        ],
        axis=2,
    )
    source_token = jnp.broadcast_to(jnp.eye(2, 3 + 2 * G, 1, dtype=F32), (ni, 2, 3 + 2 * G))
    sources = jnp.concatenate(
        [source_patch, source_token, jnp.zeros((ni, RP - PMAX - 2, 3 + 2 * G), F32)], axis=1
    ).reshape(ni * RP, 3 + 2 * G)

    stem_rows = gelu_erf(dot_nn(patches.reshape(ni * PMAX, -1), teacher_stem)).reshape(ni, PMAX, -1)
    pooled = (
        jnp.sum(stem_rows * live_float[..., None], axis=1)
        / jnp.sum(live_float, axis=1, keepdims=True)
    ).astype(BF)

    ranks = here_mp ^ jnp.arange(mp, dtype=jnp.int32)
    quarter = rows_own // mp
    patch_rows = jnp.pad(patches, ((0, 0), (0, RP - PMAX), (0, 0))).reshape(ni * RP, -1)
    sides = here_teach ^ jnp.arange(teach, dtype=jnp.int32)
    patches_t = patch_rows.T.reshape(dp, teach, mp, quarter, ni * RP).transpose(1, 2, 0, 3, 4)
    patches_t = patches_t[sides][:, ranks].reshape(-1, ni * RP)

    def wide(values):
        return jnp.pad(values.reshape(ni, -1), ((0, HR - ni), (0, 0)))

    lanes = jnp.arange(wc, dtype=jnp.int32)
    class_ids = jnp.where(lanes[None] < cl, ranks[:, None] * cl + lanes[None], -1)[:, None]
    head_small = [class_ids, wide(label_ids), wide(label_mix), wide(image_weight), wide(pooled)]

    near[0], near[1] = tie(
        (near[0], near[1]),
        *attn_bias,
        *up_bias,
        head_bias,
        *layer_vecs,
        final_vec,
        live_rows,
        sources,
        patches_t,
        *head_small,
        teacher_all,
    )
    patch_own = near[0]
    patch_other = swap(patch_own, "teach", 1)
    units = [Gather(piece) for piece in near[1:]]
    attn_units, mlp_units, head_unit = units[0::2], units[1::2], units[-1]

    first_core = here_teach == 0
    patch_full = jnp.stack(
        [
            jnp.where(first_core, patch_own, patch_other).reshape(dp, rows_own, D),
            jnp.where(first_core, patch_other, patch_own).reshape(dp, rows_own, D),
        ],
        axis=1,
    ).reshape(D, D)
    residual = dot_nn(patch_rows, patch_full) + jnp.dot(
        sources, vec_in[head_row + 2 :], precision=HIGH
    )

    n = ni * RP
    parts = copy_count(half, run, mp)
    saved = []
    units[0].square()
    units[0].corner(residual)
    units[1].square(*units[0].own[3:])

    def arrive(at, done):
        here = units[at]
        ahead = units[at + 1 : at + 2]
        if at > 0:
            here.corner(done)
            for unit in ahead:
                unit.square(*here.own[3:], done)
        here.cores(*[unit.own[0] for unit in ahead])
        return [unit.own[0] for unit in ahead]

    for layer in range(L):
        sending = arrive(2 * layer, residual)
        first, qkv, attended, lse, middle = call(
            functools.partial(attn_forward_kernel, run, mp, ni, wl),
            [
                ((n, D), BF),
                ((mp, n, 3 * wl), BF, "each"),
                ((mp, n, wl), BF, "each"),
                ((mp, n, wl // HD), F32, "each"),
                ((n, D), F32),
            ],
            [pltpu.VMEM((mp, D, 4 * wl), BF), pltpu.SemaphoreType.DMA((parts,))],
            [place, residual, layer_vecs[layer], ("each", attn_bias[layer]), live_rows]
            + attn_units[layer].refs(),
            range(mp),
            sending,
        )
        if layer == 0:
            weight_sum = sum_over(sum_over(tie(weight_part, middle), "teach"), "dp")
            for unit in units[2:]:
                unit.near = tie(unit.near, weight_sum)
        sending = arrive(2 * layer + 1, middle)
        second, hidden, slope, output = call(
            functools.partial(mlp_forward_kernel, run, mp, n // 2),
            [((n, D), BF), ((mp, n, fl), BF, "each"), ((mp, n, fl), F32, "each"), ((n, D), F32)],
            [pltpu.VMEM((mp, D, 2 * fl), BF), pltpu.SemaphoreType.DMA((parts,))],
            [place, middle, layer_vecs[layer], ("each", up_bias[layer])]
            + mlp_units[layer].refs(),
            range(mp),
            sending,
        )
        saved.append((residual, first, qkv, attended, lse, middle, second, hidden, slope))
        residual = output

    head_mine, head_other, head_bgrad, grad, final_vgrad, loss_part = call(
        functools.partial(head_kernel, run, head_columns, mp, ni, wc),
        [
            ((mp, half, 2 * wc), BF),
            ((mp, half, 2 * wc), BF),
            ((mp, 1, 2 * wc), F32),
            ((n, D), F32),
            ((8, D), F32),
            ((8, 128), F32),
        ],
        [
            pltpu.VMEM((mp, D, 2 * wc), BF),
            pltpu.VMEM((HR, D), F32),
            pltpu.VMEM((HR, D), F32),
            pltpu.VMEM((D, 2 * wc), BF),
            pltpu.SemaphoreType.DMA((parts,)),
        ],
        [
            place,
            residual,
            final_vec,
            head_bias,
            *head_small[:3],
            ("smem", weight_sum),
            *head_small[3:],
            teacher_all,
            *head_unit.refs(),
        ],
    )
    head_out = Scatter()
    head_out.cores(range(mp), head_mine, head_other)
    mlp_out, attn_out = [Scatter() for _ in range(L)], [Scatter() for _ in range(L)]
    agenda = {0: [], 1: [(head_out, "corner")], 2: [(head_out, "square")], 3: [(head_out, "rows")]}
    slot = 0
    for layer in reversed(range(L)):
        plan = (
            (mlp_out[layer], "corner", 2),
            (mlp_out[layer], "square", 3),
            (mlp_out[layer], "rows", 5 if layer else 4),
            (attn_out[layer], "corner", 4),
            (attn_out[layer], "square", 5),
            (attn_out[layer], "rows", 6),
        )
        for unit, what, moment in plan:
            agenda.setdefault(slot + moment, []).append((unit, what))
        slot += 4
    final = slot

    def proceed(moment, done):
        sent = []
        for unit, what in agenda.pop(moment, []):
            sent += getattr(unit, what)(done)
        return sent

    sending = [head_other]
    gain_list, bias_list = [None] * L, [None] * L
    slot = 0
    for layer in reversed(range(L)):
        resid_in, first, qkv, attended, lse, middle, second, hidden, slope = saved[layer]
        part = []
        up_bgrad, qkv_bgrad = {}, {}
        for steps in PARTS:
            count = len(steps)
            gmid, mine, other, bgrad, mlp_vgrad = call(
                functools.partial(mlp_backward_kernel, run, steps, steps is PARTS[-1]),
                [
                    ((n, D), F32),
                    ((count, half, 2 * fl), BF, "each"),
                    ((count, half, 2 * fl), BF, "each"),
                    ((count, 1, fl), F32, "each"),
                    ((8, D), F32),
                ],
                [
                    pltpu.VMEM((count, D, 2 * fl), BF),
                    pltpu.VMEM((n, D), BF),
                    pltpu.VMEM((D, n), BF),
                    pltpu.VMEM((D, n), BF),
                    pltpu.VMEM((D, 2 * fl), BF),
                    pltpu.SemaphoreType.DMA((copy_count(half, run, count),)),
                ],
                [place, grad, middle, layer_vecs[layer], second, ("each", hidden), ("each", slope)]
                + mlp_units[layer].refs()
                + part,
                steps,
                sending,
            )
            part = [gmid]
            up_bgrad.update({step: bgrad[at] for at, step in enumerate(steps)})
            slot += 1
            mlp_out[layer].cores(steps, mine, other)
            sending = [other] + proceed(slot, gmid)
        part = []
        for steps in PARTS:
            count = len(steps)
            grad, mine, other, bgrad, attn_vgrad = call(
                functools.partial(attn_backward_kernel, run, ni, wl, steps, steps is PARTS[-1]),
                [
                    ((n, D), F32),
                    ((count, half, 4 * wl), BF, "each"),
                    ((count, half, 4 * wl), BF, "each"),
                    ((count, 1, 3 * wl), F32, "each"),
                    ((8, D), F32),
                ],
                [
                    pltpu.VMEM((count, D, 4 * wl), BF),
                    pltpu.VMEM((n, D), BF),
                    pltpu.VMEM((D, n), BF),
                    pltpu.VMEM((D, n), BF),
                    pltpu.VMEM((n, wl), BF),
                    pltpu.VMEM((n, 3 * wl), BF),
                    pltpu.VMEM((D, 4 * wl), BF),
                    pltpu.SemaphoreType.DMA((copy_count(half, run, count),)),
                ],
                [place, gmid, resid_in, layer_vecs[layer], live_rows, first]
                + [("each", qkv), ("each", attended), ("each", lse)]
                + attn_units[layer].refs()
                + part,
                steps,
                sending,
            )
            part = [grad]
            qkv_bgrad.update({step: bgrad[at] for at, step in enumerate(steps)})
            slot += 1
            attn_out[layer].cores(steps, mine, other)
            if slot < final:
                sending = [other] + proceed(slot, grad)
        gain_list[layer] = (attn_vgrad + mlp_vgrad)[:6]
        bias_list[layer] = jnp.concatenate(
            [
                jnp.concatenate([qkv_bgrad[step][:, :wl] for step in range(mp)]),
                jnp.concatenate([qkv_bgrad[step][:, 2 * wl :] for step in range(mp)]),
                jnp.concatenate([up_bgrad[step] for step in range(mp)]),
            ],
            axis=1,
        )
    ahead = mlp_out[0].rows(grad)
    agenda[final].remove((mlp_out[0], "rows"))
    grad = tie(grad, *ahead)
    patch_grad = dot_nn(patches_t, grad.astype(BF)).astype(BF)
    patch_grad = patch_grad.reshape(teach, mp, dp * quarter, D)

    source_grads = lax.dot_general(
        sources, grad, (((0,), (0,)), ((), ())), precision=HIGH, preferred_element_type=F32
    )
    vector_grads = jnp.concatenate(gain_list + [final_vgrad[:2], source_grads], axis=0)
    bias_blocks = jnp.concatenate(
        bias_list + [head_bgrad[:, 0, :cl], head_bgrad[:, 0, wc : wc + cl]], axis=1
    )
    devices = dp * teach
    vector_piece = -(-vector_params.size // (mp * devices * 1024)) * 1024
    bias_piece = -(-split_biases.size // (devices * 1024)) * 1024

    def padded(flat, size):
        return jnp.pad(flat, ((0, 0), (0, size - flat.shape[1])))

    more_rows = -(rows_own + quarter) % 16
    while more_rows * D < vector_piece + bias_piece:
        more_rows += 16
    vector_cut = padded(vector_grads.reshape(1, -1), vector_piece * mp * devices)
    small = jnp.concatenate(
        [
            vector_cut.reshape(mp, devices, vector_piece)[ranks],
            padded(bias_blocks, bias_piece * devices).reshape(mp, devices, bias_piece),
            jnp.zeros((mp, devices, more_rows * D - vector_piece - bias_piece), F32),
        ],
        axis=2,
    )
    small = small.astype(BF).reshape(mp, teach, dp * more_rows, D)

    def small_half(core):
        return lax.dynamic_index_in_dim(small, core, 1, False)

    attn_out[0].attach(
        (patch_grad[0], patch_grad[1]),
        (small_half(here_teach), small_half(1 - here_teach)),
    )
    for moment in sorted(agenda):
        for unit, what in agenda[moment]:
            ahead += getattr(unit, what)(*ahead)
    first_rows = attn_out[0].result()
    patch_grad = outward(first_rows[rows_own : rows_own + quarter])
    small = first_rows[rows_own + quarter :].reshape(-1, 128)
    vector_grads = small[: vector_piece // 128]
    bias_grads = small[vector_piece // 128 : (vector_piece + bias_piece) // 128]

    attn_list = [first_rows[:rows_own]] + [unit.result() for unit in attn_out[1:]]
    mlp_list = [unit.result() for unit in mlp_out]
    head_grads = head_out.result()
    attn_grads = jnp.stack(
        [
            jnp.stack([attn_list[layer][:, part * wl : (part + 1) * wl] for part in range(4)])
            for layer in range(L)
        ]
    )
    mlp_grads = jnp.stack(
        [jnp.stack([mlp_list[layer][:, :fl], mlp_list[layer][:, fl:]]) for layer in range(L)]
    )
    head_grads = jnp.stack([head_grads[:, :cl], head_grads[:, wc : wc + cl]])

    step_power = step_count[0].astype(F32)
    correct_first = 1.0 - jnp.power(BETA, step_power)
    correct_second = 1.0 - jnp.power(BETA, step_power)
    weights = (patch_weight, attn_weight, mlp_weight, head_weight, vector_params, split_biases)
    firsts = (patch_first, attn_first, mlp_first, head_first, vector_first, bias_first)
    seconds = (patch_second, attn_second, mlp_second, head_second, vector_second, bias_second)
    decay_pieces = expand_params(split_params(decay_mask.astype(F32)))

    def direct(gradient, first, second, weight, decay):
        new_first, new_second, direction = adam_direction(
            gradient, first, second, correct_first, correct_second
        )
        return new_first, new_second, direction + DECAY * decay * weight

    device = lax.axis_index(("teach", "dp"))

    def patch_cut(array):
        return lax.dynamic_slice_in_dim(array, here_mp * quarter, quarter, 0)

    def vector_part(array):
        flat = padded(inward(array).reshape(1, -1), vector_piece * mp * devices)[0]
        at = (here_mp * devices + device) * vector_piece
        return lax.dynamic_slice_in_dim(flat, at, vector_piece, 0).reshape(-1, 128)

    def bias_part(array):
        flat = padded(array.reshape(1, -1), bias_piece * devices)[0]
        part = lax.dynamic_slice_in_dim(flat, device * bias_piece, bias_piece, 0)
        return part.reshape(-1, 128)

    pieces = (patch_grad, attn_grads, mlp_grads, head_grads, vector_grads, bias_grads)
    own_part = (patch_cut, None, None, None, vector_part, bias_part)
    results = []
    for slot, part in enumerate(own_part):
        others = (firsts[slot], seconds[slot], weights[slot])
        if part is not None:
            others = [part(array) for array in others]
        results.append(direct(pieces[slot], *others, decay_pieces[slot]))
    totals = jnp.concatenate(
        [
            squares_of(weights, mp_first, data_first),
            squares_of([result[2] for result in results], 1.0, 1.0),
            loss_part[0, :1],
        ]
    )
    npar = (totals.size - 1) // 2
    totals, vector_grads, bias_grads, patch_grad = sum_and_gather(
        jnp.pad(totals, (0, -totals.size % 1024)).reshape(-1, 128),
        vector_grads,
        bias_grads,
        patch_grad,
    )
    gathered = {
        0: patch_grad,
        4: outward(vector_grads.reshape(-1)[: vector_params.size].reshape(vector_params.shape)),
        5: bias_grads.reshape(-1)[: split_biases.size],
    }
    for slot, gradient in gathered.items():
        results[slot] = direct(
            gradient, firsts[slot], seconds[slot], weights[slot], decay_pieces[slot]
        )
    directions = [result[2] for result in results]
    totals = totals.reshape(-1)
    weights_sq, direction_sq, loss_value = totals[:npar], totals[npar : 2 * npar], totals[2 * npar]
    weight_norm = jnp.sqrt(weights_sq)
    update_norm = jnp.sqrt(direction_sq)
    trust_ratio = weight_norm / update_norm
    rates = BASE_RATE * jnp.power(LAYER_DECAY, 2.0 - layer_ids.astype(F32)) * trust_ratio
    rate_pieces = expand_params(split_params(rates))
    updated = [weights[slot] - rate_pieces[slot] * directions[slot] for slot in range(6)]
    norm_table = jnp.stack([weight_norm, update_norm])
    return (
        *updated,
        *[results[slot][0] for slot in range(6)],
        *[results[slot][1] for slot in range(6)],
        norm_table,
        trust_ratio,
        loss_value,
    )


def solution(mesh):
    rows = ("dp", "teach")
    moments = (
        P(rows, None),
        P(None, None, rows, "mp"),
        P(None, None, rows, "mp"),
        P(None, rows, "mp"),
        P(),
        P("mp"),
    )
    placed = (
        P(rows, None, None),
        P(rows, None),
        P(rows, None),
        P(rows),
        P(rows),
        P(),
        P(None, "mp"),
        *moments,
        *moments,
        *moments,
        P(),
        P(),
        P(),
    )
    return jax.shard_map(
        per_device,
        mesh=mesh,
        in_specs=placed,
        out_specs=(*moments, *moments, *moments, P(), P(), P()),
        check_vma=False,
    )
```
